32 devices in a mesh: groups: 2 (over x), req: 16 (over z, y, core).
Axes of the slice: x: 2, y: 2, z: 4, core: 2. Of those that a mesh axis runs over, the one named last changes fastest.
Arguments:
- queries: bfloat16 [64, 6, 4096], P(('groups', 'req')), parts along dimension 0, may hold values from -6 to 6
- keys: bfloat16 [64, 6, 4096], P(('groups', 'req')), parts along dimension 0, may hold values from -6 to 6
- values: bfloat16 [64, 6, 4096], P(('groups', 'req')), parts along dimension 0, may hold values from -6 to 6
- gates: bfloat16 [64, 6, 4096], P(('groups', 'req')), parts along dimension 0, may hold values from -6 to 6
- states: float32 [64, 32, 128, 128], P(('groups', 'req')), parts along dimension 0, may hold values from -12 to 12
- new_slot: int32 [64], P(('groups', 'req')), parts along dimension 0, may hold values from 0 to 31, as said below
- norm_gain: float32 [4096], replicated, may hold values from 0.1 to 1.9
Outputs:
- output: bfloat16 [64, 6, 4096], P(('groups', 'req')), parts along dimension 0
The draws below stay inside these ranges and needn't reach their ends.
There are 2 independent parts, one for each index of `groups`. The reference program is written for one: setup_inputs(seed, part) draws one part's arguments, and reference() takes and returns one part's arrays. A program takes and returns all parts, laid end to end along the dimension named above; an argument that names none is the same for every part. Nothing has to cross between parts.
Inputs may be any that keep to these rules, and one draw needn't show every extreme that they name: `new_slot`: A permutation of the slots. On one device (its 2 slots) at most 1 request change slot, and exactly 1 do on some devices; a request that changes slot never keeps it.
All inputs are finite; a program needn't handle non-finite values.
Results may differ from the reference program's by a relative error of at most 0.001.
Values sent between devices are 32-bit elements; how exact they have to be, the bound alone decides.
No kernel may reach another device: no remote copies, remote signals or barrier semaphores. Data moves between devices by JAX's collectives and lax.ppermute only.
A program may use at most 64 MiB of HBM per device.

```python
import jax
import jax.numpy as jnp
from jax import lax

D_HEAD = 128
HEADS = 32
SLOTS_DEV = 2
BEFORE = 3
STEPS = 6
MOVE_DEV = 1
REQUESTS = 32
WIDTH = 4096


def draw_states(key, part):
    key_scale, key_base = jax.random.split(key, 2)
    shape = (REQUESTS, HEADS, D_HEAD, D_HEAD)
    scales = jnp.exp(jax.random.uniform(key_scale, (REQUESTS, HEADS, 1, 1), jnp.float32, jnp.log(0.3), jnp.log(3.0)))
    return jnp.clip(jax.random.normal(key_base, shape, jnp.float32), -4.0, 4.0) * scales


def draw_new_slot(key, part):
    device_count = REQUESTS // SLOTS_DEV
    key_count, key_first, key_rank, key_order = jax.random.split(key, 4)
    counts = jax.random.randint(key_count, (device_count,), 0, MOVE_DEV + 1)
    first = jax.random.randint(key_first, (), 0, device_count)
    marks = jnp.arange(device_count)
    forced = (marks == first) | (marks == (first + 1) % device_count)
    counts = jnp.where(forced, MOVE_DEV, counts)
    ranks = jax.vmap(lambda sub: jax.random.permutation(sub, SLOTS_DEV))(jax.random.split(key_rank, device_count))
    moving = (ranks < counts[:, None]).reshape(-1)
    order_key = jax.random.permutation(key_order, REQUESTS)
    score = jnp.where(moving, order_key, REQUESTS + order_key)
    order = jnp.argsort(score, stable=True).astype(jnp.int32)
    moving_total = jnp.sum(moving.astype(jnp.int32))
    positions = jnp.arange(REQUESTS).astype(jnp.int32)
    following = order[(positions + 1) % moving_total]
    target = jnp.where(positions < moving_total, following, order)
    return jnp.zeros((REQUESTS,), jnp.int32).at[order].set(target.astype(jnp.int32))


def shard_levels(key, extent, cuts, low, high):
    factor_of = 1.0
    for position, shards_of in cuts:
        heights = jax.random.uniform(jax.random.fold_in(jax.random.fold_in(key, 6), position), (shards_of,), jnp.float32, low / len(cuts), high / len(cuts))
        factor_of = factor_of * jnp.repeat(jnp.exp(heights), extent[position] // shards_of).reshape((-1,) + (1,) * (len(extent) - 1 - position))
    return factor_of


def noise(rng, dims, scale, reach, cuts=(), dtype=jnp.bfloat16):
    factor_of = shard_levels(rng, dims, cuts, -0.22, 0.18) if cuts else 1.0
    result = jax.random.normal(rng, dims, jnp.float32) * scale * factor_of
    return jnp.minimum(jnp.maximum(result, -reach), reach).astype(dtype)


def setup_inputs(seed: int = 0, part: int = 0) -> dict:
    streams_of = jax.random.split(jax.random.key(seed), 8)
    part_splits = jax.random.split(jax.random.fold_in(streams_of[7], part), 8)
    return {
        "queries": noise(part_splits[0], (REQUESTS, STEPS, WIDTH), 1.0, 6.0, ((0, 16),)),
        "keys": noise(part_splits[1], (REQUESTS, STEPS, WIDTH), 1.0, 6.0, ((0, 16),)),
        "values": noise(part_splits[2], (REQUESTS, STEPS, WIDTH), 1.0, 6.0, ((0, 16),)),
        "gates": noise(part_splits[3], (REQUESTS, STEPS, WIDTH), 1.0, 6.0, ((0, 16),)),
        "states": draw_states(jax.random.fold_in(jax.random.fold_in(streams_of[7], part), 71), part),
        "new_slot": draw_new_slot(jax.random.fold_in(jax.random.fold_in(streams_of[7], part), 71), part),
        "norm_gain": jnp.clip(1.0 + 0.18 * jax.random.normal(streams_of[6], (WIDTH,), jnp.float32), 0.1, 1.9),
    }


def head_decay():
    order = jnp.arange(HEADS).astype(jnp.float32)
    slope = 2.0 ** (-8.0 * (order + 1.0) / (2.0 * HEADS))
    return jnp.exp(-slope)

def advance(current, query_row, key_row, value_row, gate_row, norm_gain):
    count = current.shape[0]
    query_act = jax.nn.silu(query_row.astype(jnp.float32)).reshape(count, HEADS, D_HEAD)
    key_act = jax.nn.silu(key_row.astype(jnp.float32)).reshape(count, HEADS, D_HEAD)
    value_act = jax.nn.silu(value_row.astype(jnp.float32)).reshape(count, HEADS, D_HEAD)
    current = head_decay()[None, :, None, None] * current + key_act[:, :, :, None] * value_act[:, :, None, :]
    mixed = jnp.einsum('nhi,nhij->nhj', query_act, current, precision=lax.Precision.HIGHEST)
    mixed = mixed.reshape(count, HEADS * D_HEAD)
    energy = lax.optimization_barrier(jnp.mean(mixed * mixed, axis=-1, keepdims=True))
    output = mixed * lax.rsqrt(energy + 1e-06) * norm_gain[None, :] * jax.nn.sigmoid(gate_row.astype(jnp.float32))
    return (current, output.astype(jnp.bfloat16))

def reference(queries, keys, values, gates, states, new_slot, norm_gain):

    def opening(request):
        current = states[request][None]
        row_list = []
        for moment in range(BEFORE):
            current, row = advance(current, queries[request, moment][None], keys[request, moment][None], values[request, moment][None], gates[request, moment][None], norm_gain)
            row_list.append(row[0])
        return (current[0], jnp.stack(row_list))
    slot_ids = jnp.arange(REQUESTS).astype(jnp.int32)
    mid_states, early_rows = lax.map(opening, slot_ids)
    inverse = jnp.zeros((REQUESTS,), jnp.int32).at[new_slot].set(slot_ids)

    def later(slot):
        anchor = inverse[slot]
        current = mid_states[anchor][None]
        row_list = []
        for moment in range(BEFORE, STEPS):
            current, row = advance(current, queries[slot, moment][None], keys[slot, moment][None], values[slot, moment][None], gates[slot, moment][None], norm_gain)
            row_list.append(row[0])
        return jnp.concatenate([early_rows[slot], jnp.stack(row_list)], axis=0)
    return lax.map(later, slot_ids)
```

```python
import functools

import jax
import jax.numpy as jnp
from jax import lax
from jax.experimental import pallas as pl
from jax.experimental.pallas import tpu as pltpu
from jax.sharding import PartitionSpec as P

BEFORE = 3
EPS = 1e-06
F32 = jnp.float32
BF16 = jnp.bfloat16
VMEM = pl.BlockSpec(memory_space=pltpu.VMEM)
SMEM = pl.BlockSpec(memory_space=pltpu.SMEM)
ANY = pl.BlockSpec(memory_space=pl.ANY)


def silu(x):
    return x / (1.0 + jnp.exp(-x))


def sigmoid(x):
    return 1.0 / (1.0 + jnp.exp(-x))


def moving_slot(slots_ref, count):
    base = lax.axis_index("req") * count
    place = jnp.int32(0)
    moves = slots_ref[0] != base
    for s in range(1, count):
        here = slots_ref[s] != base + s
        place = jnp.where(here, s, place)
        moves = jnp.logical_or(moves, here)
    return place, moves


def decay_power(heads, width, power):
    order = lax.broadcasted_iota(jnp.int32, (heads, width), 0).astype(F32)
    slope = jnp.exp2(-8.0 * (order + 1.0) / (2.0 * heads))
    return jnp.exp(slope * (-float(power)))


def split(x):
    high = x.astype(BF16)
    return high, (x - high.astype(F32)).astype(BF16)


def to_dense(source, target, slot, first, count, heads, width):
    for h in range(heads):
        rows = source[slot, :, h * width:(h + 1) * width].astype(F32)
        target[pl.ds(h, count, stride=heads), :] = rows[first:first + count]


def ask_kernel(slots_ref, queries_ref, out_ref, *, heads, width):
    count, steps, _ = queries_ref.shape
    place, _ = moving_slot(slots_ref, count)
    to_dense(queries_ref, out_ref, place, BEFORE, steps - BEFORE, heads, width)
    out_ref[...] = silu(out_ref[...])


def local_kernel(slots_ref, queries_ref, keys_ref, values_ref, gates_ref, gain_ref, states_ref,
                 out_ref, weight_ref, early_ref, late_ref,
                 state, qs, ks, vs, gs, lhs, prod, done, sems, *, heads, width, chunks):
    count, steps, _ = queries_ref.shape
    place, moves = moving_slot(slots_ref, count)
    order = [place] + [jnp.where(place == s, 0, s) for s in range(1, count)]
    size = heads // chunks

    def load(j, c):
        part = pl.ds(c * size, size)
        return pltpu.make_async_copy(
            states_ref.at[order[j], part], state.at[j, part], sems.at[j, c])

    for j in range(count):
        for c in range(chunks):
            load(j, c).start()
    decay = [decay_power(heads, width, p) for p in range(steps + 1)]
    gain = gain_ref[...]
    block = lambda ref, t: ref[t * heads:(t + 1) * heads, :]
    for j in range(count):
        slot = order[j]
        to_dense(queries_ref, qs, slot, 0, steps, heads, width)
        to_dense(keys_ref, ks, slot, 0, steps, heads, width)
        to_dense(values_ref, vs, slot, 0, steps, heads, width)
        to_dense(gates_ref, gs, slot, 0, steps, heads, width)
        q = [silu(block(qs, t)) for t in range(steps)]
        k = [silu(block(ks, t)) for t in range(steps)]
        v = [silu(block(vs, t)) for t in range(steps)]
        for t in range(steps):
            x = q[t] * decay[t + 1]
            high = x.astype(BF16).astype(F32)
            lhs[t * heads:(t + 1) * heads, :] = high
            lhs[(8 + t) * heads:(9 + t) * heads, :] = x - high
        mixed = []
        for t in range(steps):
            total = None
            far = None
            for s in range(t + 1):
                score = jnp.sum(q[t] * k[s], axis=1, keepdims=True)
                term = score * decay[t - s] * v[s]
                if t >= BEFORE and s < BEFORE:
                    far = term if far is None else far + term
                else:
                    total = term if total is None else total + term
            if j == 0 and t >= BEFORE:
                late_ref[0, (t - BEFORE) * heads:(t - BEFORE + 1) * heads, :] = total
            mixed.append(total if far is None else total + far)
        if j == 0:
            for s in range(BEFORE):
                early_ref[0, s * heads:(s + 1) * heads, :] = k[s]
                early_ref[1, s * heads:(s + 1) * heads, :] = v[s]
        for c in range(chunks):
            load(j, c).wait()
            for h in range(c * size, (c + 1) * size):
                high, low = split(state[j, h])
                weight = jnp.concatenate([high, low], axis=0)
                if j == 0:
                    weight_ref[h] = weight
                x = lhs[pl.ds(h, 16, stride=heads), :].astype(BF16)
                prod[pl.ds(h, 16, stride=heads), :] = jnp.dot(
                    jnp.concatenate([x, x], axis=1), weight, preferred_element_type=F32)
        for t in range(steps):
            x = mixed[t] + block(prod, t) + block(prod, 8 + t)
            energy = jnp.mean(x * x)
            scale = gain * sigmoid(block(gs, t))
            if j == 0 and t >= BEFORE:
                late_ref[1, (t - BEFORE) * heads:(t - BEFORE + 1) * heads, :] = scale
            done[t * heads:(t + 1) * heads, :] = x * lax.rsqrt(energy + EPS) * scale
        for h in range(heads):
            rows = done[pl.ds(h, steps, stride=heads), :]
            out_ref[slot, :, h * width:(h + 1) * width] = rows.astype(BF16)


def answer_kernel(ask_ref, weight_ref, early_ref, out_ref, lhs, prod, *, heads, width, late):
    block = lambda ref, t: ref[t * heads:(t + 1) * heads, :]
    q = [block(ask_ref, t) for t in range(late)]
    for t in range(late):
        x = q[t] * decay_power(heads, width, t + BEFORE + 1)
        high = x.astype(BF16).astype(F32)
        lhs[t * heads:(t + 1) * heads, :] = high
        lhs[(late + t) * heads:(late + t + 1) * heads, :] = x - high
    for h in range(heads):
        x = lhs[pl.ds(h, 2 * late, stride=heads), :].astype(BF16)
        prod[pl.ds(h, 2 * late, stride=heads), :] = jnp.dot(
            jnp.concatenate([x, x], axis=1), weight_ref[h], preferred_element_type=F32)
    for t in range(late):
        total = block(prod, t) + block(prod, late + t)
        for s in range(BEFORE):
            score = jnp.sum(q[t] * block(early_ref.at[0], s), axis=1, keepdims=True)
            total = total + score * decay_power(heads, width, t + BEFORE - s) * block(
                early_ref.at[1], s)
        out_ref[t * heads:(t + 1) * heads, :] = total


def finish_kernel(slots_ref, base_ref, late_ref, *refs, heads, width, late):
    parts, out_ref, done = refs[:-2], refs[-2], refs[-1]
    count, steps, _ = base_ref.shape
    place, moves = moving_slot(slots_ref, count)
    out_ref[...] = base_ref[...]

    @pl.when(moves)
    def _():
        for t in range(late):
            part = slice(t * heads, (t + 1) * heads)
            x = late_ref[0, part, :]
            for ref in parts:
                x = x + ref[part, :]
            energy = jnp.mean(x * x)
            row = (t + BEFORE) * heads
            done[row:row + heads, :] = x * lax.rsqrt(energy + EPS) * late_ref[1, part, :]
        fresh = lax.broadcasted_iota(jnp.int32, (steps, width), 0) >= BEFORE
        for h in range(heads):
            lanes = slice(h * width, (h + 1) * width)
            rows = done[pl.ds(h, steps, stride=heads), :]
            old = base_ref[place, :, lanes].astype(F32)
            out_ref[place, :, lanes] = jnp.where(fresh, rows, old).astype(BF16)


def near_square(total):
    inner = total
    for d in range(1, total + 1):
        if total % d == 0 and d * d >= total:
            inner = d
            break
    return inner, total // inner


def turn(position, step, size):
    return position ^ step if size & (size - 1) == 0 else (position + step) % size


def unturn(position, step, size):
    return position ^ step if size & (size - 1) == 0 else (position - step) % size


def on_device(queries, keys, values, gates, states, new_slot, norm_gain):
    count, steps, features = queries.shape
    heads, width = states.shape[1], states.shape[2]
    late = steps - BEFORE
    peers = lax.axis_size("req")
    inner, outer = near_square(peers)
    me = lax.axis_index("req")
    my_inner, my_outer = me % inner, me // inner

    def send_inner(x, k):
        return lax.ppermute(x, "req", [
            (o * inner + i, o * inner + turn(i, k, inner))
            for o in range(outer) for i in range(inner)])

    def send_outer(x, k):
        return lax.ppermute(x, "req", [
            (o * inner + i, turn(o, k, outer) * inner + i)
            for o in range(outer) for i in range(inner)])

    def target(slots, device):
        own = slots // count == device
        far = jnp.sum(jnp.where(own, 0, slots // count))
        return jnp.where(jnp.all(own), device, far)

    compact = dict(heads=heads, width=width)
    dense = jax.ShapeDtypeStruct((late * heads, width), F32)
    ask = pl.pallas_call(
        functools.partial(ask_kernel, **compact),
        out_shape=dense, in_specs=[SMEM, VMEM], out_specs=VMEM,
        name="ask",
    )(new_slot, queries)

    column = [ask] + [send_outer(ask, k) for k in range(1, outer)]
    wishes = [new_slot] + [send_inner(new_slot, k) for k in range(1, inner)]

    chunks = 4
    base, weight, early, late_parts = pl.pallas_call(
        functools.partial(local_kernel, chunks=chunks, **compact),
        out_shape=(
            jax.ShapeDtypeStruct((count, steps, features), BF16),
            jax.ShapeDtypeStruct((heads, 2 * width, width), BF16),
            jax.ShapeDtypeStruct((2, BEFORE * heads, width), F32),
            jax.ShapeDtypeStruct((2, late * heads, width), F32),
        ),
        in_specs=[SMEM, VMEM, VMEM, VMEM, VMEM, VMEM, ANY],
        out_specs=(VMEM, VMEM, VMEM, VMEM),
        scratch_shapes=[
            pltpu.VMEM((count, heads, width, width), F32),
            pltpu.VMEM((steps * heads, width), F32),
            pltpu.VMEM((steps * heads, width), F32),
            pltpu.VMEM((steps * heads, width), F32),
            pltpu.VMEM((steps * heads, width), F32),
            pltpu.VMEM((16 * heads, width), F32),
            pltpu.VMEM((16 * heads, width), F32),
            pltpu.VMEM((steps * heads, width), F32),
            pltpu.SemaphoreType.DMA((count, chunks)),
        ],
        compiler_params=pltpu.CompilerParams(vmem_limit_bytes=24 * 2**20),
        cost_estimate=pl.CostEstimate(
            flops=2 * count * heads * 16 * 2 * width * width,
            bytes_accessed=states.size * 4, transcendentals=0),
        name="local",
    )(new_slot, queries, keys, values, gates, norm_gain.reshape(heads, width), states)

    mates = [my_outer * inner + unturn(my_inner, k, inner) for k in range(inner)]
    wants = [target(wish, mate) for wish, mate in zip(wishes, mates)]

    def choose(options, index, size, mine):
        result = options[0]
        for k in range(1, size):
            result = jnp.where(unturn(mine, k, size) == index, options[k], result)
        return result

    def pick_outer(device):
        return choose(column, device // inner, outer, my_outer)

    sent = [pick_outer(wants[0])]
    for k in range(1, inner):
        back = [b for b in range(1, inner) if all(
            unturn(i, b, inner) == turn(i, k, inner) for i in range(inner))][0]
        sent.append(send_inner(pick_outer(wants[back]), k))
    found = choose(sent, wants[0] % inner, inner, my_inner)

    answer = pl.pallas_call(
        functools.partial(answer_kernel, late=late, **compact),
        out_shape=dense, in_specs=[VMEM, VMEM, VMEM], out_specs=VMEM,
        scratch_shapes=[
            pltpu.VMEM((2 * late * heads, width), F32),
            pltpu.VMEM((2 * late * heads, width), F32),
        ],
        compiler_params=pltpu.CompilerParams(vmem_limit_bytes=24 * 2**20),
        name="answer",
    )(found, weight, early)

    replies = [answer] + [send_inner(answer, k) for k in range(1, inner)]

    def reply_for(device):
        result = jnp.zeros_like(answer)
        for reply, want in zip(replies, wants):
            result = jnp.where(want == device, reply, result)
        return result

    parts = [reply_for(me)]
    for k in range(1, outer):
        parts.append(send_outer(reply_for(turn(my_outer, k, outer) * inner + my_inner), k))

    return pl.pallas_call(
        functools.partial(finish_kernel, late=late, **compact),
        out_shape=jax.ShapeDtypeStruct((count, steps, features), BF16),
        in_specs=[SMEM, VMEM, VMEM] + [VMEM] * outer, out_specs=VMEM,
        scratch_shapes=[pltpu.VMEM((steps * heads, width), F32)],
        name="finish",
    )(new_slot, base, late_parts, *parts)


def solution(mesh):
    rows = P(("groups", "req"), None, None)
    in_specs = (rows, rows, rows, rows, P(("groups", "req"), None, None, None),
                P(("groups", "req")), P())
    return jax.shard_map(
        on_device, mesh=mesh, in_specs=in_specs, out_specs=rows, check_vma=False)
```

```python
import functools

import jax
import jax.numpy as jnp
from jax import lax
from jax.experimental import pallas as pl
from jax.experimental.pallas import tpu as pltpu
from jax.sharding import PartitionSpec as P

BEFORE = 3
EPS = 1e-06
F32 = jnp.float32
BF16 = jnp.bfloat16
MIB = 2**20
VMEM = pl.BlockSpec(memory_space=pltpu.VMEM)
SMEM = pl.BlockSpec(memory_space=pltpu.SMEM)
HBM = pl.BlockSpec(memory_space=pltpu.HBM)


def silu(x):
    return x / (1.0 + jnp.exp(-x))


def sigmoid(x):
    return 1.0 / (1.0 + jnp.exp(-x))


def moving_slot(slots_ref, count):
    base = lax.axis_index("req") * count
    place = jnp.int32(0)
    moves = slots_ref[0] != base
    for s in range(1, count):
        here = slots_ref[s] != base + s
        place = jnp.where(here, s, place)
        moves = jnp.logical_or(moves, here)
    return place, moves


def wanted_device(slots_ref, device, count):
    result = device
    for s in range(count):
        owner = lax.div(slots_ref[s], jnp.int32(count))
        result = jnp.where(owner != device, owner, result)
    return result


def head_slope(heads, width):
    order = lax.broadcasted_iota(jnp.int32, (heads, width), 0).astype(F32)
    return jnp.exp2(-8.0 * (order + 1.0) / (2.0 * heads))


def decay_power(slope, power):
    return jnp.exp(slope * (-float(power)))


def split(x):
    high = x.astype(BF16)
    return high, (x - high.astype(F32)).astype(BF16)


def extract(packed, place, count):
    rows = packed.shape[0] // count
    result = packed[pl.ds(0, rows, stride=count), :]
    for s in range(1, count):
        result = jnp.where(place == s, packed[pl.ds(s, rows, stride=count), :], result)
    return result


def turn(position, step, size):
    return position ^ step if size & (size - 1) == 0 else (position + step) % size


def unturn(position, step, size):
    return position ^ step if size & (size - 1) == 0 else (position - step) % size


def inverse_step(step, size):
    return step if size & (size - 1) == 0 else (size - step) % size


def choose(options, index, mine, size):
    result = options[0][...]
    for k in range(1, size):
        result = jnp.where(unturn(mine, k, size) == index, options[k][...], result)
    return result


def ask_kernel(slots_ref, queries_ref, out_ref, rows_ref, wide, sem, *, count):
    late = rows_ref.shape[0]
    first = queries_ref.shape[0] - late
    copy = pltpu.make_async_copy(queries_ref.at[pl.ds(first, late)], rows_ref, sem)
    copy.start()
    copy.wait()
    place, _ = moving_slot(slots_ref, count)
    wide[...] = rows_ref[...].astype(F32)
    out_ref[...] = silu(extract(wide, place, count))


def prepare_kernel(slots_ref, keys_ref, values_ref, states_ref, weight_ref, early_ref,
                   state, wide, sems, *, count, chunks):
    heads = states_ref.shape[1]
    size = heads // chunks
    place, _ = moving_slot(slots_ref, count)

    def load(c):
        part = pl.ds(c * size, size)
        return pltpu.make_async_copy(states_ref.at[place, part], state.at[part], sems.at[c])

    for c in range(chunks):
        load(c).start()
    rows = wide.shape[0]
    for n, ref in enumerate((keys_ref, values_ref)):
        wide[...] = ref[:rows, :].astype(F32)
        early_ref[n] = silu(extract(wide, place, count))
    for c in range(chunks):
        load(c).wait()
        for h in range(c * size, (c + 1) * size):
            weight_ref[h] = jnp.concatenate(split(state[h]), axis=0)


def route_kernel(*refs, inner, outer, count):
    wishes, column = refs[:inner], refs[inner:inner + outer]
    outs = refs[inner + outer:]
    me = lax.axis_index("req")
    my_inner, my_outer = lax.rem(me, inner), lax.div(me, inner)
    for k in range(inner):
        back = inverse_step(k, inner)
        mate = my_outer * inner + unturn(my_inner, back, inner)
        wanted = wanted_device(wishes[back], mate, count)
        outs[k][...] = choose(column, lax.div(wanted, inner), my_outer, outer)


def answer_kernel(slots_ref, *refs, inner, count, late, heads, width):
    found, (weight_ref, early_ref, out_ref, lhs, prod) = refs[:inner], refs[inner:]
    me = lax.axis_index("req")
    wanted = wanted_device(slots_ref, me, count)
    block = lambda ref, t: ref[t * heads:(t + 1) * heads, :]
    rows = choose(found, lax.rem(wanted, inner), lax.rem(me, inner), inner)
    q = [rows[t * heads:(t + 1) * heads, :] for t in range(late)]
    slope = head_slope(heads, width)
    for t in range(late):
        x = q[t] * decay_power(slope, t + BEFORE + 1)
        high = x.astype(BF16).astype(F32)
        lhs[t * heads:(t + 1) * heads, :] = high
        lhs[(late + t) * heads:(late + t + 1) * heads, :] = x - high
    for h in range(heads):
        x = lhs[pl.ds(h, 2 * late, stride=heads), :].astype(BF16)
        prod[pl.ds(h, 2 * late, stride=heads), :] = jnp.dot(
            jnp.concatenate([x, x], axis=1), weight_ref[h], preferred_element_type=F32)
    for t in range(late):
        total = block(prod, t) + block(prod, late + t)
        for s in range(BEFORE):
            score = jnp.sum(q[t] * block(early_ref.at[0], s), axis=1, keepdims=True)
            total = total + score * decay_power(slope, t + BEFORE - s) * block(
                early_ref.at[1], s)
        out_ref[t * heads:(t + 1) * heads, :] = total


def reply_kernel(*refs, inner, outer, count):
    wishes, replies = refs[:inner], refs[inner:2 * inner]
    outs = refs[2 * inner:]
    me = lax.axis_index("req")
    my_inner, my_outer = lax.rem(me, inner), lax.div(me, inner)
    wanted = [
        wanted_device(wishes[k], my_outer * inner + unturn(my_inner, k, inner), count)
        for k in range(inner)]
    for k in range(outer):
        device = turn(my_outer, k, outer) * inner + my_inner
        result = jnp.where(wanted[0] == device, replies[0][...], 0.0)
        for n in range(1, inner):
            result = jnp.where(wanted[n] == device, replies[n][...], result)
        outs[k][...] = result


def local_kernel(slots_ref, queries_ref, keys_ref, values_ref, gates_ref, gain_ref, own_ref,
                 states_ref, out_ref, late_ref, state, lhs, prod, wide, sems, *, count, chunks):
    heads, width = states_ref.shape[1], states_ref.shape[2]
    span = heads * count
    steps = queries_ref.shape[0] // span
    late = steps - BEFORE
    size = heads // chunks
    place, _ = moving_slot(slots_ref, count)

    def load(j, c):
        part = pl.ds(c * size, size)
        return pltpu.make_async_copy(states_ref.at[j, part], state.at[j, part], sems.at[j, c])

    for j in range(count):
        for c in range(chunks):
            load(j, c).start()

    def spread(x):
        for s in range(count):
            wide[pl.ds(s, heads, stride=count), :] = x
        return wide[:span, :]

    slope = spread(head_slope(heads, width))
    gain = spread(gain_ref[...])
    decay = [decay_power(slope, p) for p in range(steps + 1)]
    block = lambda ref, t: ref[t * span:(t + 1) * span, :]
    q = [silu(block(queries_ref, t).astype(F32)) for t in range(steps)]
    k = [silu(block(keys_ref, t).astype(F32)) for t in range(steps)]
    v = [silu(block(values_ref, t).astype(F32)) for t in range(steps)]
    for t in range(steps):
        x = q[t] * decay[t + 1]
        high = x.astype(BF16).astype(F32)
        lhs[t * span:(t + 1) * span, :] = high
        lhs[(8 + t) * span:(9 + t) * span, :] = x - high
    mixed = []
    for t in range(steps):
        total = None
        far = None
        for s in range(t + 1):
            score = jnp.sum(q[t] * k[s], axis=1, keepdims=True)
            term = score * decay[t - s] * v[s]
            if t >= BEFORE and s < BEFORE:
                far = term if far is None else far + term
            else:
                total = term if total is None else total + term
        if t >= BEFORE:
            wide[(t - BEFORE) * span:(t - BEFORE + 1) * span, :] = total
        mixed.append(total if far is None else total + far)
    late_ref[0] = extract(wide, place, count) + own_ref[...]
    scale = [gain * sigmoid(block(gates_ref, t).astype(F32)) for t in range(steps)]
    for t in range(late):
        wide[t * span:(t + 1) * span, :] = scale[BEFORE + t]
    late_ref[1] = extract(wide, place, count)
    for j in range(count):
        for c in range(chunks):
            load(j, c).wait()
            for h in range(c * size, (c + 1) * size):
                rows = pl.ds(h * count + j, 16, stride=span)
                x = lhs[rows, :].astype(BF16)
                prod[rows, :] = jnp.dot(
                    jnp.concatenate([x, x], axis=1),
                    jnp.concatenate(split(state[j, h]), axis=0),
                    preferred_element_type=F32)
    slot = lax.rem(lax.broadcasted_iota(jnp.int32, (span, 1), 0), jnp.int32(count))
    for t in range(steps):
        x = mixed[t] + block(prod, t) + block(prod, 8 + t)
        sums = jnp.sum(x * x, axis=1, keepdims=True)
        energy = jnp.zeros((span, 1), F32)
        for s in range(count):
            whole = jnp.sum(jnp.where(slot == s, sums, 0.0), axis=0, keepdims=True)
            energy = jnp.where(slot == s, whole, energy)
        factor = lax.rsqrt(energy * (1.0 / (heads * width)) + EPS)
        out_ref[t * span:(t + 1) * span, :] = (x * factor * scale[t]).astype(BF16)


def finish_kernel(slots_ref, base_ref, late_ref, *refs, count, heads):
    parts, out_ref, wide = refs[:-2], refs[-2], refs[-1]
    place, moves = moving_slot(slots_ref, count)
    rows = wide.shape[0]
    first = base_ref.shape[0] - rows
    single = rows // count
    wide[...] = base_ref[first:, :].astype(F32)
    for t in range(single // heads):
        part = slice(t * heads, (t + 1) * heads)
        x = late_ref[0, part, :]
        for ref in parts:
            x = x + ref[part, :]
        y = x * lax.rsqrt(jnp.mean(x * x) + EPS) * late_ref[1, part, :]
        for s in range(count):
            here = pl.ds(t * heads * count + s, heads, stride=count)
            use = jnp.logical_and(moves, place == s)
            wide[here, :] = jnp.where(use, y, wide[here, :])
    out_ref[:first, :] = base_ref[:first, :]
    out_ref[first:, :] = wide[...].astype(BF16)


def near_square(total):
    return next(
        (d, total // d) for d in range(1, total + 1) if total % d == 0 and d * d >= total)


def on_device(queries, keys, values, gates, states, new_slot, norm_gain):
    count, steps, features = queries.shape
    heads, width = states.shape[1], states.shape[2]
    late = steps - BEFORE
    packed_rows, single_rows = steps * heads * count, late * heads
    inner, outer = near_square(lax.axis_size("req"))

    def pack(x):
        return x.reshape(count, steps, heads, width).transpose(1, 2, 0, 3).reshape(
            packed_rows, width)

    def unpack(x):
        return x.reshape(steps, heads, count, width).transpose(2, 0, 1, 3).reshape(
            count, steps, features)

    def send_inner(x, k):
        return lax.ppermute(x, "req", [
            (o * inner + i, o * inner + int(turn(i, k, inner)))
            for o in range(outer) for i in range(inner)])

    def send_outer(x, k):
        return lax.ppermute(x, "req", [
            (o * inner + i, int(turn(o, k, outer)) * inner + i)
            for o in range(outer) for i in range(inner)])

    def params(limit):
        return pltpu.CompilerParams(vmem_limit_bytes=limit * MIB)

    queries, keys, values, gates = pack(queries), pack(keys), pack(values), pack(gates)
    single = jax.ShapeDtypeStruct((single_rows, width), F32)
    late_packed = pltpu.VMEM((late * heads * count, width), F32)

    ask = pl.pallas_call(
        functools.partial(ask_kernel, count=count),
        out_shape=single, in_specs=[SMEM, HBM], out_specs=VMEM,
        scratch_shapes=[pltpu.VMEM((late * heads * count, width), BF16), late_packed,
                        pltpu.SemaphoreType.DMA],
        compiler_params=params(4), name="ask",
    )(new_slot, queries)

    column = [ask] + [send_outer(ask, k) for k in range(1, outer)]
    wishes = [new_slot] + [send_inner(new_slot, k) for k in range(1, inner)]

    chunks = 8
    weight, early = pl.pallas_call(
        functools.partial(prepare_kernel, count=count, chunks=chunks),
        out_shape=(jax.ShapeDtypeStruct((heads, 2 * width, width), BF16),
                   jax.ShapeDtypeStruct((2, BEFORE * heads, width), F32)),
        in_specs=[SMEM, VMEM, VMEM, HBM], out_specs=(VMEM, VMEM),
        scratch_shapes=[pltpu.VMEM((heads, width, width), F32),
                        pltpu.VMEM((BEFORE * heads * count, width), F32),
                        pltpu.SemaphoreType.DMA((chunks,))],
        compiler_params=params(12), name="prepare",
    )(new_slot, keys, values, states)

    asked = pl.pallas_call(
        functools.partial(route_kernel, inner=inner, outer=outer, count=count),
        out_shape=(single,) * inner,
        in_specs=[SMEM] * inner + [VMEM] * outer, out_specs=(VMEM,) * inner,
        compiler_params=params(4), name="route",
    )(*wishes, *column)
    found = [asked[0]] + [send_inner(asked[k], k) for k in range(1, inner)]

    answer = pl.pallas_call(
        functools.partial(answer_kernel, inner=inner, count=count, late=late, heads=heads,
                          width=width),
        out_shape=single, in_specs=[SMEM] + [VMEM] * (inner + 2), out_specs=VMEM,
        scratch_shapes=[pltpu.VMEM((2 * late * heads, width), F32)] * 2,
        compiler_params=params(8), name="answer",
    )(new_slot, *found, weight, early)
    replies = [answer] + [send_inner(answer, k) for k in range(1, inner)]

    sorted_replies = pl.pallas_call(
        functools.partial(reply_kernel, inner=inner, outer=outer, count=count),
        out_shape=(single,) * outer,
        in_specs=[SMEM] * inner + [VMEM] * inner, out_specs=(VMEM,) * outer,
        compiler_params=params(4), name="reply",
    )(*wishes, *replies)
    parts = [send_outer(sorted_replies[k], k) for k in range(1, outer)]

    chunks = 4
    base, late_rows = pl.pallas_call(
        functools.partial(local_kernel, count=count, chunks=chunks),
        out_shape=(jax.ShapeDtypeStruct((packed_rows, width), BF16),
                   jax.ShapeDtypeStruct((2, single_rows, width), F32)),
        in_specs=[SMEM] + [VMEM] * 6 + [HBM], out_specs=(VMEM, VMEM),
        scratch_shapes=[
            pltpu.VMEM((count, heads, width, width), F32),
            pltpu.VMEM((16 * heads * count, width), F32),
            pltpu.VMEM((16 * heads * count, width), F32),
            late_packed,
            pltpu.SemaphoreType.DMA((count, chunks)),
        ],
        compiler_params=params(16), name="local",
    )(new_slot, queries, keys, values, gates, norm_gain.reshape(heads, width),
      sorted_replies[0], states)

    return unpack(pl.pallas_call(
        functools.partial(finish_kernel, count=count, heads=heads),
        out_shape=jax.ShapeDtypeStruct((packed_rows, width), BF16),
        in_specs=[SMEM, VMEM, VMEM] + [VMEM] * (outer - 1), out_specs=VMEM,
        scratch_shapes=[late_packed],
        compiler_params=params(4), name="finish",
    )(new_slot, base, late_rows, *parts))


def solution(mesh):
    rows = P(("groups", "req"), None, None)
    in_specs = (rows, rows, rows, rows, P(("groups", "req"), None, None, None),
                P(("groups", "req")), P())
    return jax.shard_map(
        on_device, mesh=mesh, in_specs=in_specs, out_specs=rows, check_vma=False)
```

```python
import functools

import jax
import jax.numpy as jnp
from jax import lax
from jax.experimental import pallas as pl
from jax.experimental.pallas import tpu as pltpu
from jax.sharding import PartitionSpec as P

BEFORE = 3
EPS = 1e-06
F32 = jnp.float32
BF16 = jnp.bfloat16
MIB = 2**20
LARGE = 61
VMEM = pl.BlockSpec(memory_space=pltpu.VMEM)
SMEM = pl.BlockSpec(memory_space=pltpu.SMEM)
HBM = pl.BlockSpec(memory_space=pltpu.HBM)


def silu(x):
    return x / (1.0 + jnp.exp(-x))


def sigmoid(x):
    return 1.0 / (1.0 + jnp.exp(-x))


def moving_slot(slots_ref, count):
    base = lax.axis_index("req") * count
    place = jnp.int32(0)
    moves = slots_ref[0] != base
    for s in range(1, count):
        here = slots_ref[s] != base + s
        place = jnp.where(here, s, place)
        moves = jnp.logical_or(moves, here)
    return place, moves


def wanted_device(slots_ref, count):
    device = lax.axis_index("req")
    result = device
    for s in range(count):
        owner = lax.div(slots_ref[s], jnp.int32(count))
        result = jnp.where(owner != device, owner, result)
    return result


OUTER, INNER, SLOT = 0, 1, 2


def fact(ref, kind, rows):
    return jnp.broadcast_to(ref[kind:kind + 1, :], (rows, ref.shape[1]))


def head_slope(heads, width):
    order = lax.broadcasted_iota(jnp.int32, (heads, width), 0).astype(F32)
    return jnp.exp2(-8.0 * (order + 1.0) / (2.0 * heads))


def decay_power(slope, power):
    return jnp.exp(slope * (-float(power)))


def split(x):
    high = x.astype(BF16)
    return high, (x - high.astype(F32)).astype(BF16)


def extract(packed, place, count):
    rows = packed.shape[0] // count
    result = packed[pl.ds(0, rows, stride=count), :]
    for s in range(1, count):
        result = jnp.where(place == s, packed[pl.ds(s, rows, stride=count), :], result)
    return result


def turn(position, step, size):
    return position ^ step if size & (size - 1) == 0 else (position + step) % size


def unturn(position, step, size):
    return position ^ step if size & (size - 1) == 0 else (position - step) % size


def inverse_step(step, size):
    return step if size & (size - 1) == 0 else (size - step) % size


def choose(options, index, mine, size):
    result = options[0][...]
    for k in range(1, size):
        result = jnp.where(unturn(mine, k, size) == index, options[k][...], result)
    return result


def ask_kernel(slots_ref, queries_ref, out_ref, facts_ref, rows_ref, wide, sem, *, count, inner):
    late = rows_ref.shape[0]
    first = queries_ref.shape[0] - late
    copy = pltpu.make_async_copy(queries_ref.at[pl.ds(first, late)], rows_ref, sem)
    copy.start()
    place, moves = moving_slot(slots_ref, count)
    wanted = wanted_device(slots_ref, count)
    kind = lax.broadcasted_iota(jnp.int32, facts_ref.shape, 0)
    facts = jnp.where(kind == INNER, lax.rem(wanted, inner), jnp.where(moves, place, count))
    facts_ref[...] = jnp.where(kind == OUTER, lax.div(wanted, inner), facts)
    copy.wait()
    wide[...] = rows_ref[...].astype(F32)
    out_ref[...] = silu(extract(wide, place, count))


def prepare_kernel(slots_ref, keys_ref, values_ref, states_ref, weight_ref, early_ref,
                   state, wide, sems, *, count, chunks):
    heads = states_ref.shape[1]
    size = heads // chunks
    place, _ = moving_slot(slots_ref, count)

    def load(c):
        part = pl.ds(c * size, size)
        return pltpu.make_async_copy(states_ref.at[place, part], state.at[part], sems.at[c])

    for c in range(chunks):
        load(c).start()
    rows = wide.shape[0]
    for n, ref in enumerate((keys_ref, values_ref)):
        wide[...] = ref[:rows, :].astype(F32)
        early_ref[n] = silu(extract(wide, place, count))
    for c in range(chunks):
        load(c).wait()
        for h in range(c * size, (c + 1) * size):
            weight_ref[h] = jnp.concatenate(split(state[h]), axis=0)


def route_kernel(*refs, inner, outer):
    wishes, column = refs[:inner], refs[inner:inner + outer]
    outs = refs[inner + outer:]
    my_outer = lax.div(lax.axis_index("req"), inner)
    for k in range(inner):
        wish = fact(wishes[inverse_step(k, inner)], OUTER, outs[k].shape[0])
        outs[k][...] = choose(column, wish, my_outer, outer)


def answer_kernel(facts_ref, *refs, inner, late, heads, width):
    found, (weight_ref, early_ref, out_ref, lhs, prod) = refs[:inner], refs[inner:]
    my_inner = lax.rem(lax.axis_index("req"), inner)
    block = lambda ref, t: ref[t * heads:(t + 1) * heads, :]
    rows = choose(found, fact(facts_ref, INNER, late * heads), my_inner, inner)
    q = [rows[t * heads:(t + 1) * heads, :] for t in range(late)]
    slope = head_slope(heads, width)
    for t in range(late):
        x = q[t] * decay_power(slope, t + BEFORE + 1)
        high = x.astype(BF16).astype(F32)
        lhs[t * heads:(t + 1) * heads, :] = high
        lhs[(late + t) * heads:(late + t + 1) * heads, :] = x - high
    for h in range(heads):
        x = lhs[pl.ds(h, 2 * late, stride=heads), :].astype(BF16)
        prod[pl.ds(h, 2 * late, stride=heads), :] = jnp.dot(
            jnp.concatenate([x, x], axis=1), weight_ref[h], preferred_element_type=F32)
    for t in range(late):
        total = block(prod, t) + block(prod, late + t)
        for s in range(BEFORE):
            score = jnp.sum(q[t] * block(early_ref.at[0], s), axis=1, keepdims=True)
            total = total + score * decay_power(slope, t + BEFORE - s) * block(
                early_ref.at[1], s)
        out_ref[t * heads:(t + 1) * heads, :] = total


def reply_kernel(*refs, inner, outer):
    wishes, replies = refs[:inner], refs[inner:2 * inner]
    outs = refs[2 * inner:]
    me = lax.axis_index("req")
    my_inner, my_outer = lax.rem(me, inner), lax.div(me, inner)
    rows = outs[0].shape[0]
    owner = [
        jnp.where(fact(wish, INNER, rows) == my_inner, fact(wish, OUTER, rows), -1)
        for wish in wishes]
    for k in range(outer):
        result = 0.0
        for n in range(inner):
            result = jnp.where(owner[n] == turn(my_outer, k, outer), replies[n][...], result)
        outs[k][...] = result


def local_kernel(facts_ref, queries_ref, keys_ref, values_ref, gates_ref, gain_ref, own_ref,
                 states_ref, out_ref, last_ref, late_ref, state, lhs, prod, wide, sems, *, count, chunks):
    heads, width = states_ref.shape[1], states_ref.shape[2]
    span = heads * count
    steps = queries_ref.shape[0] // span
    late = steps - BEFORE
    size = heads // chunks
    place = fact(facts_ref, SLOT, late * heads)

    def load(j, c):
        part = pl.ds(c * size, size)
        return pltpu.make_async_copy(states_ref.at[j, part], state.at[j, part], sems.at[j, c])

    for j in range(count):
        for c in range(chunks):
            load(j, c).start()

    def spread(x):
        for s in range(count):
            wide[pl.ds(s, heads, stride=count), :] = x
        return wide[:span, :]

    slope = spread(head_slope(heads, width))
    gain = spread(gain_ref[...])
    decay = [decay_power(slope, p) for p in range(steps + 1)]
    block = lambda ref, t: ref[t * span:(t + 1) * span, :]
    q = [silu(block(queries_ref, t).astype(F32)) for t in range(steps)]
    k = [silu(block(keys_ref, t).astype(F32)) for t in range(steps)]
    v = [silu(block(values_ref, t).astype(F32)) for t in range(steps)]
    for t in range(steps):
        x = q[t] * decay[t + 1]
        high = x.astype(BF16).astype(F32)
        lhs[t * span:(t + 1) * span, :] = high
        lhs[(8 + t) * span:(9 + t) * span, :] = x - high
    mixed = []
    for t in range(steps):
        total = None
        far = None
        for s in range(t + 1):
            score = jnp.sum(q[t] * k[s], axis=1, keepdims=True)
            term = score * decay[t - s] * v[s]
            if t >= BEFORE and s < BEFORE:
                far = term if far is None else far + term
            else:
                total = term if total is None else total + term
        if t >= BEFORE:
            wide[(t - BEFORE) * span:(t - BEFORE + 1) * span, :] = total
        mixed.append(total if far is None else total + far)
    late_ref[0] = extract(wide, place, count) + own_ref[...]
    scale = [gain * sigmoid(block(gates_ref, t).astype(F32)) for t in range(steps)]
    for t in range(late):
        wide[t * span:(t + 1) * span, :] = scale[BEFORE + t]
    late_ref[1] = extract(wide, place, count)
    for j in range(count):
        for c in range(chunks):
            load(j, c).wait()
            for h in range(c * size, (c + 1) * size):
                rows = pl.ds(h * count + j, 16, stride=span)
                x = lhs[rows, :].astype(BF16)
                prod[rows, :] = jnp.dot(
                    jnp.concatenate([x, x], axis=1),
                    jnp.concatenate(split(state[j, h]), axis=0),
                    preferred_element_type=F32)
    slot = lax.rem(lax.broadcasted_iota(jnp.int32, (span, 1), 0), jnp.int32(count))
    for t in range(steps):
        x = mixed[t] + block(prod, t) + block(prod, 8 + t)
        sums = jnp.sum(x * x, axis=1, keepdims=True)
        energy = jnp.zeros((span, 1), F32)
        for s in range(count):
            whole = jnp.sum(jnp.where(slot == s, sums, 0.0), axis=0, keepdims=True)
            energy = jnp.where(slot == s, whole, energy)
        factor = lax.rsqrt(energy * (1.0 / (heads * width)) + EPS)
        y = (x * factor * scale[t]).astype(BF16)
        out_ref[t * span:(t + 1) * span, :] = y
        if t >= BEFORE:
            last_ref[(t - BEFORE) * span:(t - BEFORE + 1) * span, :] = y


def finish_kernel(facts_ref, base_ref, last_ref, late_ref, *refs, count, heads):
    parts, (out_ref, rows_ref, wide, sem) = refs[:-4], refs[-4:]
    wide[...] = last_ref[...].astype(F32)
    place = fact(facts_ref, SLOT, heads)
    for t in range(late_ref.shape[1] // heads):
        part = slice(t * heads, (t + 1) * heads)
        x = late_ref[0, part, :]
        for ref in parts:
            x = x + ref[part, :]
        y = x * lax.rsqrt(jnp.mean(x * x) + EPS) * late_ref[1, part, :]
        for s in range(count):
            here = pl.ds(t * heads * count + s, heads, stride=count)
            wide[here, :] = jnp.where(place == s, y, wide[here, :])
    rows_ref[...] = wide[...].astype(BF16)
    rows = rows_ref.shape[0]
    copy = pltpu.make_async_copy(
        rows_ref, out_ref.at[pl.ds(out_ref.shape[0] - rows, rows)], sem)
    copy.start()
    copy.wait()


def near_square(total):
    return next(
        (d, total // d) for d in range(1, total + 1) if total % d == 0 and d * d >= total)


def on_device(queries, keys, values, gates, states, new_slot, norm_gain):
    count, steps, features = queries.shape
    heads, width = states.shape[1], states.shape[2]
    late = steps - BEFORE
    packed_rows, single_rows = steps * heads * count, late * heads
    inner, outer = near_square(lax.axis_size("req"))

    def pack(x):
        return x.reshape(count, steps, heads, width).transpose(1, 2, 0, 3).reshape(
            packed_rows, width)

    def unpack(x):
        return x.reshape(steps, heads, count, width).transpose(2, 0, 1, 3).reshape(
            count, steps, features)

    def send_inner(x, k):
        return lax.ppermute(x, "req", [
            (o * inner + i, o * inner + int(turn(i, k, inner)))
            for o in range(outer) for i in range(inner)])

    def send_outer(x, k):
        return lax.ppermute(x, "req", [
            (o * inner + i, int(turn(o, k, outer)) * inner + i)
            for o in range(outer) for i in range(inner)])

    def params(limit):
        return pltpu.CompilerParams(vmem_limit_bytes=limit * MIB)

    queries, keys, values, gates = pack(queries), pack(keys), pack(values), pack(gates)
    single = jax.ShapeDtypeStruct((single_rows, width), F32)
    late_packed = pltpu.VMEM((late * heads * count, width), F32)

    late_rows = jax.ShapeDtypeStruct((late * heads * count, width), BF16)
    late_bf16 = pltpu.VMEM(late_rows.shape, BF16)

    ask, facts = pl.pallas_call(
        functools.partial(ask_kernel, count=count, inner=inner),
        out_shape=(single, jax.ShapeDtypeStruct((8, width), jnp.int32)),
        in_specs=[SMEM, HBM], out_specs=(VMEM, VMEM),
        scratch_shapes=[late_bf16, late_packed, pltpu.SemaphoreType.DMA],
        compiler_params=params(LARGE), name="ask",
    )(new_slot, queries)

    column = [ask] + [send_outer(ask, k) for k in range(1, outer)]
    wishes = [facts] + [send_inner(facts, k) for k in range(1, inner)]

    chunks = 8
    weight, early = pl.pallas_call(
        functools.partial(prepare_kernel, count=count, chunks=chunks),
        out_shape=(jax.ShapeDtypeStruct((heads, 2 * width, width), BF16),
                   jax.ShapeDtypeStruct((2, BEFORE * heads, width), F32)),
        in_specs=[SMEM, VMEM, VMEM, HBM], out_specs=(VMEM, VMEM),
        scratch_shapes=[pltpu.VMEM((heads, width, width), F32),
                        pltpu.VMEM((BEFORE * heads * count, width), F32),
                        pltpu.SemaphoreType.DMA((chunks,))],
        compiler_params=params(LARGE), name="prepare",
    )(new_slot, keys, values, states)

    asked = pl.pallas_call(
        functools.partial(route_kernel, inner=inner, outer=outer),
        out_shape=(single,) * inner,
        in_specs=[VMEM] * (inner + outer), out_specs=(VMEM,) * inner,
        compiler_params=params(4), name="route",
    )(*wishes, *column)
    found = [asked[0]] + [send_inner(asked[k], k) for k in range(1, inner)]

    answer = pl.pallas_call(
        functools.partial(answer_kernel, inner=inner, late=late, heads=heads, width=width),
        out_shape=single, in_specs=[VMEM] * (inner + 3), out_specs=VMEM,
        scratch_shapes=[pltpu.VMEM((2 * late * heads, width), F32)] * 2,
        compiler_params=params(8), name="answer",
    )(facts, *found, weight, early)
    replies = [answer] + [send_inner(answer, k) for k in range(1, inner)]

    sorted_replies = pl.pallas_call(
        functools.partial(reply_kernel, inner=inner, outer=outer),
        out_shape=(single,) * outer,
        in_specs=[VMEM] * (2 * inner), out_specs=(VMEM,) * outer,
        compiler_params=params(4), name="reply",
    )(*wishes, *replies)
    parts = [send_outer(sorted_replies[k], k) for k in range(1, outer)]

    chunks = 4
    output = jax.ShapeDtypeStruct((packed_rows, width), BF16)
    base, last, partial = pl.pallas_call(
        functools.partial(local_kernel, count=count, chunks=chunks),
        out_shape=(output, late_rows, jax.ShapeDtypeStruct((2, single_rows, width), F32)),
        in_specs=[VMEM] * 7 + [HBM], out_specs=(VMEM, VMEM, VMEM),
        scratch_shapes=[
            pltpu.VMEM((count, heads, width, width), F32),
            pltpu.VMEM((16 * heads * count, width), F32),
            pltpu.VMEM((16 * heads * count, width), F32),
            late_packed,
            pltpu.SemaphoreType.DMA((count, chunks)),
        ],
        compiler_params=params(LARGE), name="local",
    )(facts, queries, keys, values, gates, norm_gain.reshape(heads, width),
      sorted_replies[0], states)

    return unpack(pl.pallas_call(
        functools.partial(finish_kernel, count=count, heads=heads),
        out_shape=output, in_specs=[VMEM, HBM] + [VMEM] * (outer + 1), out_specs=HBM,
        scratch_shapes=[late_bf16, late_packed, pltpu.SemaphoreType.DMA],
        input_output_aliases={1: 0},
        compiler_params=params(4), name="finish",
    )(facts, base, last, partial, *parts))


def solution(mesh):
    rows = P(("groups", "req"), None, None)
    in_specs = (rows, rows, rows, rows, P(("groups", "req"), None, None, None),
                P(("groups", "req")), P())
    return jax.shard_map(
        on_device, mesh=mesh, in_specs=in_specs, out_specs=rows, check_vma=False)
```

```python
import functools

import jax
import jax.numpy as jnp
from jax import lax
from jax.experimental import pallas as pl
from jax.experimental.pallas import tpu as pltpu
from jax.sharding import PartitionSpec as P

BEFORE = 3
EPS = 1e-06
F32 = jnp.float32
BF16 = jnp.bfloat16
MIB = 2**20
VMEM = pl.BlockSpec(memory_space=pltpu.VMEM)
SMEM = pl.BlockSpec(memory_space=pltpu.SMEM)
HBM = pl.BlockSpec(memory_space=pltpu.HBM)


def silu(x):
    return x / (1.0 + jnp.exp(-x))


def sigmoid(x):
    return 1.0 / (1.0 + jnp.exp(-x))


def moving_slot(slots_ref, count):
    base = lax.axis_index("req") * count
    place = jnp.int32(0)
    moves = slots_ref[0] != base
    for s in range(1, count):
        here = slots_ref[s] != base + s
        place = jnp.where(here, s, place)
        moves = jnp.logical_or(moves, here)
    return place, moves


def wanted_device(slots_ref, count):
    device = lax.axis_index("req")
    result = device
    for s in range(count):
        owner = lax.div(slots_ref[s], jnp.int32(count))
        result = jnp.where(owner != device, owner, result)
    return result


OUTER, INNER, SLOT = 0, 1, 2


def fact(ref, kind, rows):
    return jnp.broadcast_to(ref[kind:kind + 1, :], (rows, ref.shape[1]))


def head_slope(heads, width):
    order = lax.broadcasted_iota(jnp.int32, (heads, width), 0).astype(F32)
    return jnp.exp2(-8.0 * (order + 1.0) / (2.0 * heads))


def decay_power(slope, power):
    return jnp.exp(slope * (-float(power)))


def split(x):
    high = x.astype(BF16)
    return high, (x - high.astype(F32)).astype(BF16)


def extract(packed, place, count):
    rows = packed.shape[0] // count
    result = packed[pl.ds(0, rows, stride=count), :]
    for s in range(1, count):
        result = jnp.where(place == s, packed[pl.ds(s, rows, stride=count), :], result)
    return result


def turn(position, step, size):
    return position ^ step if size & (size - 1) == 0 else (position + step) % size


def unturn(position, step, size):
    return position ^ step if size & (size - 1) == 0 else (position - step) % size


def inverse_step(step, size):
    return step if size & (size - 1) == 0 else (size - step) % size


def choose(options, index, mine, size):
    result = options[0][...]
    for k in range(1, size):
        result = jnp.where(unturn(mine, k, size) == index, options[k][...], result)
    return result


def ask_kernel(slots_ref, queries_ref, out_ref, facts_ref, rows_ref, wide, sem, *, count, inner):
    late = rows_ref.shape[0]
    first = queries_ref.shape[0] - late
    copy = pltpu.make_async_copy(queries_ref.at[pl.ds(first, late)], rows_ref, sem)
    copy.start()
    place, moves = moving_slot(slots_ref, count)
    wanted = wanted_device(slots_ref, count)
    kind = lax.broadcasted_iota(jnp.int32, facts_ref.shape, 0)
    facts = jnp.where(kind == INNER, lax.rem(wanted, inner), jnp.where(moves, place, count))
    facts_ref[...] = jnp.where(kind == OUTER, lax.div(wanted, inner), facts)
    copy.wait()
    wide[...] = rows_ref[...].astype(F32)
    out_ref[...] = silu(extract(wide, place, count))


def prepare_kernel(slots_ref, keys_ref, values_ref, states_ref, weight_ref, early_ref,
                   state, rows_ref, wide, sems, row_sems, *, count, chunks):
    heads = states_ref.shape[1]
    size = heads // chunks
    place, _ = moving_slot(slots_ref, count)
    copies = [
        pltpu.make_async_copy(
            ref.at[pl.ds(0, wide.shape[0])], rows_ref.at[n], row_sems.at[n])
        for n, ref in enumerate((keys_ref, values_ref))]
    for copy in copies:
        copy.start()

    def load(c):
        part = pl.ds(c * size, size)
        return pltpu.make_async_copy(states_ref.at[place, part], state.at[part], sems.at[c])

    for c in range(chunks):
        load(c).start()
    for n, copy in enumerate(copies):
        copy.wait()
        wide[...] = rows_ref[n].astype(F32)
        early_ref[n] = silu(extract(wide, place, count))
    for c in range(chunks):
        load(c).wait()
        for h in range(c * size, (c + 1) * size):
            weight_ref[h] = jnp.concatenate(split(state[h]), axis=0)


def route_kernel(*refs, inner, outer):
    wishes, column = refs[:inner], refs[inner:inner + outer]
    outs = refs[inner + outer:]
    my_outer = lax.div(lax.axis_index("req"), inner)
    for k in range(inner):
        wish = fact(wishes[inverse_step(k, inner)], OUTER, outs[k].shape[0])
        outs[k][...] = choose(column, wish, my_outer, outer)


def answer_kernel(facts_ref, *refs, inner, late, heads, width):
    found, (weight_ref, early_ref, out_ref, lhs, prod) = refs[:inner], refs[inner:]
    my_inner = lax.rem(lax.axis_index("req"), inner)
    block = lambda ref, t: ref[t * heads:(t + 1) * heads, :]
    rows = choose(found, fact(facts_ref, INNER, late * heads), my_inner, inner)
    q = [rows[t * heads:(t + 1) * heads, :] for t in range(late)]
    slope = head_slope(heads, width)
    for t in range(late):
        x = q[t] * decay_power(slope, t + BEFORE + 1)
        high = x.astype(BF16).astype(F32)
        lhs[t * heads:(t + 1) * heads, :] = high
        lhs[(late + t) * heads:(late + t + 1) * heads, :] = x - high
    for h in range(heads):
        x = lhs[pl.ds(h, 2 * late, stride=heads), :].astype(BF16)
        prod[pl.ds(h, 2 * late, stride=heads), :] = jnp.dot(
            jnp.concatenate([x, x], axis=1), weight_ref[h], preferred_element_type=F32)
    for t in range(late):
        total = block(prod, t) + block(prod, late + t)
        for s in range(BEFORE):
            score = jnp.sum(q[t] * block(early_ref.at[0], s), axis=1, keepdims=True)
            total = total + score * decay_power(slope, t + BEFORE - s) * block(
                early_ref.at[1], s)
        out_ref[t * heads:(t + 1) * heads, :] = total


def reply_kernel(*refs, inner, outer):
    wishes, replies = refs[:inner], refs[inner:2 * inner]
    outs = refs[2 * inner:]
    me = lax.axis_index("req")
    my_inner, my_outer = lax.rem(me, inner), lax.div(me, inner)
    rows = outs[0].shape[0]
    owner = [
        jnp.where(fact(wish, INNER, rows) == my_inner, fact(wish, OUTER, rows), -1)
        for wish in wishes]
    for k in range(outer):
        result = 0.0
        for n in range(inner):
            result = jnp.where(owner[n] == turn(my_outer, k, outer), replies[n][...], result)
        outs[k][...] = result


def local_kernel(facts_ref, queries_ref, keys_ref, values_ref, gates_ref, gain_ref, own_ref,
                 states_ref, out_ref, last_ref, late_ref, state, lhs, prod, wide, sems, *, count, chunks):
    heads, width = states_ref.shape[1], states_ref.shape[2]
    span = heads * count
    steps = queries_ref.shape[0] // span
    late = steps - BEFORE
    size = heads // chunks
    place = fact(facts_ref, SLOT, late * heads)

    def load(j, c):
        part = pl.ds(c * size, size)
        return pltpu.make_async_copy(states_ref.at[j, part], state.at[j, part], sems.at[j, c])

    for j in range(count):
        for c in range(chunks):
            load(j, c).start()

    def spread(x):
        for s in range(count):
            wide[pl.ds(s, heads, stride=count), :] = x
        return wide[:span, :]

    slope = spread(head_slope(heads, width))
    gain = spread(gain_ref[...])
    decay = [decay_power(slope, p) for p in range(steps + 1)]
    block = lambda ref, t: ref[t * span:(t + 1) * span, :]
    q = [silu(block(queries_ref, t).astype(F32)) for t in range(steps)]
    k = [silu(block(keys_ref, t).astype(F32)) for t in range(steps)]
    v = [silu(block(values_ref, t).astype(F32)) for t in range(steps)]
    for t in range(steps):
        x = q[t] * decay[t + 1]
        high = x.astype(BF16).astype(F32)
        lhs[t * span:(t + 1) * span, :] = high
        lhs[(8 + t) * span:(9 + t) * span, :] = x - high
    mixed = []
    for t in range(steps):
        total = None
        far = None
        for s in range(t + 1):
            score = jnp.sum(q[t] * k[s], axis=1, keepdims=True)
            term = score * decay[t - s] * v[s]
            if t >= BEFORE and s < BEFORE:
                far = term if far is None else far + term
            else:
                total = term if total is None else total + term
        if t >= BEFORE:
            wide[(t - BEFORE) * span:(t - BEFORE + 1) * span, :] = total
        mixed.append(total if far is None else total + far)
    late_ref[0] = extract(wide, place, count) + own_ref[...]
    scale = [gain * sigmoid(block(gates_ref, t).astype(F32)) for t in range(steps)]
    for t in range(late):
        wide[t * span:(t + 1) * span, :] = scale[BEFORE + t]
    late_ref[1] = extract(wide, place, count)
    for j in range(count):
        for c in range(chunks):
            load(j, c).wait()
            for h in range(c * size, (c + 1) * size):
                rows = pl.ds(h * count + j, 16, stride=span)
                x = lhs[rows, :].astype(BF16)
                prod[rows, :] = jnp.dot(
                    jnp.concatenate([x, x], axis=1),
                    jnp.concatenate(split(state[j, h]), axis=0),
                    preferred_element_type=F32)
    slot = lax.rem(lax.broadcasted_iota(jnp.int32, (span, 1), 0), jnp.int32(count))
    for t in range(steps):
        x = mixed[t] + block(prod, t) + block(prod, 8 + t)
        sums = jnp.sum(x * x, axis=1, keepdims=True)
        energy = jnp.zeros((span, 1), F32)
        for s in range(count):
            whole = jnp.sum(jnp.where(slot == s, sums, 0.0), axis=0, keepdims=True)
            energy = jnp.where(slot == s, whole, energy)
        factor = lax.rsqrt(energy * (1.0 / (heads * width)) + EPS)
        y = (x * factor * scale[t]).astype(BF16)
        out_ref[t * span:(t + 1) * span, :] = y
        if t >= BEFORE:
            last_ref[(t - BEFORE) * span:(t - BEFORE + 1) * span, :] = y


def finish_kernel(facts_ref, base_ref, last_ref, late_ref, *refs, count, heads):
    parts, (out_ref, rows_ref, wide, sem) = refs[:-4], refs[-4:]
    wide[...] = last_ref[...].astype(F32)
    place = fact(facts_ref, SLOT, heads)
    for t in range(late_ref.shape[1] // heads):
        part = slice(t * heads, (t + 1) * heads)
        x = late_ref[0, part, :]
        for ref in parts:
            x = x + ref[part, :]
        y = x * lax.rsqrt(jnp.mean(x * x) + EPS) * late_ref[1, part, :]
        for s in range(count):
            here = pl.ds(t * heads * count + s, heads, stride=count)
            wide[here, :] = jnp.where(place == s, y, wide[here, :])
    rows_ref[...] = wide[...].astype(BF16)
    rows = rows_ref.shape[0]
    copy = pltpu.make_async_copy(
        rows_ref, out_ref.at[pl.ds(out_ref.shape[0] - rows, rows)], sem)
    copy.start()
    copy.wait()


def in_hbm(x):
    return pltpu.with_memory_space_constraint(x, pltpu.HBM)


def near_square(total):
    return next(
        (d, total // d) for d in range(1, total + 1) if total % d == 0 and d * d >= total)


def on_device(queries, keys, values, gates, states, new_slot, norm_gain):
    count, steps, features = queries.shape
    heads, width = states.shape[1], states.shape[2]
    late = steps - BEFORE
    packed_rows, single_rows = steps * heads * count, late * heads
    inner, outer = near_square(lax.axis_size("req"))

    def pack(x):
        return x.reshape(count, steps, heads, width).transpose(1, 2, 0, 3).reshape(
            packed_rows, width)

    def unpack(x):
        return x.reshape(steps, heads, count, width).transpose(2, 0, 1, 3).reshape(
            count, steps, features)

    def send_inner(x, k):
        return lax.ppermute(x, "req", [
            (o * inner + i, o * inner + int(turn(i, k, inner)))
            for o in range(outer) for i in range(inner)])

    def send_outer(x, k):
        return lax.ppermute(x, "req", [
            (o * inner + i, int(turn(o, k, outer)) * inner + i)
            for o in range(outer) for i in range(inner)])

    def params(limit):
        return pltpu.CompilerParams(vmem_limit_bytes=limit * MIB)

    queries, keys, values, gates = pack(queries), pack(keys), pack(values), pack(gates)
    single = jax.ShapeDtypeStruct((single_rows, width), F32)
    late_packed = pltpu.VMEM((late * heads * count, width), F32)

    late_rows = jax.ShapeDtypeStruct((late * heads * count, width), BF16)
    late_bf16 = pltpu.VMEM(late_rows.shape, BF16)

    ask, facts = pl.pallas_call(
        functools.partial(ask_kernel, count=count, inner=inner),
        out_shape=(single, jax.ShapeDtypeStruct((8, width), jnp.int32)),
        in_specs=[SMEM, HBM], out_specs=(VMEM, VMEM),
        scratch_shapes=[late_bf16, late_packed, pltpu.SemaphoreType.DMA],
        compiler_params=params(4), name="ask",
    )(in_hbm(new_slot), in_hbm(queries))

    column = [ask] + [send_outer(ask, k) for k in range(1, outer)]
    wishes = [facts] + [send_inner(facts, k) for k in range(1, inner)]

    chunks = 8
    weight, early = pl.pallas_call(
        functools.partial(prepare_kernel, count=count, chunks=chunks),
        out_shape=(jax.ShapeDtypeStruct((heads, 2 * width, width), BF16),
                   jax.ShapeDtypeStruct((2, BEFORE * heads, width), F32)),
        in_specs=[SMEM, HBM, HBM, HBM], out_specs=(VMEM, VMEM),
        scratch_shapes=[pltpu.VMEM((heads, width, width), F32),
                        pltpu.VMEM((2, BEFORE * heads * count, width), BF16),
                        pltpu.VMEM((BEFORE * heads * count, width), F32),
                        pltpu.SemaphoreType.DMA((chunks,)),
                        pltpu.SemaphoreType.DMA((2,))],
        compiler_params=params(12), name="prepare",
    )(in_hbm(new_slot), in_hbm(keys), in_hbm(values), in_hbm(states))

    asked = pl.pallas_call(
        functools.partial(route_kernel, inner=inner, outer=outer),
        out_shape=(single,) * inner,
        in_specs=[VMEM] * (inner + outer), out_specs=(VMEM,) * inner,
        compiler_params=params(4), name="route",
    )(*wishes, *column)
    found = [asked[0]] + [send_inner(asked[k], k) for k in range(1, inner)]

    answer = pl.pallas_call(
        functools.partial(answer_kernel, inner=inner, late=late, heads=heads, width=width),
        out_shape=single, in_specs=[VMEM] * (inner + 3), out_specs=VMEM,
        scratch_shapes=[pltpu.VMEM((2 * late * heads, width), F32)] * 2,
        compiler_params=params(8), name="answer",
    )(facts, *found, weight, early)
    replies = [answer] + [send_inner(answer, k) for k in range(1, inner)]

    sorted_replies = pl.pallas_call(
        functools.partial(reply_kernel, inner=inner, outer=outer),
        out_shape=(single,) * outer,
        in_specs=[VMEM] * (2 * inner), out_specs=(VMEM,) * outer,
        compiler_params=params(4), name="reply",
    )(*wishes, *replies)
    parts = [send_outer(sorted_replies[k], k) for k in range(1, outer)]

    chunks = 4
    output = jax.ShapeDtypeStruct((packed_rows, width), BF16)
    base, last, partial = pl.pallas_call(
        functools.partial(local_kernel, count=count, chunks=chunks),
        out_shape=(pltpu.HBM(output.shape, output.dtype), late_rows, jax.ShapeDtypeStruct((2, single_rows, width), F32)),
        in_specs=[VMEM] * 7 + [HBM], out_specs=(VMEM, VMEM, VMEM),
        scratch_shapes=[
            pltpu.VMEM((count, heads, width, width), F32),
            pltpu.VMEM((16 * heads * count, width), F32),
            pltpu.VMEM((16 * heads * count, width), F32),
            late_packed,
            pltpu.SemaphoreType.DMA((count, chunks)),
        ],
        compiler_params=params(16), name="local",
    )(facts, queries, keys, values, gates, norm_gain.reshape(heads, width),
      sorted_replies[0], in_hbm(states))

    return unpack(pl.pallas_call(
        functools.partial(finish_kernel, count=count, heads=heads),
        out_shape=output, in_specs=[VMEM, HBM] + [VMEM] * (outer + 1), out_specs=HBM,
        scratch_shapes=[late_bf16, late_packed, pltpu.SemaphoreType.DMA],
        input_output_aliases={1: 0},
        compiler_params=params(4), name="finish",
    )(facts, in_hbm(base), last, partial, *parts))


def solution(mesh):
    rows = P(("groups", "req"), None, None)
    in_specs = (rows, rows, rows, rows, P(("groups", "req"), None, None, None),
                P(("groups", "req")), P())
    return jax.shard_map(
        on_device, mesh=mesh, in_specs=in_specs, out_specs=rows, check_vma=False)
```

```python
import functools

import jax
import jax.numpy as jnp
from jax import lax
from jax.experimental import pallas as pl
from jax.experimental.pallas import tpu as pltpu
from jax.sharding import PartitionSpec as P

BEFORE = 3
EPS = 1e-06
F32 = jnp.float32
BF16 = jnp.bfloat16
MIB = 2**20
VMEM = pl.BlockSpec(memory_space=pltpu.VMEM)
SMEM = pl.BlockSpec(memory_space=pltpu.SMEM)
HBM = pl.BlockSpec(memory_space=pltpu.HBM)


def silu(x):
    return x / (1.0 + jnp.exp(-x))


def sigmoid(x):
    return 1.0 / (1.0 + jnp.exp(-x))


def moving_slot(slots_ref, count):
    base = lax.axis_index("req") * count
    place = jnp.int32(0)
    moves = slots_ref[0] != base
    for s in range(1, count):
        here = slots_ref[s] != base + s
        place = jnp.where(here, s, place)
        moves = jnp.logical_or(moves, here)
    return place, moves


def wanted_device(slots_ref, count):
    device = lax.axis_index("req")
    result = device
    for s in range(count):
        owner = lax.div(slots_ref[s], jnp.int32(count))
        result = jnp.where(owner != device, owner, result)
    return result


OUTER, INNER, SLOT, FACTS = 0, 1, 2, 8


def fact(ref, step, kind, rows):
    row = step * FACTS + kind
    return jnp.broadcast_to(ref[row:row + 1, :], (rows, ref.shape[1]))


def head_slope(heads, width):
    order = lax.broadcasted_iota(jnp.int32, (heads, width), 0).astype(F32)
    return jnp.exp2(-8.0 * (order + 1.0) / (2.0 * heads))


def decay_power(slope, power):
    return jnp.exp(slope * (-float(power)))


def split(x):
    high = x.astype(BF16)
    return high, (x - high.astype(F32)).astype(BF16)


def extract(packed, place, count):
    rows = packed.shape[0] // count
    result = packed[pl.ds(0, rows, stride=count), :]
    for s in range(1, count):
        result = jnp.where(place == s, packed[pl.ds(s, rows, stride=count), :], result)
    return result


def turn(position, step, size):
    return position ^ step if size & (size - 1) == 0 else (position + step) % size


def unturn(position, step, size):
    return position ^ step if size & (size - 1) == 0 else (position - step) % size


def inverse_step(step, size):
    return step if size & (size - 1) == 0 else (size - step) % size


def choose(options, index, mine, size):
    result = options[0][...]
    for k in range(1, size):
        result = jnp.where(unturn(mine, k, size) == index, options[k][...], result)
    return result


def ask_kernel(new_slot_ref, queries_ref, out_ref, facts_ref, slots_ref, rows_ref, wide, sems, *,
               count, inner):
    late = rows_ref.shape[0]
    first = queries_ref.shape[0] - late
    slots_copy = pltpu.make_async_copy(new_slot_ref, slots_ref, sems.at[0])
    slots_copy.start()
    copy = pltpu.make_async_copy(queries_ref.at[pl.ds(first, late)], rows_ref, sems.at[1])
    copy.start()
    slots_copy.wait()
    place, moves = moving_slot(slots_ref, count)
    wanted = wanted_device(slots_ref, count)
    kind = lax.broadcasted_iota(jnp.int32, facts_ref.shape, 0)
    facts = jnp.where(kind == INNER, lax.rem(wanted, inner), jnp.where(moves, place, count))
    facts_ref[...] = jnp.where(kind == OUTER, lax.div(wanted, inner), facts)
    copy.wait()
    wide[...] = rows_ref[...].astype(F32)
    out_ref[...] = silu(extract(wide, place, count))


def prepare_kernel(slots_ref, keys_ref, values_ref, states_ref, weight_ref, early_ref,
                   state, rows_ref, wide, sems, row_sems, *, count, chunks):
    heads = states_ref.shape[1]
    size = heads // chunks
    place, _ = moving_slot(slots_ref, count)
    copies = [
        pltpu.make_async_copy(
            ref.at[pl.ds(0, wide.shape[0])], rows_ref.at[n], row_sems.at[n])
        for n, ref in enumerate((keys_ref, values_ref))]
    for copy in copies:
        copy.start()

    def load(c):
        part = pl.ds(c * size, size)
        return pltpu.make_async_copy(states_ref.at[place, part], state.at[part], sems.at[c])

    for c in range(chunks):
        load(c).start()
    for n, copy in enumerate(copies):
        copy.wait()
        wide[...] = rows_ref[n].astype(F32)
        early_ref[n] = silu(extract(wide, place, count))
    for c in range(chunks):
        load(c).wait()
        for h in range(c * size, (c + 1) * size):
            weight_ref[h] = jnp.concatenate(split(state[h]), axis=0)


def route_kernel(wishes_ref, *refs, inner, outer):
    column, outs = refs[:outer], refs[outer:]
    my_outer = lax.div(lax.axis_index("req"), inner)
    for k in range(inner):
        wish = fact(wishes_ref, inverse_step(k, inner), OUTER, outs[k].shape[0])
        outs[k][...] = choose(column, wish, my_outer, outer)


def answer_kernel(facts_ref, *refs, inner, late, heads, width):
    found, (weight_ref, early_ref, out_ref, lhs, prod) = refs[:inner], refs[inner:]
    my_inner = lax.rem(lax.axis_index("req"), inner)
    block = lambda ref, t: ref[t * heads:(t + 1) * heads, :]
    rows = choose(found, fact(facts_ref, 0, INNER, late * heads), my_inner, inner)
    q = [rows[t * heads:(t + 1) * heads, :] for t in range(late)]
    slope = head_slope(heads, width)
    for t in range(late):
        x = q[t] * decay_power(slope, t + BEFORE + 1)
        high = x.astype(BF16).astype(F32)
        lhs[t * heads:(t + 1) * heads, :] = high
        lhs[(late + t) * heads:(late + t + 1) * heads, :] = x - high
    for h in range(heads):
        x = lhs[pl.ds(h, 2 * late, stride=heads), :].astype(BF16)
        prod[pl.ds(h, 2 * late, stride=heads), :] = jnp.dot(
            jnp.concatenate([x, x], axis=1), weight_ref[h], preferred_element_type=F32)
    for t in range(late):
        total = block(prod, t) + block(prod, late + t)
        for s in range(BEFORE):
            score = jnp.sum(q[t] * block(early_ref.at[0], s), axis=1, keepdims=True)
            total = total + score * decay_power(slope, t + BEFORE - s) * block(
                early_ref.at[1], s)
        out_ref[t * heads:(t + 1) * heads, :] = total


def reply_kernel(wishes_ref, *refs, inner, outer):
    replies, outs = refs[:inner], refs[inner:]
    me = lax.axis_index("req")
    my_inner, my_outer = lax.rem(me, inner), lax.div(me, inner)
    rows = outs[0].shape[0]
    owner = [
        jnp.where(fact(wishes_ref, k, INNER, rows) == my_inner,
                  fact(wishes_ref, k, OUTER, rows), -1)
        for k in range(inner)]
    for k in range(outer):
        result = 0.0
        for n in range(inner):
            result = jnp.where(owner[n] == turn(my_outer, k, outer), replies[n][...], result)
        outs[k][...] = result


def local_kernel(facts_ref, queries_ref, keys_ref, values_ref, gates_ref, gain_ref, own_ref,
                 states_ref, out_ref, last_ref, late_ref, state, lhs, prod, wide, sems, *, count, chunks):
    heads, width = states_ref.shape[1], states_ref.shape[2]
    span = heads * count
    steps = queries_ref.shape[0] // span
    late = steps - BEFORE
    size = heads // chunks
    place = fact(facts_ref, 0, SLOT, late * heads)

    def load(j, c):
        part = pl.ds(c * size, size)
        return pltpu.make_async_copy(states_ref.at[j, part], state.at[j, part], sems.at[j, c])

    for j in range(count):
        for c in range(chunks):
            load(j, c).start()

    def spread(x):
        for s in range(count):
            wide[pl.ds(s, heads, stride=count), :] = x
        return wide[:span, :]

    slope = spread(head_slope(heads, width))
    gain = spread(gain_ref[...])
    decay = [decay_power(slope, p) for p in range(steps + 1)]
    block = lambda ref, t: ref[t * span:(t + 1) * span, :]
    q = [silu(block(queries_ref, t).astype(F32)) for t in range(steps)]
    k = [silu(block(keys_ref, t).astype(F32)) for t in range(steps)]
    v = [silu(block(values_ref, t).astype(F32)) for t in range(steps)]
    for t in range(steps):
        x = q[t] * decay[t + 1]
        high = x.astype(BF16).astype(F32)
        lhs[t * span:(t + 1) * span, :] = high
        lhs[(8 + t) * span:(9 + t) * span, :] = x - high
    mixed = []
    for t in range(steps):
        total = None
        far = None
        for s in range(t + 1):
            score = jnp.sum(q[t] * k[s], axis=1, keepdims=True)
            term = score * decay[t - s] * v[s]
            if t >= BEFORE and s < BEFORE:
                far = term if far is None else far + term
            else:
                total = term if total is None else total + term
        if t >= BEFORE:
            wide[(t - BEFORE) * span:(t - BEFORE + 1) * span, :] = total
        mixed.append(total if far is None else total + far)
    late_ref[0] = extract(wide, place, count) + own_ref[...]
    scale = [gain * sigmoid(block(gates_ref, t).astype(F32)) for t in range(steps)]
    for t in range(late):
        wide[t * span:(t + 1) * span, :] = scale[BEFORE + t]
    late_ref[1] = extract(wide, place, count)
    for j in range(count):
        for c in range(chunks):
            load(j, c).wait()
            for h in range(c * size, (c + 1) * size):
                rows = pl.ds(h * count + j, 16, stride=span)
                x = lhs[rows, :].astype(BF16)
                prod[rows, :] = jnp.dot(
                    jnp.concatenate([x, x], axis=1),
                    jnp.concatenate(split(state[j, h]), axis=0),
                    preferred_element_type=F32)
    slot = lax.rem(lax.broadcasted_iota(jnp.int32, (span, 1), 0), jnp.int32(count))
    for t in range(steps):
        x = mixed[t] + block(prod, t) + block(prod, 8 + t)
        sums = jnp.sum(x * x, axis=1, keepdims=True)
        energy = jnp.zeros((span, 1), F32)
        for s in range(count):
            whole = jnp.sum(jnp.where(slot == s, sums, 0.0), axis=0, keepdims=True)
            energy = jnp.where(slot == s, whole, energy)
        factor = lax.rsqrt(energy * (1.0 / (heads * width)) + EPS)
        y = (x * factor * scale[t]).astype(BF16)
        out_ref[t * span:(t + 1) * span, :] = y
        if t >= BEFORE:
            last_ref[(t - BEFORE) * span:(t - BEFORE + 1) * span, :] = y


def finish_kernel(facts_ref, base_ref, last_ref, late_ref, *refs, count, heads):
    parts, (out_ref, rows_ref, wide, sem) = refs[:-4], refs[-4:]
    wide[...] = last_ref[...].astype(F32)
    place = fact(facts_ref, 0, SLOT, heads)
    for t in range(late_ref.shape[1] // heads):
        part = slice(t * heads, (t + 1) * heads)
        x = late_ref[0, part, :]
        for ref in parts:
            x = x + ref[part, :]
        y = x * lax.rsqrt(jnp.mean(x * x) + EPS) * late_ref[1, part, :]
        for s in range(count):
            here = pl.ds(t * heads * count + s, heads, stride=count)
            wide[here, :] = jnp.where(place == s, y, wide[here, :])
    rows_ref[...] = wide[...].astype(BF16)
    rows = rows_ref.shape[0]
    copy = pltpu.make_async_copy(
        rows_ref, out_ref.at[pl.ds(out_ref.shape[0] - rows, rows)], sem)
    copy.start()
    copy.wait()


def in_hbm(x):
    return pltpu.with_memory_space_constraint(x, pltpu.HBM)


def near_square(total):
    return next(
        (d, total // d) for d in range(1, total + 1) if total % d == 0 and d * d >= total)


def on_device(queries, keys, values, gates, states, new_slot, norm_gain):
    count, steps, features = queries.shape
    heads, width = states.shape[1], states.shape[2]
    late = steps - BEFORE
    packed_rows, single_rows = steps * heads * count, late * heads
    inner, outer = near_square(lax.axis_size("req"))

    def pack(x):
        return x.reshape(count, steps, heads, width).transpose(1, 2, 0, 3).reshape(
            packed_rows, width)

    def unpack(x):
        return x.reshape(steps, heads, count, width).transpose(2, 0, 1, 3).reshape(
            count, steps, features)

    def send_inner(x, k):
        return lax.ppermute(x, "req", [
            (o * inner + i, o * inner + int(turn(i, k, inner)))
            for o in range(outer) for i in range(inner)])

    def send_outer(x, k):
        return lax.ppermute(x, "req", [
            (o * inner + i, int(turn(o, k, outer)) * inner + i)
            for o in range(outer) for i in range(inner)])

    def gather_inner(x):
        if inner & (inner - 1):
            return jnp.concatenate([x] + [send_inner(x, k) for k in range(1, inner)])
        step = 1
        while step < inner:
            x = jnp.concatenate([x, send_inner(x, step)])
            step *= 2
        return x

    def params(limit):
        return pltpu.CompilerParams(vmem_limit_bytes=limit * MIB)

    queries, keys, values, gates = pack(queries), pack(keys), pack(values), pack(gates)
    single = jax.ShapeDtypeStruct((single_rows, width), F32)
    late_packed = pltpu.VMEM((late * heads * count, width), F32)

    late_rows = jax.ShapeDtypeStruct((late * heads * count, width), BF16)
    late_bf16 = pltpu.VMEM(late_rows.shape, BF16)

    ask, facts = pl.pallas_call(
        functools.partial(ask_kernel, count=count, inner=inner),
        out_shape=(single, jax.ShapeDtypeStruct((FACTS, width), jnp.int32)),
        in_specs=[HBM, HBM], out_specs=(VMEM, VMEM),
        scratch_shapes=[pltpu.SMEM((count,), jnp.int32), late_bf16, late_packed,
                        pltpu.SemaphoreType.DMA((2,))],
        compiler_params=params(4), name="ask",
    )(in_hbm(new_slot), in_hbm(queries))

    column = [ask] + [send_outer(ask, k) for k in range(1, outer)]
    wishes = gather_inner(facts)

    chunks = 8
    weight, early = pl.pallas_call(
        functools.partial(prepare_kernel, count=count, chunks=chunks),
        out_shape=(jax.ShapeDtypeStruct((heads, 2 * width, width), BF16),
                   jax.ShapeDtypeStruct((2, BEFORE * heads, width), F32)),
        in_specs=[SMEM, HBM, HBM, HBM], out_specs=(VMEM, VMEM),
        scratch_shapes=[pltpu.VMEM((heads, width, width), F32),
                        pltpu.VMEM((2, BEFORE * heads * count, width), BF16),
                        pltpu.VMEM((BEFORE * heads * count, width), F32),
                        pltpu.SemaphoreType.DMA((chunks,)),
                        pltpu.SemaphoreType.DMA((2,))],
        compiler_params=params(12), name="prepare",
    )(in_hbm(new_slot), in_hbm(keys), in_hbm(values), in_hbm(states))

    asked = pl.pallas_call(
        functools.partial(route_kernel, inner=inner, outer=outer),
        out_shape=(single,) * inner,
        in_specs=[VMEM] * (1 + outer), out_specs=(VMEM,) * inner,
        compiler_params=params(4), name="route",
    )(wishes, *column)
    found = [asked[0]] + [send_inner(asked[k], k) for k in range(inner - 1, 0, -1)][::-1]

    answer = pl.pallas_call(
        functools.partial(answer_kernel, inner=inner, late=late, heads=heads, width=width),
        out_shape=single, in_specs=[VMEM] * (inner + 3), out_specs=VMEM,
        scratch_shapes=[pltpu.VMEM((2 * late * heads, width), F32)] * 2,
        compiler_params=params(8), name="answer",
    )(facts, *found, weight, early)
    replies = [answer] + [send_inner(answer, k) for k in range(1, inner)]

    sorted_replies = pl.pallas_call(
        functools.partial(reply_kernel, inner=inner, outer=outer),
        out_shape=(single,) * outer,
        in_specs=[VMEM] * (1 + inner), out_specs=(VMEM,) * outer,
        compiler_params=params(4), name="reply",
    )(wishes, *replies)
    parts = [send_outer(sorted_replies[k], k) for k in range(outer - 1, 0, -1)]

    chunks = 4
    output = jax.ShapeDtypeStruct((packed_rows, width), BF16)
    base, last, partial = pl.pallas_call(
        functools.partial(local_kernel, count=count, chunks=chunks),
        out_shape=(pltpu.HBM(output.shape, output.dtype), late_rows, jax.ShapeDtypeStruct((2, single_rows, width), F32)),
        in_specs=[VMEM] * 7 + [HBM], out_specs=(VMEM, VMEM, VMEM),
        scratch_shapes=[
            pltpu.VMEM((count, heads, width, width), F32),
            pltpu.VMEM((16 * heads * count, width), F32),
            pltpu.VMEM((16 * heads * count, width), F32),
            late_packed,
            pltpu.SemaphoreType.DMA((count, chunks)),
        ],
        compiler_params=params(16), name="local",
    )(facts, queries, keys, values, gates, norm_gain.reshape(heads, width),
      sorted_replies[0], in_hbm(states))

    return unpack(pl.pallas_call(
        functools.partial(finish_kernel, count=count, heads=heads),
        out_shape=output, in_specs=[VMEM, HBM] + [VMEM] * (outer + 1), out_specs=HBM,
        scratch_shapes=[late_bf16, late_packed, pltpu.SemaphoreType.DMA],
        input_output_aliases={1: 0},
        compiler_params=params(4), name="finish",
    )(facts, in_hbm(base), last, partial, *parts))


def solution(mesh):
    rows = P(("groups", "req"), None, None)
    in_specs = (rows, rows, rows, rows, P(("groups", "req"), None, None, None),
                P(("groups", "req")), P())
    return jax.shard_map(
        on_device, mesh=mesh, in_specs=in_specs, out_specs=rows, check_vma=False)
```

```python
import functools

import jax
import jax.numpy as jnp
from jax import lax
from jax.experimental import pallas as pl
from jax.experimental.pallas import tpu as pltpu
from jax.sharding import PartitionSpec as P

BEFORE = 3
EPS = 1e-06
F32 = jnp.float32
BF16 = jnp.bfloat16
MIB = 2**20
VMEM = pl.BlockSpec(memory_space=pltpu.VMEM)
SMEM = pl.BlockSpec(memory_space=pltpu.SMEM)
HBM = pl.BlockSpec(memory_space=pltpu.HBM)


def silu(x):
    return x / (1.0 + jnp.exp(-x))


def sigmoid(x):
    return 1.0 / (1.0 + jnp.exp(-x))


def moving_slot(slots_ref, count):
    base = lax.axis_index("req") * count
    place = jnp.int32(0)
    moves = slots_ref[0] != base
    for s in range(1, count):
        here = slots_ref[s] != base + s
        place = jnp.where(here, s, place)
        moves = jnp.logical_or(moves, here)
    return place, moves


def wanted_device(slots_ref, count):
    device = lax.axis_index("req")
    result = device
    for s in range(count):
        owner = lax.div(slots_ref[s], jnp.int32(count))
        result = jnp.where(owner != device, owner, result)
    return result


OUTER, INNER, SLOT, FACTS = 0, 1, 2, 8


def wish_steps(inner):
    if inner & (inner - 1):
        return list(range(inner))
    steps, step = [0], inner // 2
    while step:
        steps, step = steps + [s ^ step for s in steps], step // 2
    return steps


def fact(ref, place, kind, rows):
    row = place * FACTS + kind
    return jnp.broadcast_to(ref[row:row + 1, :], (rows, ref.shape[1]))


def head_slope(heads, width):
    order = lax.broadcasted_iota(jnp.int32, (heads, width), 0).astype(F32)
    return jnp.exp2(-8.0 * (order + 1.0) / (2.0 * heads))


def decay_power(slope, power):
    return jnp.exp(slope * (-float(power)))


def split(x):
    high = x.astype(BF16)
    return high, (x - high.astype(F32)).astype(BF16)


def extract(packed, place, count):
    rows = packed.shape[0] // count
    result = packed[pl.ds(0, rows, stride=count), :]
    for s in range(1, count):
        result = jnp.where(place == s, packed[pl.ds(s, rows, stride=count), :], result)
    return result


def turn(position, step, size):
    return position ^ step if size & (size - 1) == 0 else (position + step) % size


def unturn(position, step, size):
    return position ^ step if size & (size - 1) == 0 else (position - step) % size


def inverse_step(step, size):
    return step if size & (size - 1) == 0 else (size - step) % size


def choose(options, index, mine, size):
    result = options[0][...]
    for k in range(1, size):
        result = jnp.where(unturn(mine, k, size) == index, options[k][...], result)
    return result


def ask_kernel(new_slot_ref, queries_ref, out_ref, facts_ref, slots_ref, rows_ref, wide, sems, *,
               count, inner):
    late = rows_ref.shape[0]
    first = queries_ref.shape[0] - late
    slots_copy = pltpu.make_async_copy(new_slot_ref, slots_ref, sems.at[0])
    slots_copy.start()
    copy = pltpu.make_async_copy(queries_ref.at[pl.ds(first, late)], rows_ref, sems.at[1])
    copy.start()
    slots_copy.wait()
    place, moves = moving_slot(slots_ref, count)
    wanted = wanted_device(slots_ref, count)
    kind = lax.broadcasted_iota(jnp.int32, facts_ref.shape, 0)
    facts = jnp.where(kind == INNER, lax.rem(wanted, inner), jnp.where(moves, place, count))
    facts_ref[...] = jnp.where(kind == OUTER, lax.div(wanted, inner), facts)
    copy.wait()
    wide[...] = rows_ref[...].astype(F32)
    out_ref[...] = silu(extract(wide, place, count))


def prepare_kernel(slots_ref, keys_ref, values_ref, states_ref, weight_ref, early_ref,
                   state, rows_ref, wide, sems, row_sems, *, count, chunks):
    heads = states_ref.shape[1]
    size = heads // chunks
    place, _ = moving_slot(slots_ref, count)
    copies = [
        pltpu.make_async_copy(
            ref.at[pl.ds(0, wide.shape[0])], rows_ref.at[n], row_sems.at[n])
        for n, ref in enumerate((keys_ref, values_ref))]
    for copy in copies:
        copy.start()

    def load(c):
        part = pl.ds(c * size, size)
        return pltpu.make_async_copy(states_ref.at[place, part], state.at[part], sems.at[c])

    for c in range(chunks):
        load(c).start()
    for n, copy in enumerate(copies):
        copy.wait()
        wide[...] = rows_ref[n].astype(F32)
        early_ref[n] = silu(extract(wide, place, count))
    for c in range(chunks):
        load(c).wait()
        for h in range(c * size, (c + 1) * size):
            weight_ref[h] = jnp.concatenate(split(state[h]), axis=0)


def route_kernel(wishes_ref, *refs, inner, outer):
    column, outs = refs[:outer], refs[outer:]
    my_outer = lax.div(lax.axis_index("req"), inner)
    for k in range(inner):
        back = wish_steps(inner).index(inverse_step(k, inner))
        wish = fact(wishes_ref, back, OUTER, outs[k].shape[0])
        outs[k][...] = choose(column, wish, my_outer, outer)


def answer_kernel(facts_ref, *refs, inner, late, heads, width):
    found, (weight_ref, early_ref, out_ref, lhs, prod) = refs[:inner][::-1], refs[inner:]
    my_inner = lax.rem(lax.axis_index("req"), inner)
    block = lambda ref, t: ref[t * heads:(t + 1) * heads, :]
    rows = choose(found, fact(facts_ref, 0, INNER, late * heads), my_inner, inner)
    q = [rows[t * heads:(t + 1) * heads, :] for t in range(late)]
    slope = head_slope(heads, width)
    for t in range(late):
        x = q[t] * decay_power(slope, t + BEFORE + 1)
        high = x.astype(BF16).astype(F32)
        lhs[t * heads:(t + 1) * heads, :] = high
        lhs[(late + t) * heads:(late + t + 1) * heads, :] = x - high
    for h in range(heads):
        x = lhs[pl.ds(h, 2 * late, stride=heads), :].astype(BF16)
        prod[pl.ds(h, 2 * late, stride=heads), :] = jnp.dot(
            jnp.concatenate([x, x], axis=1), weight_ref[h], preferred_element_type=F32)
    for t in range(late):
        total = block(prod, t) + block(prod, late + t)
        for s in range(BEFORE):
            score = jnp.sum(q[t] * block(early_ref.at[0], s), axis=1, keepdims=True)
            total = total + score * decay_power(slope, t + BEFORE - s) * block(
                early_ref.at[1], s)
        out_ref[t * heads:(t + 1) * heads, :] = total


def reply_kernel(wishes_ref, *refs, inner, outer):
    replies, outs = refs[:inner], refs[inner:]
    me = lax.axis_index("req")
    my_inner, my_outer = lax.rem(me, inner), lax.div(me, inner)
    rows = outs[0].shape[0]
    owner = [
        jnp.where(fact(wishes_ref, n, INNER, rows) == my_inner,
                  fact(wishes_ref, n, OUTER, rows), -1)
        for n in map(wish_steps(inner).index, range(inner))]
    for k in range(outer):
        result = 0.0
        for n in range(inner):
            result = jnp.where(owner[n] == turn(my_outer, k, outer), replies[n][...], result)
        outs[k][...] = result


def local_kernel(facts_ref, queries_ref, keys_ref, values_ref, gates_ref, gain_ref, own_ref,
                 states_ref, out_ref, last_ref, late_ref, state, lhs, prod, wide, sems, *, count, chunks):
    heads, width = states_ref.shape[1], states_ref.shape[2]
    span = heads * count
    steps = queries_ref.shape[0] // span
    late = steps - BEFORE
    size = heads // chunks
    place = fact(facts_ref, 0, SLOT, late * heads)

    def load(j, c):
        part = pl.ds(c * size, size)
        return pltpu.make_async_copy(states_ref.at[j, part], state.at[j, part], sems.at[j, c])

    for j in range(count):
        for c in range(chunks):
            load(j, c).start()

    def spread(x):
        for s in range(count):
            wide[pl.ds(s, heads, stride=count), :] = x
        return wide[:span, :]

    slope = spread(head_slope(heads, width))
    gain = spread(gain_ref[...])
    decay = [decay_power(slope, p) for p in range(steps + 1)]
    block = lambda ref, t: ref[t * span:(t + 1) * span, :]
    q = [silu(block(queries_ref, t).astype(F32)) for t in range(steps)]
    k = [silu(block(keys_ref, t).astype(F32)) for t in range(steps)]
    v = [silu(block(values_ref, t).astype(F32)) for t in range(steps)]
    for t in range(steps):
        x = q[t] * decay[t + 1]
        high = x.astype(BF16).astype(F32)
        lhs[t * span:(t + 1) * span, :] = high
        lhs[(8 + t) * span:(9 + t) * span, :] = x - high
    mixed = []
    for t in range(steps):
        total = None
        far = None
        for s in range(t + 1):
            score = jnp.sum(q[t] * k[s], axis=1, keepdims=True)
            term = score * decay[t - s] * v[s]
            if t >= BEFORE and s < BEFORE:
                far = term if far is None else far + term
            else:
                total = term if total is None else total + term
        if t >= BEFORE:
            wide[(t - BEFORE) * span:(t - BEFORE + 1) * span, :] = total
        mixed.append(total if far is None else total + far)
    late_ref[0] = extract(wide, place, count) + own_ref[...]
    scale = [gain * sigmoid(block(gates_ref, t).astype(F32)) for t in range(steps)]
    for t in range(late):
        wide[t * span:(t + 1) * span, :] = scale[BEFORE + t]
    late_ref[1] = extract(wide, place, count)
    for j in range(count):
        for c in range(chunks):
            load(j, c).wait()
            for h in range(c * size, (c + 1) * size):
                rows = pl.ds(h * count + j, 16, stride=span)
                x = lhs[rows, :].astype(BF16)
                prod[rows, :] = jnp.dot(
                    jnp.concatenate([x, x], axis=1),
                    jnp.concatenate(split(state[j, h]), axis=0),
                    preferred_element_type=F32)
    slot = lax.rem(lax.broadcasted_iota(jnp.int32, (span, 1), 0), jnp.int32(count))
    for t in range(steps):
        x = mixed[t] + block(prod, t) + block(prod, 8 + t)
        sums = jnp.sum(x * x, axis=1, keepdims=True)
        energy = jnp.zeros((span, 1), F32)
        for s in range(count):
            whole = jnp.sum(jnp.where(slot == s, sums, 0.0), axis=0, keepdims=True)
            energy = jnp.where(slot == s, whole, energy)
        factor = lax.rsqrt(energy * (1.0 / (heads * width)) + EPS)
        y = (x * factor * scale[t]).astype(BF16)
        out_ref[t * span:(t + 1) * span, :] = y
        if t >= BEFORE:
            last_ref[(t - BEFORE) * span:(t - BEFORE + 1) * span, :] = y


def finish_kernel(facts_ref, base_ref, last_ref, late_ref, *refs, count, heads):
    parts, (out_ref, rows_ref, wide, sems) = refs[:-4], refs[-4:]
    place = fact(facts_ref, 0, SLOT, heads)
    span = heads * count
    steps = late_ref.shape[1] // heads
    first = out_ref.shape[0] - steps * span
    copies = []
    for t in range(steps):
        part = slice(t * heads, (t + 1) * heads)
        x = late_ref[0, part, :]
        for ref in parts:
            x = x + ref[part, :]
        y = x * lax.rsqrt(jnp.mean(x * x) + EPS) * late_ref[1, part, :]
        rows = slice(t * span, (t + 1) * span)
        wide[rows, :] = last_ref[rows, :].astype(F32)
        for s in range(count):
            here = pl.ds(t * span + s, heads, stride=count)
            wide[here, :] = jnp.where(place == s, y, wide[here, :])
        rows_ref[rows, :] = wide[rows, :].astype(BF16)
        copies.append(pltpu.make_async_copy(
            rows_ref.at[pl.ds(t * span, span)], out_ref.at[pl.ds(first + t * span, span)],
            sems.at[t]))
        copies[t].start()
    for copy in copies:
        copy.wait()


def in_hbm(x):
    return pltpu.with_memory_space_constraint(x, pltpu.HBM)


def near_square(total):
    return next(
        (d, total // d) for d in range(1, total + 1) if total % d == 0 and d * d >= total)


def on_device(queries, keys, values, gates, states, new_slot, norm_gain):
    count, steps, features = queries.shape
    heads, width = states.shape[1], states.shape[2]
    late = steps - BEFORE
    packed_rows, single_rows = steps * heads * count, late * heads
    inner, outer = near_square(lax.axis_size("req"))

    def pack(x):
        return x.reshape(count, steps, heads, width).transpose(1, 2, 0, 3).reshape(
            packed_rows, width)

    def unpack(x):
        return x.reshape(steps, heads, count, width).transpose(2, 0, 1, 3).reshape(
            count, steps, features)

    def send_inner(x, k):
        return lax.ppermute(x, "req", [
            (o * inner + i, o * inner + int(turn(i, k, inner)))
            for o in range(outer) for i in range(inner)])

    def send_outer(x, k):
        return lax.ppermute(x, "req", [
            (o * inner + i, int(turn(o, k, outer)) * inner + i)
            for o in range(outer) for i in range(inner)])

    def gather_inner(x):
        if inner & (inner - 1):
            return jnp.concatenate([x] + [send_inner(x, k) for k in range(1, inner)])
        step = inner // 2
        while step:
            x, step = jnp.concatenate([x, send_inner(x, step)]), step // 2
        return x

    def params(limit):
        return pltpu.CompilerParams(vmem_limit_bytes=limit * MIB)

    queries, keys, values, gates = pack(queries), pack(keys), pack(values), pack(gates)
    single = jax.ShapeDtypeStruct((single_rows, width), F32)
    late_packed = pltpu.VMEM((late * heads * count, width), F32)

    late_rows = jax.ShapeDtypeStruct((late * heads * count, width), BF16)
    late_bf16 = pltpu.VMEM(late_rows.shape, BF16)

    ask, facts = pl.pallas_call(
        functools.partial(ask_kernel, count=count, inner=inner),
        out_shape=(single, jax.ShapeDtypeStruct((FACTS, width), jnp.int32)),
        in_specs=[HBM, HBM], out_specs=(VMEM, VMEM),
        scratch_shapes=[pltpu.SMEM((count,), jnp.int32), late_bf16, late_packed,
                        pltpu.SemaphoreType.DMA((2,))],
        compiler_params=params(4), name="ask",
    )(in_hbm(new_slot), in_hbm(queries))

    column = [ask] + [send_outer(ask, k) for k in range(1, outer)]
    wishes = gather_inner(facts)

    chunks = 8
    weight, early = pl.pallas_call(
        functools.partial(prepare_kernel, count=count, chunks=chunks),
        out_shape=(jax.ShapeDtypeStruct((heads, 2 * width, width), BF16),
                   jax.ShapeDtypeStruct((2, BEFORE * heads, width), F32)),
        in_specs=[SMEM, HBM, HBM, HBM], out_specs=(VMEM, VMEM),
        scratch_shapes=[pltpu.VMEM((heads, width, width), F32),
                        pltpu.VMEM((2, BEFORE * heads * count, width), BF16),
                        pltpu.VMEM((BEFORE * heads * count, width), F32),
                        pltpu.SemaphoreType.DMA((chunks,)),
                        pltpu.SemaphoreType.DMA((2,))],
        compiler_params=params(12), name="prepare",
    )(in_hbm(new_slot), in_hbm(keys), in_hbm(values), in_hbm(states))

    asked = pl.pallas_call(
        functools.partial(route_kernel, inner=inner, outer=outer),
        out_shape=(single,) * inner,
        in_specs=[VMEM] * (1 + outer), out_specs=(VMEM,) * inner,
        compiler_params=params(4), name="route",
    )(wishes, *column)
    found = [send_inner(asked[k], k) for k in range(inner - 1, 0, -1)] + [asked[0]]

    answer = pl.pallas_call(
        functools.partial(answer_kernel, inner=inner, late=late, heads=heads, width=width),
        out_shape=single, in_specs=[VMEM] * (inner + 3), out_specs=VMEM,
        scratch_shapes=[pltpu.VMEM((2 * late * heads, width), F32)] * 2,
        compiler_params=params(8), name="answer",
    )(facts, *found, weight, early)
    replies = [answer] + [send_inner(answer, k) for k in range(1, inner)]

    sorted_replies = pl.pallas_call(
        functools.partial(reply_kernel, inner=inner, outer=outer),
        out_shape=(single,) * outer,
        in_specs=[VMEM] * (1 + inner), out_specs=(VMEM,) * outer,
        compiler_params=params(4), name="reply",
    )(wishes, *replies)
    parts = [send_outer(sorted_replies[k], k) for k in range(outer - 1, 0, -1)]

    chunks = 4
    output = jax.ShapeDtypeStruct((packed_rows, width), BF16)
    base, last, partial = pl.pallas_call(
        functools.partial(local_kernel, count=count, chunks=chunks),
        out_shape=(pltpu.HBM(output.shape, output.dtype), late_rows, jax.ShapeDtypeStruct((2, single_rows, width), F32)),
        in_specs=[VMEM] * 7 + [HBM], out_specs=(VMEM, VMEM, VMEM),
        scratch_shapes=[
            pltpu.VMEM((count, heads, width, width), F32),
            pltpu.VMEM((16 * heads * count, width), F32),
            pltpu.VMEM((16 * heads * count, width), F32),
            late_packed,
            pltpu.SemaphoreType.DMA((count, chunks)),
        ],
        compiler_params=params(16), name="local",
    )(facts, queries, keys, values, gates, norm_gain.reshape(heads, width),
      sorted_replies[0], in_hbm(states))

    return unpack(pl.pallas_call(
        functools.partial(finish_kernel, count=count, heads=heads),
        out_shape=output, in_specs=[VMEM, HBM] + [VMEM] * (outer + 1), out_specs=HBM,
        scratch_shapes=[late_bf16, late_packed, pltpu.SemaphoreType.DMA((late,))],
        input_output_aliases={1: 0},
        compiler_params=params(4), name="finish",
    )(facts, in_hbm(base), last, partial, *parts))


def solution(mesh):
    rows = P(("groups", "req"), None, None)
    in_specs = (rows, rows, rows, rows, P(("groups", "req"), None, None, None),
                P(("groups", "req")), P())
    return jax.shard_map(
        on_device, mesh=mesh, in_specs=in_specs, out_specs=rows, check_vma=False)
```

```python
import functools

import jax
import jax.numpy as jnp
from jax import lax
from jax.experimental import pallas as pl
from jax.experimental.pallas import tpu as pltpu
from jax.sharding import PartitionSpec as P

BEFORE = 3
EPS = 1e-06
F32 = jnp.float32
BF16 = jnp.bfloat16
MIB = 2**20
VMEM = pl.BlockSpec(memory_space=pltpu.VMEM)
SMEM = pl.BlockSpec(memory_space=pltpu.SMEM)
HBM = pl.BlockSpec(memory_space=pltpu.HBM)


def silu(x):
    return x / (1.0 + jnp.exp(-x))


def sigmoid(x):
    return 1.0 / (1.0 + jnp.exp(-x))


def moving_slot(slots_ref, count):
    base = lax.axis_index("req") * count
    place = jnp.int32(0)
    moves = slots_ref[0] != base
    for s in range(1, count):
        here = slots_ref[s] != base + s
        place = jnp.where(here, s, place)
        moves = jnp.logical_or(moves, here)
    return place, moves


def wanted_device(slots_ref, count):
    device = lax.axis_index("req")
    result = device
    for s in range(count):
        owner = lax.div(slots_ref[s], jnp.int32(count))
        result = jnp.where(owner != device, owner, result)
    return result


OUTER, INNER, SLOT, FACTS = 0, 1, 2, 8


def wish_steps(inner):
    if inner & (inner - 1):
        return list(range(inner))
    steps, step = [0], 1
    while step < inner:
        steps, step = steps + [s ^ step for s in steps], step * 2
    return steps


def fact(ref, place, kind, rows):
    row = place * FACTS + kind
    return jnp.broadcast_to(ref[row:row + 1, :], (rows, ref.shape[1]))


def head_slope(heads, width):
    order = lax.broadcasted_iota(jnp.int32, (heads, width), 0).astype(F32)
    return jnp.exp2(-8.0 * (order + 1.0) / (2.0 * heads))


def decay_power(slope, power):
    return jnp.exp(slope * (-float(power)))


def split(x):
    high = x.astype(BF16)
    return high, (x - high.astype(F32)).astype(BF16)


def extract(packed, place, count):
    rows = packed.shape[0] // count
    result = packed[pl.ds(0, rows, stride=count), :]
    for s in range(1, count):
        result = jnp.where(place == s, packed[pl.ds(s, rows, stride=count), :], result)
    return result


def turn(position, step, size):
    return position ^ step if size & (size - 1) == 0 else (position + step) % size


def unturn(position, step, size):
    return position ^ step if size & (size - 1) == 0 else (position - step) % size


def inverse_step(step, size):
    return step if size & (size - 1) == 0 else (size - step) % size


def in_steps(refs, order):
    result = [refs[0]] * len(refs)
    for step, ref in zip(order, refs[1:]):
        result[step] = ref
    return result


def choose(options, index, mine, size):
    result = options[0][...]
    for k in range(1, size):
        result = jnp.where(unturn(mine, k, size) == index, options[k][...], result)
    return result


def ask_kernel(new_slot_ref, queries_ref, out_ref, facts_ref, slots_ref, rows_ref, wide, sems, *,
               count, inner):
    late = rows_ref.shape[0]
    first = queries_ref.shape[0] - late
    slots_copy = pltpu.make_async_copy(new_slot_ref, slots_ref, sems.at[0])
    slots_copy.start()
    copy = pltpu.make_async_copy(queries_ref.at[pl.ds(first, late)], rows_ref, sems.at[1])
    copy.start()
    slots_copy.wait()
    place, moves = moving_slot(slots_ref, count)
    wanted = wanted_device(slots_ref, count)
    kind = lax.broadcasted_iota(jnp.int32, facts_ref.shape, 0)
    facts = jnp.where(kind == INNER, lax.rem(wanted, inner), jnp.where(moves, place, count))
    facts_ref[...] = jnp.where(kind == OUTER, lax.div(wanted, inner), facts)
    copy.wait()
    wide[...] = rows_ref[...].astype(F32)
    out_ref[...] = silu(extract(wide, place, count))


def prepare_kernel(slots_ref, keys_ref, values_ref, states_ref, weight_ref, early_ref,
                   state, rows_ref, wide, sems, row_sems, *, count, chunks):
    heads = states_ref.shape[1]
    size = heads // chunks
    place, _ = moving_slot(slots_ref, count)
    copies = [
        pltpu.make_async_copy(
            ref.at[pl.ds(0, wide.shape[0])], rows_ref.at[n], row_sems.at[n])
        for n, ref in enumerate((keys_ref, values_ref))]
    for copy in copies:
        copy.start()

    def load(c):
        part = pl.ds(c * size, size)
        return pltpu.make_async_copy(states_ref.at[place, part], state.at[part], sems.at[c])

    for c in range(chunks):
        load(c).start()
    for n, copy in enumerate(copies):
        copy.wait()
        wide[...] = rows_ref[n].astype(F32)
        early_ref[n] = silu(extract(wide, place, count))
    for c in range(chunks):
        load(c).wait()
        for h in range(c * size, (c + 1) * size):
            weight_ref[h] = jnp.concatenate(split(state[h]), axis=0)


def route_kernel(wishes_ref, *refs, inner, outer, order):
    column, outs = in_steps(refs[:outer], order), refs[outer:]
    my_outer = lax.div(lax.axis_index("req"), inner)
    for k in range(inner):
        back = wish_steps(inner).index(inverse_step(k, inner))
        wish = fact(wishes_ref, back, OUTER, outs[k].shape[0])
        outs[k][...] = choose(column, wish, my_outer, outer)


def answer_kernel(facts_ref, *refs, inner, late, heads, width, order):
    found, (weight_ref, early_ref, out_ref, lhs, prod) = refs[:inner], refs[inner:]
    found = in_steps(found, order)
    my_inner = lax.rem(lax.axis_index("req"), inner)
    block = lambda ref, t: ref[t * heads:(t + 1) * heads, :]
    rows = choose(found, fact(facts_ref, 0, INNER, late * heads), my_inner, inner)
    q = [rows[t * heads:(t + 1) * heads, :] for t in range(late)]
    slope = head_slope(heads, width)
    for t in range(late):
        x = q[t] * decay_power(slope, t + BEFORE + 1)
        high = x.astype(BF16).astype(F32)
        lhs[t * heads:(t + 1) * heads, :] = high
        lhs[(late + t) * heads:(late + t + 1) * heads, :] = x - high
    for h in range(heads):
        x = lhs[pl.ds(h, 2 * late, stride=heads), :].astype(BF16)
        prod[pl.ds(h, 2 * late, stride=heads), :] = jnp.dot(
            jnp.concatenate([x, x], axis=1), weight_ref[h], preferred_element_type=F32)
    for t in range(late):
        total = block(prod, t) + block(prod, late + t)
        for s in range(BEFORE):
            score = jnp.sum(q[t] * block(early_ref.at[0], s), axis=1, keepdims=True)
            total = total + score * decay_power(slope, t + BEFORE - s) * block(
                early_ref.at[1], s)
        out_ref[t * heads:(t + 1) * heads, :] = total


def reply_kernel(wishes_ref, *refs, inner, outer, order):
    replies, outs = in_steps(refs[:inner], order), refs[inner:]
    me = lax.axis_index("req")
    my_inner, my_outer = lax.rem(me, inner), lax.div(me, inner)
    rows = outs[0].shape[0]
    owner = [
        jnp.where(fact(wishes_ref, n, INNER, rows) == my_inner,
                  fact(wishes_ref, n, OUTER, rows), -1)
        for n in map(wish_steps(inner).index, range(inner))]
    for k in range(outer):
        result = 0.0
        for n in range(inner):
            result = jnp.where(owner[n] == turn(my_outer, k, outer), replies[n][...], result)
        outs[k][...] = result


def local_kernel(facts_ref, queries_ref, keys_ref, values_ref, gates_ref, gain_ref, own_ref,
                 states_ref, out_ref, last_ref, late_ref, state, lhs, prod, wide, sems, *, count, chunks):
    heads, width = states_ref.shape[1], states_ref.shape[2]
    span = heads * count
    steps = queries_ref.shape[0] // span
    late = steps - BEFORE
    size = heads // chunks
    place = fact(facts_ref, 0, SLOT, late * heads)

    def load(j, c):
        part = pl.ds(c * size, size)
        return pltpu.make_async_copy(states_ref.at[j, part], state.at[j, part], sems.at[j, c])

    for j in range(count):
        for c in range(chunks):
            load(j, c).start()

    def spread(x):
        for s in range(count):
            wide[pl.ds(s, heads, stride=count), :] = x
        return wide[:span, :]

    slope = spread(head_slope(heads, width))
    gain = spread(gain_ref[...])
    decay = [decay_power(slope, p) for p in range(steps + 1)]
    block = lambda ref, t: ref[t * span:(t + 1) * span, :]
    q = [silu(block(queries_ref, t).astype(F32)) for t in range(steps)]
    k = [silu(block(keys_ref, t).astype(F32)) for t in range(steps)]
    v = [silu(block(values_ref, t).astype(F32)) for t in range(steps)]
    for t in range(steps):
        x = q[t] * decay[t + 1]
        high = x.astype(BF16).astype(F32)
        lhs[t * span:(t + 1) * span, :] = high
        lhs[(8 + t) * span:(9 + t) * span, :] = x - high
    mixed = []
    for t in range(steps):
        total = None
        far = None
        for s in range(t + 1):
            score = jnp.sum(q[t] * k[s], axis=1, keepdims=True)
            term = score * decay[t - s] * v[s]
            if t >= BEFORE and s < BEFORE:
                far = term if far is None else far + term
            else:
                total = term if total is None else total + term
        if t >= BEFORE:
            wide[(t - BEFORE) * span:(t - BEFORE + 1) * span, :] = total
        mixed.append(total if far is None else total + far)
    late_ref[0] = extract(wide, place, count) + own_ref[...]
    scale = [gain * sigmoid(block(gates_ref, t).astype(F32)) for t in range(steps)]
    for t in range(late):
        wide[t * span:(t + 1) * span, :] = scale[BEFORE + t]
    late_ref[1] = extract(wide, place, count)
    for j in range(count):
        for c in range(chunks):
            load(j, c).wait()
            for h in range(c * size, (c + 1) * size):
                rows = pl.ds(h * count + j, 16, stride=span)
                x = lhs[rows, :].astype(BF16)
                prod[rows, :] = jnp.dot(
                    jnp.concatenate([x, x], axis=1),
                    jnp.concatenate(split(state[j, h]), axis=0),
                    preferred_element_type=F32)
    slot = lax.rem(lax.broadcasted_iota(jnp.int32, (span, 1), 0), jnp.int32(count))
    for t in range(steps):
        x = mixed[t] + block(prod, t) + block(prod, 8 + t)
        sums = jnp.sum(x * x, axis=1, keepdims=True)
        energy = jnp.zeros((span, 1), F32)
        for s in range(count):
            whole = jnp.sum(jnp.where(slot == s, sums, 0.0), axis=0, keepdims=True)
            energy = jnp.where(slot == s, whole, energy)
        factor = lax.rsqrt(energy * (1.0 / (heads * width)) + EPS)
        y = (x * factor * scale[t]).astype(BF16)
        out_ref[t * span:(t + 1) * span, :] = y
        if t >= BEFORE:
            last_ref[(t - BEFORE) * span:(t - BEFORE + 1) * span, :] = y


def finish_kernel(facts_ref, base_ref, last_ref, late_ref, *refs, count, heads):
    parts, (out_ref, rows_ref, wide, sems) = refs[:-4], refs[-4:]
    place = fact(facts_ref, 0, SLOT, heads)
    span = heads * count
    steps = late_ref.shape[1] // heads
    first = out_ref.shape[0] - steps * span
    copies = []
    for t in range(steps):
        part = slice(t * heads, (t + 1) * heads)
        x = late_ref[0, part, :]
        for ref in parts:
            x = x + ref[part, :]
        y = x * lax.rsqrt(jnp.mean(x * x) + EPS) * late_ref[1, part, :]
        rows = slice(t * span, (t + 1) * span)
        wide[rows, :] = last_ref[rows, :].astype(F32)
        for s in range(count):
            here = pl.ds(t * span + s, heads, stride=count)
            wide[here, :] = jnp.where(place == s, y, wide[here, :])
        rows_ref[rows, :] = wide[rows, :].astype(BF16)
        copies.append(pltpu.make_async_copy(
            rows_ref.at[pl.ds(t * span, span)], out_ref.at[pl.ds(first + t * span, span)],
            sems.at[t]))
        copies[t].start()
    for copy in copies:
        copy.wait()


def in_hbm(x):
    return pltpu.with_memory_space_constraint(x, pltpu.HBM)


def near_square(total):
    return next(
        (d, total // d) for d in range(1, total + 1) if total % d == 0 and d * d >= total)


def on_device(queries, keys, values, gates, states, new_slot, norm_gain):
    count, steps, features = queries.shape
    heads, width = states.shape[1], states.shape[2]
    late = steps - BEFORE
    packed_rows, single_rows = steps * heads * count, late * heads
    inner, outer = near_square(lax.axis_size("req"))

    def pack(x):
        return x.reshape(count, steps, heads, width).transpose(1, 2, 0, 3).reshape(
            packed_rows, width)

    def unpack(x):
        return x.reshape(steps, heads, count, width).transpose(2, 0, 1, 3).reshape(
            count, steps, features)

    def send_inner(x, k):
        return lax.ppermute(x, "req", [
            (o * inner + i, o * inner + int(turn(i, k, inner)))
            for o in range(outer) for i in range(inner)])

    def send_outer(x, k):
        return lax.ppermute(x, "req", [
            (o * inner + i, int(turn(o, k, outer)) * inner + i)
            for o in range(outer) for i in range(inner)])

    def gather_inner(x):
        if inner & (inner - 1):
            return jnp.concatenate([x] + [send_inner(x, k) for k in range(1, inner)])
        own, step = x[:FACTS], 1
        x = jnp.concatenate([own, send_inner(x, step)[:FACTS]])
        while 2 * step < inner:
            step *= 2
            x = jnp.concatenate([x, send_inner(x, step)])
        return x

    def params(limit):
        return pltpu.CompilerParams(vmem_limit_bytes=limit * MIB)

    queries, keys, values, gates = pack(queries), pack(keys), pack(values), pack(gates)
    single = jax.ShapeDtypeStruct((single_rows, width), F32)
    late_packed = pltpu.VMEM((late * heads * count, width), F32)

    late_rows = jax.ShapeDtypeStruct((late * heads * count, width), BF16)
    late_bf16 = pltpu.VMEM(late_rows.shape, BF16)

    ask, facts = pl.pallas_call(
        functools.partial(ask_kernel, count=count, inner=inner),
        out_shape=(single, jax.ShapeDtypeStruct((FACTS, width), jnp.int32)),
        in_specs=[HBM, HBM], out_specs=(VMEM, VMEM),
        scratch_shapes=[pltpu.SMEM((count,), jnp.int32), late_bf16, late_packed,
                        pltpu.SemaphoreType.DMA((2,))],
        compiler_params=params(4), name="ask",
    )(in_hbm(new_slot), in_hbm(queries))

    up, half = list(range(1, outer)), outer // 2
    z1, z2 = up, up[half - 1:] + up[:half - 1]
    q1, q2 = list(range(inner - 1, 0, -1)), list(range(1, inner))
    column = [ask] + [send_outer(ask, k) for k in z1]
    wishes = gather_inner(facts)

    chunks = 8
    weight, early = pl.pallas_call(
        functools.partial(prepare_kernel, count=count, chunks=chunks),
        out_shape=(jax.ShapeDtypeStruct((heads, 2 * width, width), BF16),
                   jax.ShapeDtypeStruct((2, BEFORE * heads, width), F32)),
        in_specs=[SMEM, HBM, HBM, HBM], out_specs=(VMEM, VMEM),
        scratch_shapes=[pltpu.VMEM((heads, width, width), F32),
                        pltpu.VMEM((2, BEFORE * heads * count, width), BF16),
                        pltpu.VMEM((BEFORE * heads * count, width), F32),
                        pltpu.SemaphoreType.DMA((chunks,)),
                        pltpu.SemaphoreType.DMA((2,))],
        compiler_params=params(12), name="prepare",
    )(in_hbm(new_slot), in_hbm(keys), in_hbm(values), in_hbm(states))

    asked = pl.pallas_call(
        functools.partial(route_kernel, inner=inner, outer=outer, order=z1),
        out_shape=(single,) * inner,
        in_specs=[VMEM] * (1 + outer), out_specs=(VMEM,) * inner,
        compiler_params=params(4), name="route",
    )(wishes, *column)
    found = [asked[0]] + [send_inner(asked[k], k) for k in q1]

    answer = pl.pallas_call(
        functools.partial(answer_kernel, inner=inner, late=late, heads=heads, width=width,
                          order=q1),
        out_shape=single, in_specs=[VMEM] * (inner + 3), out_specs=VMEM,
        scratch_shapes=[pltpu.VMEM((2 * late * heads, width), F32)] * 2,
        compiler_params=params(8), name="answer",
    )(facts, *found, weight, early)
    replies = [answer] + [send_inner(answer, k) for k in q2]

    sorted_replies = pl.pallas_call(
        functools.partial(reply_kernel, inner=inner, outer=outer, order=q2),
        out_shape=(single,) * outer,
        in_specs=[VMEM] * (1 + inner), out_specs=(VMEM,) * outer,
        compiler_params=params(4), name="reply",
    )(wishes, *replies)
    parts = [send_outer(sorted_replies[k], k) for k in z2]

    chunks = 4
    output = jax.ShapeDtypeStruct((packed_rows, width), BF16)
    base, last, partial = pl.pallas_call(
        functools.partial(local_kernel, count=count, chunks=chunks),
        out_shape=(pltpu.HBM(output.shape, output.dtype), late_rows, jax.ShapeDtypeStruct((2, single_rows, width), F32)),
        in_specs=[VMEM] * 7 + [HBM], out_specs=(VMEM, VMEM, VMEM),
        scratch_shapes=[
            pltpu.VMEM((count, heads, width, width), F32),
            pltpu.VMEM((16 * heads * count, width), F32),
            pltpu.VMEM((16 * heads * count, width), F32),
            late_packed,
            pltpu.SemaphoreType.DMA((count, chunks)),
        ],
        compiler_params=params(16), name="local",
    )(facts, queries, keys, values, gates, norm_gain.reshape(heads, width),
      sorted_replies[0], in_hbm(states))

    return unpack(pl.pallas_call(
        functools.partial(finish_kernel, count=count, heads=heads),
        out_shape=output, in_specs=[VMEM, HBM] + [VMEM] * (outer + 1), out_specs=HBM,
        scratch_shapes=[late_bf16, late_packed, pltpu.SemaphoreType.DMA((late,))],
        input_output_aliases={1: 0},
        compiler_params=params(4), name="finish",
    )(facts, in_hbm(base), last, partial, *parts))


def solution(mesh):
    rows = P(("groups", "req"), None, None)
    in_specs = (rows, rows, rows, rows, P(("groups", "req"), None, None, None),
                P(("groups", "req")), P())
    return jax.shard_map(
        on_device, mesh=mesh, in_specs=in_specs, out_specs=rows, check_vma=False)
```

```python
import functools

import jax
import jax.numpy as jnp
from jax import lax
from jax.experimental import pallas as pl
from jax.experimental.pallas import tpu as pltpu
from jax.sharding import PartitionSpec as P

BEFORE = 3
EPS = 1e-06
F32 = jnp.float32
BF16 = jnp.bfloat16
MIB = 2**20
VMEM = pl.BlockSpec(memory_space=pltpu.VMEM)
SMEM = pl.BlockSpec(memory_space=pltpu.SMEM)
HBM = pl.BlockSpec(memory_space=pltpu.HBM)


def silu(x):
    return x / (1.0 + jnp.exp(-x))


def sigmoid(x):
    return 1.0 / (1.0 + jnp.exp(-x))


def moving_slot(slots_ref, count):
    base = lax.axis_index("req") * count
    place = jnp.int32(0)
    moves = slots_ref[0] != base
    for s in range(1, count):
        here = slots_ref[s] != base + s
        place = jnp.where(here, s, place)
        moves = jnp.logical_or(moves, here)
    return place, moves


def wanted_device(slots_ref, count):
    device = lax.axis_index("req")
    result = device
    for s in range(count):
        owner = lax.div(slots_ref[s], jnp.int32(count))
        result = jnp.where(owner != device, owner, result)
    return result


OUTER, INNER, SLOT, FACTS = 0, 1, 2, 8


def wish_steps(inner):
    if inner & (inner - 1):
        return list(range(inner))
    steps, step = [0], 1
    while step < inner:
        steps, step = steps + [s ^ step for s in steps], step * 2
    return steps


def fact(ref, place, kind, rows):
    row = place * FACTS + kind
    return jnp.broadcast_to(ref[row:row + 1, :], (rows, ref.shape[1]))


def head_slope(heads, width):
    order = lax.broadcasted_iota(jnp.int32, (heads, width), 0).astype(F32)
    return jnp.exp2(-8.0 * (order + 1.0) / (2.0 * heads))


def decay_power(slope, power):
    return jnp.exp(slope * (-float(power)))


def split(x):
    high = x.astype(BF16)
    return high, (x - high.astype(F32)).astype(BF16)


def extract(packed, place, count):
    rows = packed.shape[0] // count
    result = packed[pl.ds(0, rows, stride=count), :]
    for s in range(1, count):
        result = jnp.where(place == s, packed[pl.ds(s, rows, stride=count), :], result)
    return result


def turn(position, step, size):
    return position ^ step if size & (size - 1) == 0 else (position + step) % size


def unturn(position, step, size):
    return position ^ step if size & (size - 1) == 0 else (position - step) % size


def inverse_step(step, size):
    return step if size & (size - 1) == 0 else (size - step) % size


def in_steps(refs, order):
    result = [refs[0]] * len(refs)
    for step, ref in zip(order, refs[1:]):
        result[step] = ref
    return result


def choose(options, index, mine, size):
    rows = index.shape[0]
    result = options[0][:rows, :]
    for k in range(1, size):
        result = jnp.where(unturn(mine, k, size) == index, options[k][:rows, :], result)
    return result


def ask_kernel(new_slot_ref, queries_ref, out_ref, long_ref, facts_ref, slots_ref, rows_ref, wide,
               sems, *, count, inner):
    late = rows_ref.shape[0]
    first = queries_ref.shape[0] - late
    slots_copy = pltpu.make_async_copy(new_slot_ref, slots_ref, sems.at[0])
    slots_copy.start()
    copy = pltpu.make_async_copy(queries_ref.at[pl.ds(first, late)], rows_ref, sems.at[1])
    copy.start()
    slots_copy.wait()
    place, moves = moving_slot(slots_ref, count)
    wanted = wanted_device(slots_ref, count)
    kind = lax.broadcasted_iota(jnp.int32, facts_ref.shape, 0)
    facts = jnp.where(kind == INNER, lax.rem(wanted, inner), jnp.where(moves, place, count))
    facts_ref[...] = jnp.where(kind == OUTER, lax.div(wanted, inner), facts)
    copy.wait()
    wide[...] = rows_ref[...].astype(F32)
    rows = silu(extract(wide, place, count))
    out_ref[...] = rows
    long_ref[:rows.shape[0], :] = rows
    long_ref[rows.shape[0]:, :] = jnp.zeros_like(long_ref[rows.shape[0]:, :])


def pair_kernel(near_ref, far_ref, out_ref):
    rows = out_ref.shape[0] // 2
    out_ref[:rows, :] = near_ref[:rows, :]
    out_ref[rows:, :] = far_ref[:rows, :]


def prepare_kernel(slots_ref, keys_ref, values_ref, states_ref, weight_ref, early_ref,
                   state, rows_ref, wide, sems, row_sems, *, count, chunks):
    heads = states_ref.shape[1]
    size = heads // chunks
    place, _ = moving_slot(slots_ref, count)
    copies = [
        pltpu.make_async_copy(
            ref.at[pl.ds(0, wide.shape[0])], rows_ref.at[n], row_sems.at[n])
        for n, ref in enumerate((keys_ref, values_ref))]
    for copy in copies:
        copy.start()

    def load(c):
        part = pl.ds(c * size, size)
        return pltpu.make_async_copy(states_ref.at[place, part], state.at[part], sems.at[c])

    for c in range(chunks):
        load(c).start()
    for n, copy in enumerate(copies):
        copy.wait()
        wide[...] = rows_ref[n].astype(F32)
        early_ref[n] = silu(extract(wide, place, count))
    for c in range(chunks):
        load(c).wait()
        for h in range(c * size, (c + 1) * size):
            weight_ref[h] = jnp.concatenate(split(state[h]), axis=0)


def route_kernel(wishes_ref, *refs, inner, outer, order):
    column, outs = in_steps(refs[:outer], order), refs[outer:]
    my_outer = lax.div(lax.axis_index("req"), inner)
    for k in range(inner):
        back = wish_steps(inner).index(inverse_step(k, inner))
        wish = fact(wishes_ref, back, OUTER, outs[k].shape[0])
        outs[k][...] = choose(column, wish, my_outer, outer)


def answer_kernel(facts_ref, *refs, inner, late, heads, width, order):
    found, (weight_ref, early_ref, out_ref, lhs, prod) = refs[:inner], refs[inner:]
    found = in_steps(found, order)
    my_inner = lax.rem(lax.axis_index("req"), inner)
    block = lambda ref, t: ref[t * heads:(t + 1) * heads, :]
    rows = choose(found, fact(facts_ref, 0, INNER, late * heads), my_inner, inner)
    q = [rows[t * heads:(t + 1) * heads, :] for t in range(late)]
    slope = head_slope(heads, width)
    for t in range(late):
        x = q[t] * decay_power(slope, t + BEFORE + 1)
        high = x.astype(BF16).astype(F32)
        lhs[t * heads:(t + 1) * heads, :] = high
        lhs[(late + t) * heads:(late + t + 1) * heads, :] = x - high
    for h in range(heads):
        x = lhs[pl.ds(h, 2 * late, stride=heads), :].astype(BF16)
        prod[pl.ds(h, 2 * late, stride=heads), :] = jnp.dot(
            jnp.concatenate([x, x], axis=1), weight_ref[h], preferred_element_type=F32)
    for t in range(late):
        total = block(prod, t) + block(prod, late + t)
        for s in range(BEFORE):
            score = jnp.sum(q[t] * block(early_ref.at[0], s), axis=1, keepdims=True)
            total = total + score * decay_power(slope, t + BEFORE - s) * block(
                early_ref.at[1], s)
        out_ref[t * heads:(t + 1) * heads, :] = total


def reply_kernel(wishes_ref, *refs, inner, outer, order):
    replies, outs = in_steps(refs[:inner], order), refs[inner:]
    me = lax.axis_index("req")
    my_inner, my_outer = lax.rem(me, inner), lax.div(me, inner)
    rows = outs[0].shape[0]
    owner = [
        jnp.where(fact(wishes_ref, n, INNER, rows) == my_inner,
                  fact(wishes_ref, n, OUTER, rows), -1)
        for n in map(wish_steps(inner).index, range(inner))]
    for k in range(outer):
        result = 0.0
        for n in range(inner):
            result = jnp.where(owner[n] == turn(my_outer, k, outer), replies[n][...], result)
        outs[k][...] = result


def local_kernel(facts_ref, queries_ref, keys_ref, values_ref, gates_ref, gain_ref, own_ref,
                 states_ref, out_ref, last_ref, late_ref, state, lhs, prod, wide, sems, *, count, chunks):
    heads, width = states_ref.shape[1], states_ref.shape[2]
    span = heads * count
    steps = queries_ref.shape[0] // span
    late = steps - BEFORE
    size = heads // chunks
    place = fact(facts_ref, 0, SLOT, late * heads)

    def load(j, c):
        part = pl.ds(c * size, size)
        return pltpu.make_async_copy(states_ref.at[j, part], state.at[j, part], sems.at[j, c])

    for j in range(count):
        for c in range(chunks):
            load(j, c).start()

    def spread(x):
        for s in range(count):
            wide[pl.ds(s, heads, stride=count), :] = x
        return wide[:span, :]

    slope = spread(head_slope(heads, width))
    gain = spread(gain_ref[...])
    decay = [decay_power(slope, p) for p in range(steps + 1)]
    block = lambda ref, t: ref[t * span:(t + 1) * span, :]
    q = [silu(block(queries_ref, t).astype(F32)) for t in range(steps)]
    k = [silu(block(keys_ref, t).astype(F32)) for t in range(steps)]
    v = [silu(block(values_ref, t).astype(F32)) for t in range(steps)]
    for t in range(steps):
        x = q[t] * decay[t + 1]
        high = x.astype(BF16).astype(F32)
        lhs[t * span:(t + 1) * span, :] = high
        lhs[(8 + t) * span:(9 + t) * span, :] = x - high
    mixed = []
    for t in range(steps):
        total = None
        far = None
        for s in range(t + 1):
            score = jnp.sum(q[t] * k[s], axis=1, keepdims=True)
            term = score * decay[t - s] * v[s]
            if t >= BEFORE and s < BEFORE:
                far = term if far is None else far + term
            else:
                total = term if total is None else total + term
        if t >= BEFORE:
            wide[(t - BEFORE) * span:(t - BEFORE + 1) * span, :] = total
        mixed.append(total if far is None else total + far)
    late_ref[0] = extract(wide, place, count) + own_ref[...]
    scale = [gain * sigmoid(block(gates_ref, t).astype(F32)) for t in range(steps)]
    for t in range(late):
        wide[t * span:(t + 1) * span, :] = scale[BEFORE + t]
    late_ref[1] = extract(wide, place, count)
    for j in range(count):
        for c in range(chunks):
            load(j, c).wait()
            for h in range(c * size, (c + 1) * size):
                rows = pl.ds(h * count + j, 16, stride=span)
                x = lhs[rows, :].astype(BF16)
                prod[rows, :] = jnp.dot(
                    jnp.concatenate([x, x], axis=1),
                    jnp.concatenate(split(state[j, h]), axis=0),
                    preferred_element_type=F32)
    slot = lax.rem(lax.broadcasted_iota(jnp.int32, (span, 1), 0), jnp.int32(count))
    for t in range(steps):
        x = mixed[t] + block(prod, t) + block(prod, 8 + t)
        sums = jnp.sum(x * x, axis=1, keepdims=True)
        energy = jnp.zeros((span, 1), F32)
        for s in range(count):
            whole = jnp.sum(jnp.where(slot == s, sums, 0.0), axis=0, keepdims=True)
            energy = jnp.where(slot == s, whole, energy)
        factor = lax.rsqrt(energy * (1.0 / (heads * width)) + EPS)
        y = (x * factor * scale[t]).astype(BF16)
        out_ref[t * span:(t + 1) * span, :] = y
        if t >= BEFORE:
            last_ref[(t - BEFORE) * span:(t - BEFORE + 1) * span, :] = y


def finish_kernel(facts_ref, base_ref, last_ref, late_ref, *refs, count, heads):
    parts, (out_ref, rows_ref, wide, sems) = refs[:-4], refs[-4:]
    place = fact(facts_ref, 0, SLOT, heads)
    span = heads * count
    steps = late_ref.shape[1] // heads
    first = out_ref.shape[0] - steps * span
    copies = []
    for t in range(steps):
        part = slice(t * heads, (t + 1) * heads)
        x = late_ref[0, part, :]
        for ref in parts:
            x = x + ref[part, :]
        y = x * lax.rsqrt(jnp.mean(x * x) + EPS) * late_ref[1, part, :]
        rows = slice(t * span, (t + 1) * span)
        wide[rows, :] = last_ref[rows, :].astype(F32)
        for s in range(count):
            here = pl.ds(t * span + s, heads, stride=count)
            wide[here, :] = jnp.where(place == s, y, wide[here, :])
        rows_ref[rows, :] = wide[rows, :].astype(BF16)
        copies.append(pltpu.make_async_copy(
            rows_ref.at[pl.ds(t * span, span)], out_ref.at[pl.ds(first + t * span, span)],
            sems.at[t]))
        copies[t].start()
    for copy in copies:
        copy.wait()


def in_hbm(x):
    return pltpu.with_memory_space_constraint(x, pltpu.HBM)


def near_square(total):
    return next(
        (d, total // d) for d in range(1, total + 1) if total % d == 0 and d * d >= total)


def on_device(queries, keys, values, gates, states, new_slot, norm_gain):
    count, steps, features = queries.shape
    heads, width = states.shape[1], states.shape[2]
    late = steps - BEFORE
    packed_rows, single_rows = steps * heads * count, late * heads
    inner, outer = near_square(lax.axis_size("req"))

    def pack(x):
        return x.reshape(count, steps, heads, width).transpose(1, 2, 0, 3).reshape(
            packed_rows, width)

    def unpack(x):
        return x.reshape(steps, heads, count, width).transpose(2, 0, 1, 3).reshape(
            count, steps, features)

    def send_inner(x, k):
        return lax.ppermute(x, "req", [
            (o * inner + i, o * inner + int(turn(i, k, inner)))
            for o in range(outer) for i in range(inner)])

    def send_outer(x, k):
        return lax.ppermute(x, "req", [
            (o * inner + i, int(turn(o, k, outer)) * inner + i)
            for o in range(outer) for i in range(inner)])

    def gather_inner(x):
        if inner & (inner - 1):
            x = x[:FACTS]
            return jnp.concatenate([x] + [send_inner(x, k) for k in range(1, inner)])
        step, result = 1, x
        while step < inner:
            result = pl.pallas_call(
                pair_kernel,
                out_shape=jax.ShapeDtypeStruct((2 * step * FACTS, width), jnp.int32),
                in_specs=[VMEM, VMEM], out_specs=VMEM, compiler_params=params(4), name="pair",
            )(result, send_inner(result, step))
            step *= 2
        return result

    def params(limit):
        return pltpu.CompilerParams(vmem_limit_bytes=limit * MIB)

    queries, keys, values, gates = pack(queries), pack(keys), pack(values), pack(gates)
    single = jax.ShapeDtypeStruct((single_rows, width), F32)
    late_packed = pltpu.VMEM((late * heads * count, width), F32)

    late_rows = jax.ShapeDtypeStruct((late * heads * count, width), BF16)
    late_bf16 = pltpu.VMEM(late_rows.shape, BF16)

    long = jax.ShapeDtypeStruct((single_rows + FACTS, width), F32)
    facts_rows = max(single_rows * 5 // (6 * FACTS), 1) * FACTS
    ask, ask_long, facts = pl.pallas_call(
        functools.partial(ask_kernel, count=count, inner=inner),
        out_shape=(single, long, jax.ShapeDtypeStruct((facts_rows, width), jnp.int32)),
        in_specs=[HBM, HBM], out_specs=(VMEM, VMEM, VMEM),
        scratch_shapes=[pltpu.SMEM((count,), jnp.int32), late_bf16, late_packed,
                        pltpu.SemaphoreType.DMA((2,))],
        compiler_params=params(4), name="ask",
    )(in_hbm(new_slot), in_hbm(queries))

    up, half = list(range(1, outer)), outer // 2
    z1, z2 = up, up[half - 1:] + up[:half - 1]
    q1, q2 = list(range(inner - 1, 0, -1)), list(range(1, inner))
    column = [ask] + [send_outer(ask_long if k == outer - 1 else ask, k) for k in z1]
    wishes = gather_inner(facts)

    chunks = 8
    weight, early = pl.pallas_call(
        functools.partial(prepare_kernel, count=count, chunks=chunks),
        out_shape=(jax.ShapeDtypeStruct((heads, 2 * width, width), BF16),
                   jax.ShapeDtypeStruct((2, BEFORE * heads, width), F32)),
        in_specs=[SMEM, HBM, HBM, HBM], out_specs=(VMEM, VMEM),
        scratch_shapes=[pltpu.VMEM((heads, width, width), F32),
                        pltpu.VMEM((2, BEFORE * heads * count, width), BF16),
                        pltpu.VMEM((BEFORE * heads * count, width), F32),
                        pltpu.SemaphoreType.DMA((chunks,)),
                        pltpu.SemaphoreType.DMA((2,))],
        compiler_params=params(12), name="prepare",
    )(in_hbm(new_slot), in_hbm(keys), in_hbm(values), in_hbm(states))

    asked = pl.pallas_call(
        functools.partial(route_kernel, inner=inner, outer=outer, order=z1),
        out_shape=(single,) * inner,
        in_specs=[VMEM] * (1 + outer), out_specs=(VMEM,) * inner,
        compiler_params=params(4), name="route",
    )(wishes, *column)
    found = [asked[0]] + [send_inner(asked[k], k) for k in q1]

    answer = pl.pallas_call(
        functools.partial(answer_kernel, inner=inner, late=late, heads=heads, width=width,
                          order=q1),
        out_shape=single, in_specs=[VMEM] * (inner + 3), out_specs=VMEM,
        scratch_shapes=[pltpu.VMEM((2 * late * heads, width), F32)] * 2,
        compiler_params=params(8), name="answer",
    )(facts, *found, weight, early)
    replies = [answer] + [send_inner(answer, k) for k in q2]

    sorted_replies = pl.pallas_call(
        functools.partial(reply_kernel, inner=inner, outer=outer, order=q2),
        out_shape=(single,) * outer,
        in_specs=[VMEM] * (1 + inner), out_specs=(VMEM,) * outer,
        compiler_params=params(4), name="reply",
    )(wishes, *replies)
    parts = [send_outer(sorted_replies[k], k) for k in z2]

    chunks = 4
    output = jax.ShapeDtypeStruct((packed_rows, width), BF16)
    base, last, partial = pl.pallas_call(
        functools.partial(local_kernel, count=count, chunks=chunks),
        out_shape=(pltpu.HBM(output.shape, output.dtype), late_rows, jax.ShapeDtypeStruct((2, single_rows, width), F32)),
        in_specs=[VMEM] * 7 + [HBM], out_specs=(VMEM, VMEM, VMEM),
        scratch_shapes=[
            pltpu.VMEM((count, heads, width, width), F32),
            pltpu.VMEM((16 * heads * count, width), F32),
            pltpu.VMEM((16 * heads * count, width), F32),
            late_packed,
            pltpu.SemaphoreType.DMA((count, chunks)),
        ],
        compiler_params=params(16), name="local",
    )(facts, queries, keys, values, gates, norm_gain.reshape(heads, width),
      sorted_replies[0], in_hbm(states))

    return unpack(pl.pallas_call(
        functools.partial(finish_kernel, count=count, heads=heads),
        out_shape=output, in_specs=[VMEM, HBM] + [VMEM] * (outer + 1), out_specs=HBM,
        scratch_shapes=[late_bf16, late_packed, pltpu.SemaphoreType.DMA((late,))],
        input_output_aliases={1: 0},
        compiler_params=params(4), name="finish",
    )(facts, in_hbm(base), last, partial, *parts))


def solution(mesh):
    rows = P(("groups", "req"), None, None)
    in_specs = (rows, rows, rows, rows, P(("groups", "req"), None, None, None),
                P(("groups", "req")), P())
    return jax.shard_map(
        on_device, mesh=mesh, in_specs=in_specs, out_specs=rows, check_vma=False)
```

```python
import functools

import jax
import jax.numpy as jnp
from jax import lax
from jax.experimental import pallas as pl
from jax.experimental.pallas import tpu as pltpu
from jax.sharding import PartitionSpec as P

BEFORE = 3
EPS = 1e-06
F32 = jnp.float32
BF16 = jnp.bfloat16
MIB = 2**20
VMEM = pl.BlockSpec(memory_space=pltpu.VMEM)
SMEM = pl.BlockSpec(memory_space=pltpu.SMEM)
HBM = pl.BlockSpec(memory_space=pltpu.HBM)
ANY = pl.BlockSpec(memory_space=pl.ANY)


def silu(x):
    return x / (1.0 + jnp.exp(-x))


def sigmoid(x):
    return 1.0 / (1.0 + jnp.exp(-x))


def moving_slot(slots_ref, count):
    base = lax.axis_index("req") * count
    place = jnp.int32(0)
    moves = slots_ref[0] != base
    for s in range(1, count):
        here = slots_ref[s] != base + s
        place = jnp.where(here, s, place)
        moves = jnp.logical_or(moves, here)
    return place, moves


def wanted_device(slots_ref, count):
    device = lax.axis_index("req")
    result = device
    for s in range(count):
        owner = lax.div(slots_ref[s], jnp.int32(count))
        result = jnp.where(owner != device, owner, result)
    return result


OUTER, INNER, SLOT, FACTS = 0, 1, 2, 8


def wish_steps(inner):
    if inner & (inner - 1):
        return list(range(inner))
    steps, step = [0], 1
    while step < inner:
        steps, step = steps + [s ^ step for s in steps], step * 2
    return steps


def fact(ref, place, kind, rows):
    row = place * FACTS + kind
    return jnp.broadcast_to(ref[row:row + 1, :], (rows, ref.shape[1]))


def head_slope(heads, width):
    order = lax.broadcasted_iota(jnp.int32, (heads, width), 0).astype(F32)
    return jnp.exp2(-8.0 * (order + 1.0) / (2.0 * heads))


def decay_power(slope, power):
    return jnp.exp(slope * (-float(power)))


def split(x):
    high = x.astype(BF16)
    return high, (x - high.astype(F32)).astype(BF16)


def extract(packed, place, count):
    rows = packed.shape[0] // count
    result = packed[pl.ds(0, rows, stride=count), :]
    for s in range(1, count):
        result = jnp.where(place == s, packed[pl.ds(s, rows, stride=count), :], result)
    return result


def turn(position, step, size):
    return position ^ step if size & (size - 1) == 0 else (position + step) % size


def unturn(position, step, size):
    return position ^ step if size & (size - 1) == 0 else (position - step) % size


def inverse_step(step, size):
    return step if size & (size - 1) == 0 else (size - step) % size


def in_steps(refs, order):
    result = [refs[0]] * len(refs)
    for step, ref in zip(order, refs[1:]):
        result[step] = ref
    return result


def choose(options, index, mine, size):
    rows = index.shape[0]
    result = options[0][:rows, :]
    for k in range(1, size):
        result = jnp.where(unturn(mine, k, size) == index, options[k][:rows, :], result)
    return result


def ask_kernel(new_slot_ref, queries_ref, out_ref, long_ref, facts_ref, slots_ref, rows_ref, wide,
               sems, *, count, inner):
    late = rows_ref.shape[0]
    first = queries_ref.shape[0] - late
    slots_copy = pltpu.make_async_copy(new_slot_ref, slots_ref, sems.at[0])
    slots_copy.start()
    copy = pltpu.make_async_copy(queries_ref.at[pl.ds(first, late)], rows_ref, sems.at[1])
    copy.start()
    slots_copy.wait()
    place, moves = moving_slot(slots_ref, count)
    wanted = wanted_device(slots_ref, count)
    kind = lax.broadcasted_iota(jnp.int32, facts_ref.shape, 0)
    facts = jnp.where(kind == INNER, lax.rem(wanted, inner), jnp.where(moves, place, count))
    facts_ref[...] = jnp.where(kind == OUTER, lax.div(wanted, inner), facts)
    copy.wait()
    wide[...] = rows_ref[...].astype(F32)
    rows = silu(extract(wide, place, count))
    out_ref[...] = rows
    long_ref[:rows.shape[0], :] = rows
    long_ref[rows.shape[0]:, :] = jnp.zeros_like(long_ref[rows.shape[0]:, :])


def pair_kernel(near_ref, far_ref, out_ref):
    rows = out_ref.shape[0] // 2
    out_ref[:rows, :] = near_ref[:rows, :]
    out_ref[rows:, :] = far_ref[:rows, :]


def prepare_kernel(slots_ref, keys_ref, values_ref, states_ref, weight_ref, early_ref,
                   state, rows_ref, wide, sems, row_sems, *, count, chunks):
    heads = states_ref.shape[1]
    size = heads // chunks
    place, _ = moving_slot(slots_ref, count)
    copies = [
        pltpu.make_async_copy(
            ref.at[pl.ds(0, wide.shape[0])], rows_ref.at[n], row_sems.at[n])
        for n, ref in enumerate((keys_ref, values_ref))]
    for copy in copies:
        copy.start()

    def load(c):
        part = pl.ds(c * size, size)
        return pltpu.make_async_copy(states_ref.at[place, part], state.at[part], sems.at[c])

    for c in range(chunks):
        load(c).start()
    for n, copy in enumerate(copies):
        copy.wait()
        wide[...] = rows_ref[n].astype(F32)
        early_ref[n] = silu(extract(wide, place, count))
    for c in range(chunks):
        load(c).wait()
        for h in range(c * size, (c + 1) * size):
            weight_ref[h] = jnp.concatenate(split(state[h]), axis=0)


def route_kernel(wishes_ref, *refs, inner, outer, order):
    column, outs = in_steps(refs[:outer], order), refs[outer:]
    my_outer = lax.div(lax.axis_index("req"), inner)
    for k in range(inner):
        back = wish_steps(inner).index(inverse_step(k, inner))
        wish = fact(wishes_ref, back, OUTER, outs[k].shape[0])
        outs[k][...] = choose(column, wish, my_outer, outer)


def answer_kernel(facts_ref, *refs, inner, late, heads, width, order):
    found, (weight_ref, early_ref, out_ref, lhs, prod) = refs[:inner], refs[inner:]
    found = in_steps(found, order)
    my_inner = lax.rem(lax.axis_index("req"), inner)
    block = lambda ref, t: ref[t * heads:(t + 1) * heads, :]
    rows = choose(found, fact(facts_ref, 0, INNER, late * heads), my_inner, inner)
    q = [rows[t * heads:(t + 1) * heads, :] for t in range(late)]
    slope = head_slope(heads, width)
    for t in range(late):
        x = q[t] * decay_power(slope, t + BEFORE + 1)
        high = x.astype(BF16).astype(F32)
        lhs[t * heads:(t + 1) * heads, :] = high
        lhs[(late + t) * heads:(late + t + 1) * heads, :] = x - high
    for h in range(heads):
        x = lhs[pl.ds(h, 2 * late, stride=heads), :].astype(BF16)
        prod[pl.ds(h, 2 * late, stride=heads), :] = jnp.dot(
            jnp.concatenate([x, x], axis=1), weight_ref[h], preferred_element_type=F32)
    for t in range(late):
        total = block(prod, t) + block(prod, late + t)
        for s in range(BEFORE):
            score = jnp.sum(q[t] * block(early_ref.at[0], s), axis=1, keepdims=True)
            total = total + score * decay_power(slope, t + BEFORE - s) * block(
                early_ref.at[1], s)
        out_ref[t * heads:(t + 1) * heads, :] = total


def reply_kernel(wishes_ref, after_ref, *refs, inner, outer, order):
    replies, outs = in_steps(refs[:inner], order), refs[inner:]
    me = lax.axis_index("req")
    my_inner, my_outer = lax.rem(me, inner), lax.div(me, inner)
    rows = outs[0].shape[0]
    owner = [
        jnp.where(fact(wishes_ref, n, INNER, rows) == my_inner,
                  fact(wishes_ref, n, OUTER, rows), -1)
        for n in map(wish_steps(inner).index, range(inner))]
    for k in range(outer):
        result = 0.0
        for n in range(inner):
            result = jnp.where(owner[n] == turn(my_outer, k, outer), replies[n][...], result)
        outs[k][...] = result


def load_states(states_ref, state, sems, slots, chunks):
    size = states_ref.shape[1] // chunks

    def load(n, c):
        part = pl.ds(c * size, size)
        return pltpu.make_async_copy(
            states_ref.at[slots[n], part], state.at[n, part], sems.at[n, c])

    for n in range(len(slots)):
        for c in range(chunks):
            load(n, c).start()
    return load


def times_states(load, state, lhs, prod, slots, count, chunks):
    heads = state.shape[1]
    size = heads // chunks
    for n, slot in enumerate(slots):
        for c in range(chunks):
            load(n, c).wait()
            for h in range(c * size, (c + 1) * size):
                rows = pl.ds(h * count + slot, 16, stride=heads * count)
                x = lhs[rows, :].astype(BF16)
                prod[rows, :] = jnp.dot(
                    jnp.concatenate([x, x], axis=1),
                    jnp.concatenate(split(state[n, h]), axis=0),
                    preferred_element_type=F32)


def row_slot(span, count):
    return lax.rem(lax.broadcasted_iota(jnp.int32, (span, 1), 0), jnp.int32(count))


def block(ref, t, rows):
    return ref[t * rows:(t + 1) * rows, :]


def scores_kernel(facts_ref, queries_ref, keys_ref, values_ref, gates_ref, gain_ref, after_ref,
                  states_ref, mixed_ref, scale_ref, late_ref, lhs, state, prod, wide, sems,
                  *, slots, count, chunks):
    heads, width = states_ref.shape[1], states_ref.shape[2]
    span = heads * count
    steps = queries_ref.shape[0] // span
    late = steps - BEFORE
    place = fact(facts_ref, 0, SLOT, late * heads)
    load = load_states(states_ref, state, sems, slots, chunks)

    def spread(x):
        for s in range(count):
            wide[pl.ds(s, heads, stride=count), :] = x
        return wide[:span, :]

    slope = spread(head_slope(heads, width))
    gain = spread(gain_ref[...])
    decay = [decay_power(slope, p) for p in range(steps + 1)]
    q = [silu(block(queries_ref, t, span).astype(F32)) for t in range(steps)]
    k = [silu(block(keys_ref, t, span).astype(F32)) for t in range(steps)]
    v = [silu(block(values_ref, t, span).astype(F32)) for t in range(steps)]
    for t in range(steps):
        x = q[t] * decay[t + 1]
        high = x.astype(BF16).astype(F32)
        lhs[t * span:(t + 1) * span, :] = high
        lhs[(8 + t) * span:(9 + t) * span, :] = x - high
    for t in range(steps):
        total = None
        far = None
        for s in range(t + 1):
            score = jnp.sum(q[t] * k[s], axis=1, keepdims=True)
            term = score * decay[t - s] * v[s]
            if t >= BEFORE and s < BEFORE:
                far = term if far is None else far + term
            else:
                total = term if total is None else total + term
        if t >= BEFORE:
            wide[(t - BEFORE) * span:(t - BEFORE + 1) * span, :] = total
        mixed_ref[t * span:(t + 1) * span, :] = total if far is None else total + far
    late_ref[0] = extract(wide, place, count)
    for t in range(steps):
        scale = gain * sigmoid(block(gates_ref, t, span).astype(F32))
        scale_ref[t * span:(t + 1) * span, :] = scale
        if t >= BEFORE:
            wide[(t - BEFORE) * span:(t - BEFORE + 1) * span, :] = scale
    late_ref[1] = extract(wide, place, count)
    times_states(load, state, lhs, prod, slots, count, chunks)
    slot = row_slot(span, count)
    for t in range(steps):
        x = block(prod, t, span) + block(prod, 8 + t, span)
        for s in slots:
            rows = slice(t * span, (t + 1) * span)
            mixed_ref[rows, :] = mixed_ref[rows, :] + jnp.where(slot == s, x, 0.0)


def local_kernel(mixed_ref, scale_ref, lhs, after_ref, states_ref, out_ref, last_ref, state, prod,
                 sems, *, slots, count, chunks):
    heads, width = states_ref.shape[1], states_ref.shape[2]
    span = heads * count
    steps = mixed_ref.shape[0] // span
    load = load_states(states_ref, state, sems, slots, chunks)
    times_states(load, state, lhs, prod, slots, count, chunks)
    slot = row_slot(span, count)
    for t in range(steps):
        x = block(mixed_ref, t, span)
        for s in slots:
            x = x + jnp.where(slot == s, block(prod, t, span) + block(prod, 8 + t, span), 0.0)
        sums = jnp.sum(x * x, axis=1, keepdims=True)
        energy = jnp.zeros((span, 1), F32)
        for s in range(count):
            whole = jnp.sum(jnp.where(slot == s, sums, 0.0), axis=0, keepdims=True)
            energy = jnp.where(slot == s, whole, energy)
        factor = lax.rsqrt(energy * (1.0 / (heads * width)) + EPS)
        y = (x * factor * block(scale_ref, t, span)).astype(BF16)
        out_ref[t * span:(t + 1) * span, :] = y
        if t >= BEFORE:
            last_ref[(t - BEFORE) * span:(t - BEFORE + 1) * span, :] = y


def finish_kernel(facts_ref, base_ref, last_ref, late_ref, *refs, count, heads):
    parts, (out_ref, rows_ref, wide, sems) = refs[:-4], refs[-4:]
    place = fact(facts_ref, 0, SLOT, heads)
    span = heads * count
    steps = late_ref.shape[1] // heads
    first = out_ref.shape[0] - steps * span
    copies = []
    for t in range(steps):
        part = slice(t * heads, (t + 1) * heads)
        x = late_ref[0, part, :]
        for ref in parts:
            x = x + ref[part, :]
        energy = jnp.sum(jnp.sum(x * x, axis=0, keepdims=True), axis=1, keepdims=True)
        y = x * lax.rsqrt(energy * (1.0 / x.size) + EPS) * late_ref[1, part, :]
        rows = slice(t * span, (t + 1) * span)
        wide[rows, :] = last_ref[rows, :].astype(F32)
        for s in range(count):
            here = pl.ds(t * span + s, heads, stride=count)
            wide[here, :] = jnp.where(place == s, y, wide[here, :])
        rows_ref[rows, :] = wide[rows, :].astype(BF16)
        copies.append(pltpu.make_async_copy(
            rows_ref.at[pl.ds(t * span, span)], out_ref.at[pl.ds(first + t * span, span)],
            sems.at[t]))
        copies[t].start()
    for copy in copies:
        copy.wait()


def in_hbm(x):
    return pltpu.with_memory_space_constraint(x, pltpu.HBM)


def near_square(total):
    return next(
        (d, total // d) for d in range(1, total + 1) if total % d == 0 and d * d >= total)


def on_device(queries, keys, values, gates, states, new_slot, norm_gain):
    count, steps, features = queries.shape
    heads, width = states.shape[1], states.shape[2]
    late = steps - BEFORE
    packed_rows, single_rows = steps * heads * count, late * heads
    inner, outer = near_square(lax.axis_size("req"))

    def pack(x):
        return x.reshape(count, steps, heads, width).transpose(1, 2, 0, 3).reshape(
            packed_rows, width)

    def unpack(x):
        return x.reshape(steps, heads, count, width).transpose(2, 0, 1, 3).reshape(
            count, steps, features)

    def send_inner(x, k):
        return lax.ppermute(x, "req", [
            (o * inner + i, o * inner + int(turn(i, k, inner)))
            for o in range(outer) for i in range(inner)])

    def send_outer(x, k):
        return lax.ppermute(x, "req", [
            (o * inner + i, int(turn(o, k, outer)) * inner + i)
            for o in range(outer) for i in range(inner)])

    def gather_inner(x):
        if inner & (inner - 1):
            x = x[:FACTS]
            return jnp.concatenate([x] + [send_inner(x, k) for k in range(1, inner)])
        step, result = 1, x
        while step < inner:
            result = pl.pallas_call(
                pair_kernel,
                out_shape=jax.ShapeDtypeStruct((2 * step * FACTS, width), jnp.int32),
                in_specs=[VMEM, VMEM], out_specs=VMEM, compiler_params=params(4), name="pair",
            )(result, send_inner(result, step))
            step *= 2
        return result

    def params(limit):
        return pltpu.CompilerParams(vmem_limit_bytes=limit * MIB)

    queries, keys, values, gates = pack(queries), pack(keys), pack(values), pack(gates)
    single = jax.ShapeDtypeStruct((single_rows, width), F32)
    late_packed = pltpu.VMEM((late * heads * count, width), F32)

    late_rows = jax.ShapeDtypeStruct((late * heads * count, width), BF16)
    late_bf16 = pltpu.VMEM(late_rows.shape, BF16)

    long = jax.ShapeDtypeStruct((single_rows + FACTS, width), F32)
    facts_rows = max(single_rows * 5 // (6 * FACTS), 1) * FACTS
    ask, ask_long, facts = pl.pallas_call(
        functools.partial(ask_kernel, count=count, inner=inner),
        out_shape=(single, long, jax.ShapeDtypeStruct((facts_rows, width), jnp.int32)),
        in_specs=[HBM, HBM], out_specs=(VMEM, VMEM, VMEM),
        scratch_shapes=[pltpu.SMEM((count,), jnp.int32), late_bf16, late_packed,
                        pltpu.SemaphoreType.DMA((2,))],
        compiler_params=params(4), name="ask",
    )(in_hbm(new_slot), in_hbm(queries))

    up, half = list(range(1, outer)), outer // 2
    z1, z2 = up, up[half - 1:] + up[:half - 1]
    q1, q2 = list(range(inner - 1, 0, -1)), list(range(1, inner))
    column = [ask] + [send_outer(ask_long if k == outer - 1 else ask, k) for k in z1]
    wishes = gather_inner(facts)

    chunks = 8
    weight, early = pl.pallas_call(
        functools.partial(prepare_kernel, count=count, chunks=chunks),
        out_shape=(jax.ShapeDtypeStruct((heads, 2 * width, width), BF16),
                   jax.ShapeDtypeStruct((2, BEFORE * heads, width), F32)),
        in_specs=[SMEM, HBM, HBM, HBM], out_specs=(VMEM, VMEM),
        scratch_shapes=[pltpu.VMEM((heads, width, width), F32),
                        pltpu.VMEM((2, BEFORE * heads * count, width), BF16),
                        pltpu.VMEM((BEFORE * heads * count, width), F32),
                        pltpu.SemaphoreType.DMA((chunks,)),
                        pltpu.SemaphoreType.DMA((2,))],
        compiler_params=params(12), name="prepare",
    )(in_hbm(new_slot), in_hbm(keys), in_hbm(values), in_hbm(states))

    asked = pl.pallas_call(
        functools.partial(route_kernel, inner=inner, outer=outer, order=z1),
        out_shape=(single,) * inner,
        in_specs=[VMEM] * (1 + outer), out_specs=(VMEM,) * inner,
        compiler_params=params(4), name="route",
    )(wishes, *column)
    found = [asked[0]] + [send_inner(asked[k], k) for k in q1]

    answer = pl.pallas_call(
        functools.partial(answer_kernel, inner=inner, late=late, heads=heads, width=width,
                          order=q1),
        out_shape=single, in_specs=[VMEM] * (inner + 3), out_specs=VMEM,
        scratch_shapes=[pltpu.VMEM((2 * late * heads, width), F32)] * 2,
        compiler_params=params(8), name="answer",
    )(facts, *found, weight, early)
    replies = [answer] + [send_inner(answer, k) for k in q2]

    chunks = 4
    first_slots, last_slots = list(range(count // 2)), list(range(count // 2, count))
    packed = jax.ShapeDtypeStruct((packed_rows, width), F32)
    products = jax.ShapeDtypeStruct((16 * heads * count, width), F32)
    mixed, scale, partial, lhs = pl.pallas_call(
        functools.partial(scores_kernel, slots=first_slots, count=count, chunks=chunks),
        out_shape=(packed, packed, jax.ShapeDtypeStruct((2, single_rows, width), F32), products),
        in_specs=[VMEM] * 6 + [ANY, HBM], out_specs=(VMEM,) * 4,
        scratch_shapes=[
            pltpu.VMEM((max(len(first_slots), 1), heads, width, width), F32),
            pltpu.VMEM(products.shape, F32),
            late_packed,
            pltpu.SemaphoreType.DMA((max(len(first_slots), 1), chunks)),
        ],
        compiler_params=params(16), name="scores",
    )(facts, queries, keys, values, gates, norm_gain.reshape(heads, width), answer,
      in_hbm(states))

    sorted_replies = pl.pallas_call(
        functools.partial(reply_kernel, inner=inner, outer=outer, order=q2),
        out_shape=(single,) * outer,
        in_specs=[VMEM, ANY] + [VMEM] * inner, out_specs=(VMEM,) * outer,
        compiler_params=params(4), name="reply",
    )(wishes, partial, *replies)
    parts = [send_outer(sorted_replies[k], k) for k in z2]

    output = jax.ShapeDtypeStruct((packed_rows, width), BF16)
    base, last = pl.pallas_call(
        functools.partial(local_kernel, slots=last_slots, count=count, chunks=chunks),
        out_shape=(pltpu.HBM(output.shape, output.dtype), late_rows),
        in_specs=[VMEM] * 3 + [ANY, HBM], out_specs=(VMEM, VMEM),
        scratch_shapes=[
            pltpu.VMEM((len(last_slots), heads, width, width), F32),
            pltpu.VMEM(products.shape, F32),
            pltpu.SemaphoreType.DMA((len(last_slots), chunks)),
        ],
        compiler_params=params(16), name="local",
    )(mixed, scale, lhs, sorted_replies[0], in_hbm(states))

    return unpack(pl.pallas_call(
        functools.partial(finish_kernel, count=count, heads=heads),
        out_shape=output, in_specs=[VMEM, HBM] + [VMEM] * (outer + 2), out_specs=HBM,
        scratch_shapes=[late_bf16, late_packed, pltpu.SemaphoreType.DMA((late,))],
        input_output_aliases={1: 0},
        compiler_params=params(4), name="finish",
    )(facts, in_hbm(base), last, partial, sorted_replies[0], *parts))


def solution(mesh):
    rows = P(("groups", "req"), None, None)
    in_specs = (rows, rows, rows, rows, P(("groups", "req"), None, None, None),
                P(("groups", "req")), P())
    return jax.shard_map(
        on_device, mesh=mesh, in_specs=in_specs, out_specs=rows, check_vma=False)
```

```python
import functools

import jax
import jax.numpy as jnp
from jax import lax
from jax.experimental import pallas as pl
from jax.experimental.pallas import tpu as pltpu
from jax.sharding import PartitionSpec as P

BEFORE = 3
EPS = 1e-06
F32 = jnp.float32
BF16 = jnp.bfloat16
MIB = 2**20
VMEM = pl.BlockSpec(memory_space=pltpu.VMEM)
SMEM = pl.BlockSpec(memory_space=pltpu.SMEM)
HBM = pl.BlockSpec(memory_space=pltpu.HBM)
ANY = pl.BlockSpec(memory_space=pl.ANY)


def silu(x):
    return x / (1.0 + jnp.exp(-x))


def sigmoid(x):
    return 1.0 / (1.0 + jnp.exp(-x))


def moving_slot(slots_ref, count):
    base = lax.axis_index("req") * count
    place = jnp.int32(0)
    moves = slots_ref[0] != base
    for s in range(1, count):
        here = slots_ref[s] != base + s
        place = jnp.where(here, s, place)
        moves = jnp.logical_or(moves, here)
    return place, moves


def wanted_device(slots_ref, count):
    device = lax.axis_index("req")
    result = device
    for s in range(count):
        owner = lax.div(slots_ref[s], jnp.int32(count))
        result = jnp.where(owner != device, owner, result)
    return result


OUTER, INNER, SLOT, FACTS = 0, 1, 2, 8


def wish_steps(inner):
    if inner & (inner - 1):
        return list(range(inner))
    steps, step = [0], 1
    while step < inner:
        steps, step = steps + [s ^ step for s in steps], step * 2
    return steps


def fact(ref, place, kind, rows):
    row = place * FACTS + kind
    return jnp.broadcast_to(ref[row:row + 1, :], (rows, ref.shape[1]))


def head_slope(heads, width):
    order = lax.broadcasted_iota(jnp.int32, (heads, width), 0).astype(F32)
    return jnp.exp2(-8.0 * (order + 1.0) / (2.0 * heads))


def decay_power(slope, power):
    return jnp.exp(slope * (-float(power)))


def split(x):
    high = x.astype(BF16)
    return high, (x - high.astype(F32)).astype(BF16)


def extract(packed, place, count):
    rows = packed.shape[0] // count
    result = packed[pl.ds(0, rows, stride=count), :]
    for s in range(1, count):
        result = jnp.where(place == s, packed[pl.ds(s, rows, stride=count), :], result)
    return result


def turn(position, step, size):
    return position ^ step if size & (size - 1) == 0 else (position + step) % size


def unturn(position, step, size):
    return position ^ step if size & (size - 1) == 0 else (position - step) % size


def shift(position, step, size):
    return lax.rem(position + step, size)


def inverse_step(step, size):
    return step if size & (size - 1) == 0 else (size - step) % size


def in_steps(refs, order):
    result = [refs[0]] * len(refs)
    for step, ref in zip(order, refs[1:]):
        result[step] = ref
    return result


def choose(options, index, sources):
    rows = index.shape[0]
    result = options[0][:rows, :]
    for option, source in zip(options[1:], sources[1:]):
        result = jnp.where(source == index, option[:rows, :], result)
    return result


def ask_kernel(new_slot_ref, queries_ref, out_ref, long_ref, facts_ref, slots_ref, rows_ref, wide,
               sems, *, count, inner):
    late = rows_ref.shape[0]
    first = queries_ref.shape[0] - late
    slots_copy = pltpu.make_async_copy(new_slot_ref, slots_ref, sems.at[0])
    slots_copy.start()
    copy = pltpu.make_async_copy(queries_ref.at[pl.ds(first, late)], rows_ref, sems.at[1])
    copy.start()
    slots_copy.wait()
    place, moves = moving_slot(slots_ref, count)
    wanted = wanted_device(slots_ref, count)
    kind = lax.broadcasted_iota(jnp.int32, facts_ref.shape, 0)
    facts = jnp.where(kind == INNER, lax.rem(wanted, inner), jnp.where(moves, place, count))
    facts_ref[...] = jnp.where(kind == OUTER, lax.div(wanted, inner), facts)
    copy.wait()
    wide[...] = rows_ref[...].astype(F32)
    rows = silu(extract(wide, place, count))
    out_ref[...] = rows
    long_ref[:rows.shape[0], :] = rows
    long_ref[rows.shape[0]:, :] = jnp.zeros_like(long_ref[rows.shape[0]:, :])


def pair_kernel(near_ref, far_ref, out_ref):
    rows = out_ref.shape[0] // 2
    out_ref[:rows, :] = near_ref[:rows, :]
    out_ref[rows:, :] = far_ref[:rows, :]


def prepare_kernel(slots_ref, keys_ref, values_ref, states_ref, weight_ref, early_ref,
                   state, rows_ref, wide, sems, row_sems, *, count, chunks):
    heads = states_ref.shape[1]
    size = heads // chunks
    place, _ = moving_slot(slots_ref, count)
    copies = [
        pltpu.make_async_copy(
            ref.at[pl.ds(0, wide.shape[0])], rows_ref.at[n], row_sems.at[n])
        for n, ref in enumerate((keys_ref, values_ref))]
    for copy in copies:
        copy.start()

    def load(c):
        part = pl.ds(c * size, size)
        return pltpu.make_async_copy(states_ref.at[place, part], state.at[part], sems.at[c])

    for c in range(chunks):
        load(c).start()
    for n, copy in enumerate(copies):
        copy.wait()
        wide[...] = rows_ref[n].astype(F32)
        early_ref[n] = silu(extract(wide, place, count))
    for c in range(chunks):
        load(c).wait()
        for h in range(c * size, (c + 1) * size):
            weight_ref[h] = jnp.concatenate(split(state[h]), axis=0)


def route_kernel(wishes_ref, *refs, inner, outer, order):
    column, outs = in_steps(refs[:outer], order), refs[outer:]
    my_outer = lax.div(lax.axis_index("req"), inner)
    for k in range(inner):
        back = wish_steps(inner).index(inverse_step(k, inner))
        wish = fact(wishes_ref, back, OUTER, outs[k].shape[0])
        outs[k][...] = choose(column, wish, [unturn(my_outer, k, outer) for k in range(outer)])


def answer_kernel(facts_ref, *refs, inner, late, heads, width, order):
    found, (weight_ref, early_ref, out_ref, lhs, prod) = refs[:inner], refs[inner:]
    found = in_steps(found, order)
    my_inner = lax.rem(lax.axis_index("req"), inner)
    block = lambda ref, t: ref[t * heads:(t + 1) * heads, :]
    sources = [unturn(my_inner, k, inner) for k in range(inner)]
    rows = choose(found, fact(facts_ref, 0, INNER, late * heads), sources)
    q = [rows[t * heads:(t + 1) * heads, :] for t in range(late)]
    slope = head_slope(heads, width)
    for t in range(late):
        x = q[t] * decay_power(slope, t + BEFORE + 1)
        high = x.astype(BF16).astype(F32)
        lhs[t * heads:(t + 1) * heads, :] = high
        lhs[(late + t) * heads:(late + t + 1) * heads, :] = x - high
    for h in range(heads):
        x = lhs[pl.ds(h, 2 * late, stride=heads), :].astype(BF16)
        prod[pl.ds(h, 2 * late, stride=heads), :] = jnp.dot(
            jnp.concatenate([x, x], axis=1), weight_ref[h], preferred_element_type=F32)
    for t in range(late):
        total = block(prod, t) + block(prod, late + t)
        for s in range(BEFORE):
            score = jnp.sum(q[t] * block(early_ref.at[0], s), axis=1, keepdims=True)
            total = total + score * decay_power(slope, t + BEFORE - s) * block(
                early_ref.at[1], s)
        out_ref[t * heads:(t + 1) * heads, :] = total


def reply_kernel(wishes_ref, after_ref, *refs, inner, outer, order):
    replies, outs = in_steps(refs[:inner], order), refs[inner:]
    me = lax.axis_index("req")
    my_inner, my_outer = lax.rem(me, inner), lax.div(me, inner)
    rows = outs[0].shape[0]
    owner = [
        jnp.where(fact(wishes_ref, n, INNER, rows) == my_inner,
                  fact(wishes_ref, n, OUTER, rows), -1)
        for n in map(wish_steps(inner).index, range(inner))]
    for k in range(outer):
        result = 0.0
        for n in range(inner):
            result = jnp.where(owner[n] == shift(my_outer, k, outer), replies[n][...], result)
        outs[k][...] = result


def load_states(states_ref, state, sems, slots, chunks):
    size = states_ref.shape[1] // chunks

    def load(n, c):
        part = pl.ds(c * size, size)
        return pltpu.make_async_copy(
            states_ref.at[slots[n], part], state.at[n, part], sems.at[n, c])

    for n in range(len(slots)):
        for c in range(chunks):
            load(n, c).start()
    return load


def times_states(load, state, lhs, prod, slots, count, chunks):
    heads = state.shape[1]
    size = heads // chunks
    for n, slot in enumerate(slots):
        for c in range(chunks):
            load(n, c).wait()
            for h in range(c * size, (c + 1) * size):
                rows = pl.ds(h * count + slot, 16, stride=heads * count)
                x = lhs[rows, :].astype(BF16)
                prod[rows, :] = jnp.dot(
                    jnp.concatenate([x, x], axis=1),
                    jnp.concatenate(split(state[n, h]), axis=0),
                    preferred_element_type=F32)


def row_slot(span, count):
    return lax.rem(lax.broadcasted_iota(jnp.int32, (span, 1), 0), jnp.int32(count))


def block(ref, t, rows):
    return ref[t * rows:(t + 1) * rows, :]


def scores_kernel(facts_ref, queries_ref, keys_ref, values_ref, gates_ref, gain_ref, after_ref,
                  states_ref, mixed_ref, scale_ref, late_ref, lhs, state, prod, wide, sems,
                  *, slots, count, chunks):
    heads, width = states_ref.shape[1], states_ref.shape[2]
    span = heads * count
    steps = queries_ref.shape[0] // span
    late = steps - BEFORE
    place = fact(facts_ref, 0, SLOT, late * heads)
    load = load_states(states_ref, state, sems, slots, chunks)

    def spread(x):
        for s in range(count):
            wide[pl.ds(s, heads, stride=count), :] = x
        return wide[:span, :]

    slope = spread(head_slope(heads, width))
    gain = spread(gain_ref[...])
    decay = [decay_power(slope, p) for p in range(steps + 1)]
    q = [silu(block(queries_ref, t, span).astype(F32)) for t in range(steps)]
    k = [silu(block(keys_ref, t, span).astype(F32)) for t in range(steps)]
    v = [silu(block(values_ref, t, span).astype(F32)) for t in range(steps)]
    for t in range(steps):
        x = q[t] * decay[t + 1]
        high = x.astype(BF16).astype(F32)
        lhs[t * span:(t + 1) * span, :] = high
        lhs[(8 + t) * span:(9 + t) * span, :] = x - high
    for t in range(steps):
        total = None
        far = None
        for s in range(t + 1):
            score = jnp.sum(q[t] * k[s], axis=1, keepdims=True)
            term = score * decay[t - s] * v[s]
            if t >= BEFORE and s < BEFORE:
                far = term if far is None else far + term
            else:
                total = term if total is None else total + term
        if t >= BEFORE:
            wide[(t - BEFORE) * span:(t - BEFORE + 1) * span, :] = total
        mixed_ref[t * span:(t + 1) * span, :] = total if far is None else total + far
    late_ref[0] = extract(wide, place, count)
    for t in range(steps):
        scale = gain * sigmoid(block(gates_ref, t, span).astype(F32))
        scale_ref[t * span:(t + 1) * span, :] = scale
        if t >= BEFORE:
            wide[(t - BEFORE) * span:(t - BEFORE + 1) * span, :] = scale
    late_ref[1] = extract(wide, place, count)
    times_states(load, state, lhs, prod, slots, count, chunks)
    slot = row_slot(span, count)
    for t in range(steps):
        x = block(prod, t, span) + block(prod, 8 + t, span)
        for s in slots:
            rows = slice(t * span, (t + 1) * span)
            mixed_ref[rows, :] = mixed_ref[rows, :] + jnp.where(slot == s, x, 0.0)


def local_kernel(mixed_ref, scale_ref, lhs, after_ref, states_ref, out_ref, last_ref, state, prod,
                 sems, *, slots, count, chunks):
    heads, width = states_ref.shape[1], states_ref.shape[2]
    span = heads * count
    steps = mixed_ref.shape[0] // span
    load = load_states(states_ref, state, sems, slots, chunks)
    times_states(load, state, lhs, prod, slots, count, chunks)
    slot = row_slot(span, count)
    for t in range(steps):
        x = block(mixed_ref, t, span)
        for s in slots:
            x = x + jnp.where(slot == s, block(prod, t, span) + block(prod, 8 + t, span), 0.0)
        sums = jnp.sum(x * x, axis=1, keepdims=True)
        energy = jnp.zeros((span, 1), F32)
        for s in range(count):
            whole = jnp.sum(jnp.where(slot == s, sums, 0.0), axis=0, keepdims=True)
            energy = jnp.where(slot == s, whole, energy)
        factor = lax.rsqrt(energy * (1.0 / (heads * width)) + EPS)
        y = (x * factor * block(scale_ref, t, span)).astype(BF16)
        out_ref[t * span:(t + 1) * span, :] = y
        if t >= BEFORE:
            last_ref[(t - BEFORE) * span:(t - BEFORE + 1) * span, :] = y


def finish_kernel(facts_ref, base_ref, last_ref, late_ref, *refs, count, heads):
    parts, (out_ref, rows_ref, wide, sems) = refs[:-4], refs[-4:]
    place = fact(facts_ref, 0, SLOT, heads)
    span = heads * count
    steps = late_ref.shape[1] // heads
    first = out_ref.shape[0] - steps * span
    copies = []
    for t in range(steps):
        part = slice(t * heads, (t + 1) * heads)
        x = late_ref[0, part, :]
        for ref in parts:
            x = x + ref[part, :]
        energy = jnp.sum(jnp.sum(x * x, axis=0, keepdims=True), axis=1, keepdims=True)
        y = x * lax.rsqrt(energy * (1.0 / x.size) + EPS) * late_ref[1, part, :]
        rows = slice(t * span, (t + 1) * span)
        wide[rows, :] = last_ref[rows, :].astype(F32)
        for s in range(count):
            here = pl.ds(t * span + s, heads, stride=count)
            wide[here, :] = jnp.where(place == s, y, wide[here, :])
        rows_ref[rows, :] = wide[rows, :].astype(BF16)
        copies.append(pltpu.make_async_copy(
            rows_ref.at[pl.ds(t * span, span)], out_ref.at[pl.ds(first + t * span, span)],
            sems.at[t]))
        copies[t].start()
    for copy in copies:
        copy.wait()


def in_hbm(x):
    return pltpu.with_memory_space_constraint(x, pltpu.HBM)


def near_square(total):
    return next(
        (d, total // d) for d in range(1, total + 1) if total % d == 0 and d * d >= total)


def on_device(queries, keys, values, gates, states, new_slot, norm_gain):
    count, steps, features = queries.shape
    heads, width = states.shape[1], states.shape[2]
    late = steps - BEFORE
    packed_rows, single_rows = steps * heads * count, late * heads
    inner, outer = near_square(lax.axis_size("req"))

    def pack(x):
        return x.reshape(count, steps, heads, width).transpose(1, 2, 0, 3).reshape(
            packed_rows, width)

    def unpack(x):
        return x.reshape(steps, heads, count, width).transpose(2, 0, 1, 3).reshape(
            count, steps, features)

    def send_inner(x, k):
        return lax.ppermute(x, "req", [
            (o * inner + i, o * inner + int(turn(i, k, inner)))
            for o in range(outer) for i in range(inner)])

    def send_outer(x, k):
        return lax.ppermute(x, "req", [
            (o * inner + i, int(turn(o, k, outer)) * inner + i)
            for o in range(outer) for i in range(inner)])

    def gather_inner(x):
        if inner & (inner - 1):
            x = x[:FACTS]
            return jnp.concatenate([x] + [send_inner(x, k) for k in range(1, inner)])
        step, result = 1, x
        while step < inner:
            result = pl.pallas_call(
                pair_kernel,
                out_shape=jax.ShapeDtypeStruct((2 * step * FACTS, width), jnp.int32),
                in_specs=[VMEM, VMEM], out_specs=VMEM, compiler_params=params(4), name="pair",
            )(result, send_inner(result, step))
            step *= 2
        return result

    def shift_outer(x, k):
        return lax.ppermute(x, "req", [
            (o * inner + i, (o + k) % outer * inner + i)
            for o in range(outer) for i in range(inner)])

    def params(limit):
        return pltpu.CompilerParams(vmem_limit_bytes=limit * MIB)

    queries, keys, values, gates = pack(queries), pack(keys), pack(values), pack(gates)
    single = jax.ShapeDtypeStruct((single_rows, width), F32)
    late_packed = pltpu.VMEM((late * heads * count, width), F32)

    late_rows = jax.ShapeDtypeStruct((late * heads * count, width), BF16)
    late_bf16 = pltpu.VMEM(late_rows.shape, BF16)

    long = jax.ShapeDtypeStruct((single_rows + FACTS, width), F32)
    facts_rows = max(single_rows * 5 // (6 * FACTS), 1) * FACTS
    ask, ask_long, facts = pl.pallas_call(
        functools.partial(ask_kernel, count=count, inner=inner),
        out_shape=(single, long, jax.ShapeDtypeStruct((facts_rows, width), jnp.int32)),
        in_specs=[HBM, HBM], out_specs=(VMEM, VMEM, VMEM),
        scratch_shapes=[pltpu.SMEM((count,), jnp.int32), late_bf16, late_packed,
                        pltpu.SemaphoreType.DMA((2,))],
        compiler_params=params(4), name="ask",
    )(in_hbm(new_slot), in_hbm(queries))

    z1, z2 = list(range(1, outer)), list(range(1, outer))
    q1, q2 = list(range(inner - 1, 0, -1)), list(range(1, inner))
    column = [ask] + [send_outer(ask_long if k == outer - 1 else ask, k) for k in z1]
    wishes = gather_inner(facts)

    chunks = 8
    weight, early = pl.pallas_call(
        functools.partial(prepare_kernel, count=count, chunks=chunks),
        out_shape=(jax.ShapeDtypeStruct((heads, 2 * width, width), BF16),
                   jax.ShapeDtypeStruct((2, BEFORE * heads, width), F32)),
        in_specs=[SMEM, HBM, HBM, HBM], out_specs=(VMEM, VMEM),
        scratch_shapes=[pltpu.VMEM((heads, width, width), F32),
                        pltpu.VMEM((2, BEFORE * heads * count, width), BF16),
                        pltpu.VMEM((BEFORE * heads * count, width), F32),
                        pltpu.SemaphoreType.DMA((chunks,)),
                        pltpu.SemaphoreType.DMA((2,))],
        compiler_params=params(12), name="prepare",
    )(in_hbm(new_slot), in_hbm(keys), in_hbm(values), in_hbm(states))

    asked = pl.pallas_call(
        functools.partial(route_kernel, inner=inner, outer=outer, order=z1),
        out_shape=(single,) * inner,
        in_specs=[VMEM] * (1 + outer), out_specs=(VMEM,) * inner,
        compiler_params=params(4), name="route",
    )(wishes, *column)
    found = [asked[0]] + [send_inner(asked[k], k) for k in q1]

    answer = pl.pallas_call(
        functools.partial(answer_kernel, inner=inner, late=late, heads=heads, width=width,
                          order=q1),
        out_shape=single, in_specs=[VMEM] * (inner + 3), out_specs=VMEM,
        scratch_shapes=[pltpu.VMEM((2 * late * heads, width), F32)] * 2,
        compiler_params=params(8), name="answer",
    )(facts, *found, weight, early)
    replies = [answer] + [send_inner(answer, k) for k in q2]

    chunks = 4
    first_slots, last_slots = list(range(count // 2)), list(range(count // 2, count))
    packed = jax.ShapeDtypeStruct((packed_rows, width), F32)
    products = jax.ShapeDtypeStruct((16 * heads * count, width), F32)
    mixed, scale, partial, lhs = pl.pallas_call(
        functools.partial(scores_kernel, slots=first_slots, count=count, chunks=chunks),
        out_shape=(packed, packed, jax.ShapeDtypeStruct((2, single_rows, width), F32), products),
        in_specs=[VMEM] * 6 + [ANY, HBM], out_specs=(VMEM,) * 4,
        scratch_shapes=[
            pltpu.VMEM((max(len(first_slots), 1), heads, width, width), F32),
            pltpu.VMEM(products.shape, F32),
            late_packed,
            pltpu.SemaphoreType.DMA((max(len(first_slots), 1), chunks)),
        ],
        compiler_params=params(16), name="scores",
    )(facts, queries, keys, values, gates, norm_gain.reshape(heads, width), answer,
      in_hbm(states))

    sorted_replies = pl.pallas_call(
        functools.partial(reply_kernel, inner=inner, outer=outer, order=q2),
        out_shape=(single,) * outer,
        in_specs=[VMEM, ANY] + [VMEM] * inner, out_specs=(VMEM,) * outer,
        compiler_params=params(4), name="reply",
    )(wishes, partial, *replies)
    parts = [shift_outer(sorted_replies[k], k) for k in z2]

    output = jax.ShapeDtypeStruct((packed_rows, width), BF16)
    base, last = pl.pallas_call(
        functools.partial(local_kernel, slots=last_slots, count=count, chunks=chunks),
        out_shape=(pltpu.HBM(output.shape, output.dtype), late_rows),
        in_specs=[VMEM] * 3 + [ANY, HBM], out_specs=(VMEM, VMEM),
        scratch_shapes=[
            pltpu.VMEM((len(last_slots), heads, width, width), F32),
            pltpu.VMEM(products.shape, F32),
            pltpu.SemaphoreType.DMA((len(last_slots), chunks)),
        ],
        compiler_params=params(16), name="local",
    )(mixed, scale, lhs, sorted_replies[0], in_hbm(states))

    return unpack(pl.pallas_call(
        functools.partial(finish_kernel, count=count, heads=heads),
        out_shape=output, in_specs=[VMEM, HBM] + [VMEM] * (outer + 2), out_specs=HBM,
        scratch_shapes=[late_bf16, late_packed, pltpu.SemaphoreType.DMA((late,))],
        input_output_aliases={1: 0},
        compiler_params=params(4), name="finish",
    )(facts, in_hbm(base), last, partial, sorted_replies[0], *parts))


def solution(mesh):
    rows = P(("groups", "req"), None, None)
    in_specs = (rows, rows, rows, rows, P(("groups", "req"), None, None, None),
                P(("groups", "req")), P())
    return jax.shard_map(
        on_device, mesh=mesh, in_specs=in_specs, out_specs=rows, check_vma=False)
```

```python
import functools

import jax
import jax.numpy as jnp
from jax import lax
from jax.experimental import pallas as pl
from jax.experimental.pallas import tpu as pltpu
from jax.sharding import PartitionSpec as P

BEFORE = 3
EPS = 1e-06
F32 = jnp.float32
BF16 = jnp.bfloat16
MIB = 2**20
VMEM = pl.BlockSpec(memory_space=pltpu.VMEM)
SMEM = pl.BlockSpec(memory_space=pltpu.SMEM)
HBM = pl.BlockSpec(memory_space=pltpu.HBM)
ANY = pl.BlockSpec(memory_space=pl.ANY)


def silu(x):
    return x / (1.0 + jnp.exp(-x))


def sigmoid(x):
    return 1.0 / (1.0 + jnp.exp(-x))


def moving_slot(slots_ref, count):
    base = lax.axis_index("req") * count
    place = jnp.int32(0)
    moves = slots_ref[0] != base
    for s in range(1, count):
        here = slots_ref[s] != base + s
        place = jnp.where(here, s, place)
        moves = jnp.logical_or(moves, here)
    return place, moves


def wanted_device(slots_ref, count):
    device = lax.axis_index("req")
    result = device
    for s in range(count):
        owner = lax.div(slots_ref[s], jnp.int32(count))
        result = jnp.where(owner != device, owner, result)
    return result


OUTER, INNER, SLOT, FACTS = 0, 1, 2, 8


def wish_steps(inner):
    if inner & (inner - 1):
        return list(range(inner))
    steps, step = [0], 1
    while step < inner:
        steps, step = steps + [s ^ step for s in steps], step * 2
    return steps


def fact(ref, place, kind, rows):
    row = place * FACTS + kind
    return jnp.broadcast_to(ref[row:row + 1, :], (rows, ref.shape[1]))


def head_slope(heads, width):
    order = lax.broadcasted_iota(jnp.int32, (heads, width), 0).astype(F32)
    return jnp.exp2(-8.0 * (order + 1.0) / (2.0 * heads))


def decay_power(slope, power):
    return jnp.exp(slope * (-float(power)))


def split(x):
    high = x.astype(BF16)
    return high, (x - high.astype(F32)).astype(BF16)


def extract(packed, place, count):
    rows = packed.shape[0] // count
    result = packed[pl.ds(0, rows, stride=count), :]
    for s in range(1, count):
        result = jnp.where(place == s, packed[pl.ds(s, rows, stride=count), :], result)
    return result


def turn(position, step, size):
    return position ^ step if size & (size - 1) == 0 else (position + step) % size


def unturn(position, step, size):
    return position ^ step if size & (size - 1) == 0 else (position - step) % size


def shift(position, step, size):
    return lax.rem(position + step, size)


def inverse_step(step, size):
    return step if size & (size - 1) == 0 else (size - step) % size


def in_steps(refs, order):
    result = [refs[0]] * len(refs)
    for step, ref in zip(order, refs[1:]):
        result[step] = ref
    return result


def choose(options, index, sources):
    rows = index.shape[0]
    result = options[0][:rows, :]
    for option, source in zip(options[1:], sources[1:]):
        result = jnp.where(source == index, option[:rows, :], result)
    return result


def ask_kernel(new_slot_ref, queries_ref, out_ref, long_ref, facts_ref, slots_ref, rows_ref, wide,
               sems, *, count, inner):
    late = rows_ref.shape[0]
    first = queries_ref.shape[0] - late
    slots_copy = pltpu.make_async_copy(new_slot_ref, slots_ref, sems.at[0])
    slots_copy.start()
    copy = pltpu.make_async_copy(queries_ref.at[pl.ds(first, late)], rows_ref, sems.at[1])
    copy.start()
    slots_copy.wait()
    place, moves = moving_slot(slots_ref, count)
    wanted = wanted_device(slots_ref, count)
    kind = lax.broadcasted_iota(jnp.int32, facts_ref.shape, 0)
    facts = jnp.where(kind == INNER, lax.rem(wanted, inner), jnp.where(moves, place, count))
    facts_ref[...] = jnp.where(kind == OUTER, lax.div(wanted, inner), facts)
    copy.wait()
    wide[...] = rows_ref[...].astype(F32)
    rows = silu(extract(wide, place, count))
    out_ref[...] = rows
    long_ref[:rows.shape[0], :] = rows
    long_ref[rows.shape[0]:, :] = jnp.zeros_like(long_ref[rows.shape[0]:, :])


def pair_kernel(near_ref, far_ref, out_ref):
    rows = out_ref.shape[0] // 2
    out_ref[:rows, :] = near_ref[:rows, :]
    out_ref[rows:, :] = far_ref[:rows, :]


def prepare_kernel(slots_ref, queries_ref, keys_ref, values_ref, gates_ref, gain_ref, states_ref,
                   weight_ref, early_ref, rows_ref, gain_rows_ref, state, wide, sems, row_sems,
                   *, count, chunks):
    heads = states_ref.shape[1]
    size = heads // chunks
    place, _ = moving_slot(slots_ref, count)
    sources = (keys_ref, values_ref, queries_ref, gates_ref)
    copies = [
        pltpu.make_async_copy(ref, rows_ref.at[n], row_sems.at[n])
        for n, ref in enumerate(sources)]
    copies.append(pltpu.make_async_copy(gain_ref, gain_rows_ref, row_sems.at[len(sources)]))

    def load(c):
        part = pl.ds(c * size, size)
        return pltpu.make_async_copy(states_ref.at[place, part], state.at[part], sems.at[c])

    for copy in copies[:2]:
        copy.start()
    for c in range(chunks):
        load(c).start()
    for copy in copies[2:]:
        copy.start()
    for n, copy in enumerate(copies[:2]):
        copy.wait()
        wide[...] = rows_ref[n, :wide.shape[0], :].astype(F32)
        early_ref[n] = silu(extract(wide, place, count))
    for c in range(chunks):
        load(c).wait()
        for h in range(c * size, (c + 1) * size):
            weight_ref[h] = jnp.concatenate(split(state[h]), axis=0)
    for copy in copies[2:]:
        copy.wait()


def route_kernel(wishes_ref, *refs, inner, outer, order):
    column, outs = in_steps(refs[:outer], order), refs[outer:]
    my_outer = lax.div(lax.axis_index("req"), inner)
    for k in range(inner):
        back = wish_steps(inner).index(inverse_step(k, inner))
        wish = fact(wishes_ref, back, OUTER, outs[k].shape[0])
        outs[k][...] = choose(column, wish, [unturn(my_outer, k, outer) for k in range(outer)])


def answer_kernel(facts_ref, *refs, inner, late, heads, width, order):
    found, (weight_ref, early_ref, out_ref, lhs, prod) = refs[:inner], refs[inner:]
    found = in_steps(found, order)
    my_inner = lax.rem(lax.axis_index("req"), inner)
    block = lambda ref, t: ref[t * heads:(t + 1) * heads, :]
    sources = [unturn(my_inner, k, inner) for k in range(inner)]
    rows = choose(found, fact(facts_ref, 0, INNER, late * heads), sources)
    q = [rows[t * heads:(t + 1) * heads, :] for t in range(late)]
    slope = head_slope(heads, width)
    for t in range(late):
        x = q[t] * decay_power(slope, t + BEFORE + 1)
        high = x.astype(BF16).astype(F32)
        lhs[t * heads:(t + 1) * heads, :] = high
        lhs[(late + t) * heads:(late + t + 1) * heads, :] = x - high
    for h in range(heads):
        x = lhs[pl.ds(h, 2 * late, stride=heads), :].astype(BF16)
        prod[pl.ds(h, 2 * late, stride=heads), :] = jnp.dot(
            jnp.concatenate([x, x], axis=1), weight_ref[h], preferred_element_type=F32)
    for t in range(late):
        total = block(prod, t) + block(prod, late + t)
        for s in range(BEFORE):
            score = jnp.sum(q[t] * block(early_ref.at[0], s), axis=1, keepdims=True)
            total = total + score * decay_power(slope, t + BEFORE - s) * block(
                early_ref.at[1], s)
        out_ref[t * heads:(t + 1) * heads, :] = total


def reply_kernel(wishes_ref, after_ref, *refs, inner, outer, order):
    replies, outs = in_steps(refs[:inner], order), refs[inner:]
    me = lax.axis_index("req")
    my_inner, my_outer = lax.rem(me, inner), lax.div(me, inner)
    rows = outs[0].shape[0]
    owner = [
        jnp.where(fact(wishes_ref, n, INNER, rows) == my_inner,
                  fact(wishes_ref, n, OUTER, rows), -1)
        for n in map(wish_steps(inner).index, range(inner))]
    for k in range(outer):
        result = 0.0
        for n in range(inner):
            result = jnp.where(owner[n] == shift(my_outer, k, outer), replies[n][...], result)
        outs[k][...] = result


def load_states(states_ref, state, sems, slots, chunks):
    size = states_ref.shape[1] // chunks

    def load(n, c):
        part = pl.ds(c * size, size)
        return pltpu.make_async_copy(
            states_ref.at[slots[n], part], state.at[n, part], sems.at[n, c])

    for n in range(len(slots)):
        for c in range(chunks):
            load(n, c).start()
    return load


def times_states(load, state, lhs, prod, slots, count, chunks):
    heads = state.shape[1]
    size = heads // chunks
    for n, slot in enumerate(slots):
        for c in range(chunks):
            load(n, c).wait()
            for h in range(c * size, (c + 1) * size):
                rows = pl.ds(h * count + slot, 16, stride=heads * count)
                x = lhs[rows, :].astype(BF16)
                prod[rows, :] = jnp.dot(
                    jnp.concatenate([x, x], axis=1),
                    jnp.concatenate(split(state[n, h]), axis=0),
                    preferred_element_type=F32)


def row_slot(span, count):
    return lax.rem(lax.broadcasted_iota(jnp.int32, (span, 1), 0), jnp.int32(count))


def block(ref, t, rows):
    return ref[t * rows:(t + 1) * rows, :]


def scores_kernel(facts_ref, rows_ref, gain_ref, after_ref, states_ref, mixed_ref, scale_ref, late_ref, lhs, state, prod, wide, sems,
                  *, slots, count, chunks):
    heads, width = states_ref.shape[1], states_ref.shape[2]
    span = heads * count
    keys_ref, values_ref, queries_ref, gates_ref = [rows_ref.at[n] for n in range(4)]
    steps = rows_ref.shape[1] // span
    late = steps - BEFORE
    place = fact(facts_ref, 0, SLOT, late * heads)
    load = load_states(states_ref, state, sems, slots, chunks)

    def spread(x):
        for s in range(count):
            wide[pl.ds(s, heads, stride=count), :] = x
        return wide[:span, :]

    slope = spread(head_slope(heads, width))
    gain = spread(gain_ref[...])
    decay = [decay_power(slope, p) for p in range(steps + 1)]
    q = [silu(block(queries_ref, t, span).astype(F32)) for t in range(steps)]
    k = [silu(block(keys_ref, t, span).astype(F32)) for t in range(steps)]
    v = [silu(block(values_ref, t, span).astype(F32)) for t in range(steps)]
    for t in range(steps):
        x = q[t] * decay[t + 1]
        high = x.astype(BF16).astype(F32)
        lhs[t * span:(t + 1) * span, :] = high
        lhs[(8 + t) * span:(9 + t) * span, :] = x - high
    for t in range(steps):
        total = None
        far = None
        for s in range(t + 1):
            score = jnp.sum(q[t] * k[s], axis=1, keepdims=True)
            term = score * decay[t - s] * v[s]
            if t >= BEFORE and s < BEFORE:
                far = term if far is None else far + term
            else:
                total = term if total is None else total + term
        if t >= BEFORE:
            wide[(t - BEFORE) * span:(t - BEFORE + 1) * span, :] = total
        mixed_ref[t * span:(t + 1) * span, :] = total if far is None else total + far
    late_ref[0] = extract(wide, place, count)
    for t in range(steps):
        scale = gain * sigmoid(block(gates_ref, t, span).astype(F32))
        scale_ref[t * span:(t + 1) * span, :] = scale
        if t >= BEFORE:
            wide[(t - BEFORE) * span:(t - BEFORE + 1) * span, :] = scale
    late_ref[1] = extract(wide, place, count)
    times_states(load, state, lhs, prod, slots, count, chunks)
    slot = row_slot(span, count)
    for t in range(steps):
        x = block(prod, t, span) + block(prod, 8 + t, span)
        for s in slots:
            rows = slice(t * span, (t + 1) * span)
            mixed_ref[rows, :] = mixed_ref[rows, :] + jnp.where(slot == s, x, 0.0)


def local_kernel(mixed_ref, scale_ref, lhs, after_ref, states_ref, out_ref, last_ref, state, prod,
                 sems, *, slots, count, chunks):
    heads, width = states_ref.shape[1], states_ref.shape[2]
    span = heads * count
    steps = mixed_ref.shape[0] // span
    load = load_states(states_ref, state, sems, slots, chunks)
    times_states(load, state, lhs, prod, slots, count, chunks)
    slot = row_slot(span, count)
    for t in range(steps):
        x = block(mixed_ref, t, span)
        for s in slots:
            x = x + jnp.where(slot == s, block(prod, t, span) + block(prod, 8 + t, span), 0.0)
        sums = jnp.sum(x * x, axis=1, keepdims=True)
        energy = jnp.zeros((span, 1), F32)
        for s in range(count):
            whole = jnp.sum(jnp.where(slot == s, sums, 0.0), axis=0, keepdims=True)
            energy = jnp.where(slot == s, whole, energy)
        factor = lax.rsqrt(energy * (1.0 / (heads * width)) + EPS)
        y = (x * factor * block(scale_ref, t, span)).astype(BF16)
        out_ref[t * span:(t + 1) * span, :] = y
        if t >= BEFORE:
            last_ref[(t - BEFORE) * span:(t - BEFORE + 1) * span, :] = y


def finish_kernel(facts_ref, base_ref, last_ref, late_ref, *refs, count, heads):
    parts, (out_ref, rows_ref, wide, sems) = refs[:-4], refs[-4:]
    place = fact(facts_ref, 0, SLOT, heads)
    span = heads * count
    steps = late_ref.shape[1] // heads
    first = out_ref.shape[0] - steps * span
    copies = []
    for t in range(steps):
        part = slice(t * heads, (t + 1) * heads)
        x = late_ref[0, part, :]
        for ref in parts:
            x = x + ref[part, :]
        energy = jnp.sum(jnp.sum(x * x, axis=0, keepdims=True), axis=1, keepdims=True)
        y = x * lax.rsqrt(energy * (1.0 / x.size) + EPS) * late_ref[1, part, :]
        rows = slice(t * span, (t + 1) * span)
        wide[rows, :] = last_ref[rows, :].astype(F32)
        for s in range(count):
            here = pl.ds(t * span + s, heads, stride=count)
            wide[here, :] = jnp.where(place == s, y, wide[here, :])
        rows_ref[rows, :] = wide[rows, :].astype(BF16)
        copies.append(pltpu.make_async_copy(
            rows_ref.at[pl.ds(t * span, span)], out_ref.at[pl.ds(first + t * span, span)],
            sems.at[t]))
        copies[t].start()
    for copy in copies:
        copy.wait()


def in_hbm(x):
    return pltpu.with_memory_space_constraint(x, pltpu.HBM)


def near_square(total):
    return next(
        (d, total // d) for d in range(1, total + 1) if total % d == 0 and d * d >= total)


def on_device(queries, keys, values, gates, states, new_slot, norm_gain):
    count, steps, features = queries.shape
    heads, width = states.shape[1], states.shape[2]
    late = steps - BEFORE
    packed_rows, single_rows = steps * heads * count, late * heads
    inner, outer = near_square(lax.axis_size("req"))

    def pack(x):
        return x.reshape(count, steps, heads, width).transpose(1, 2, 0, 3).reshape(
            packed_rows, width)

    def unpack(x):
        return x.reshape(steps, heads, count, width).transpose(2, 0, 1, 3).reshape(
            count, steps, features)

    def send_inner(x, k):
        return lax.ppermute(x, "req", [
            (o * inner + i, o * inner + int(turn(i, k, inner)))
            for o in range(outer) for i in range(inner)])

    def send_outer(x, k):
        return lax.ppermute(x, "req", [
            (o * inner + i, int(turn(o, k, outer)) * inner + i)
            for o in range(outer) for i in range(inner)])

    def gather_inner(x):
        if inner & (inner - 1):
            x = x[:FACTS]
            return jnp.concatenate([x] + [send_inner(x, k) for k in range(1, inner)])
        step, result = 1, x
        while step < inner:
            result = pl.pallas_call(
                pair_kernel,
                out_shape=jax.ShapeDtypeStruct((2 * step * FACTS, width), jnp.int32),
                in_specs=[VMEM, VMEM], out_specs=VMEM, compiler_params=params(4), name="pair",
            )(result, send_inner(result, step))
            step *= 2
        return result

    def shift_outer(x, k):
        return lax.ppermute(x, "req", [
            (o * inner + i, (o + k) % outer * inner + i)
            for o in range(outer) for i in range(inner)])

    def params(limit):
        return pltpu.CompilerParams(vmem_limit_bytes=limit * MIB)

    queries, keys, values, gates = pack(queries), pack(keys), pack(values), pack(gates)
    single = jax.ShapeDtypeStruct((single_rows, width), F32)
    late_packed = pltpu.VMEM((late * heads * count, width), F32)

    late_rows = jax.ShapeDtypeStruct((late * heads * count, width), BF16)
    late_bf16 = pltpu.VMEM(late_rows.shape, BF16)

    long = jax.ShapeDtypeStruct((single_rows + FACTS, width), F32)
    facts_rows = max(single_rows * 5 // (6 * FACTS), 1) * FACTS
    ask, ask_long, facts = pl.pallas_call(
        functools.partial(ask_kernel, count=count, inner=inner),
        out_shape=(single, long, jax.ShapeDtypeStruct((facts_rows, width), jnp.int32)),
        in_specs=[HBM, HBM], out_specs=(VMEM, VMEM, VMEM),
        scratch_shapes=[pltpu.SMEM((count,), jnp.int32), late_bf16, late_packed,
                        pltpu.SemaphoreType.DMA((2,))],
        compiler_params=params(4), name="ask",
    )(in_hbm(new_slot), in_hbm(queries))

    z1, z2 = list(range(1, outer)), list(range(1, outer))
    q1, q2 = list(range(inner - 1, 0, -1)), list(range(1, inner))
    column = [ask] + [send_outer(ask_long if k == outer - 1 else ask, k) for k in z1]
    wishes = gather_inner(facts)

    chunks = 8
    gain = norm_gain.reshape(heads, width)
    weight, early, rows, gain_rows = pl.pallas_call(
        functools.partial(prepare_kernel, count=count, chunks=chunks),
        out_shape=(jax.ShapeDtypeStruct((heads, 2 * width, width), BF16),
                   jax.ShapeDtypeStruct((2, BEFORE * heads, width), F32),
                   jax.ShapeDtypeStruct((4, packed_rows, width), BF16),
                   jax.ShapeDtypeStruct(gain.shape, F32)),
        in_specs=[SMEM] + [HBM] * 6, out_specs=(VMEM,) * 4,
        scratch_shapes=[pltpu.VMEM((heads, width, width), F32),
                        pltpu.VMEM((BEFORE * heads * count, width), F32),
                        pltpu.SemaphoreType.DMA((chunks,)),
                        pltpu.SemaphoreType.DMA((5,))],
        compiler_params=params(12), name="prepare",
    )(*map(in_hbm, (new_slot, queries, keys, values, gates, gain, states)))

    asked = pl.pallas_call(
        functools.partial(route_kernel, inner=inner, outer=outer, order=z1),
        out_shape=(single,) * inner,
        in_specs=[VMEM] * (1 + outer), out_specs=(VMEM,) * inner,
        compiler_params=params(4), name="route",
    )(wishes, *column)
    found = [asked[0]] + [send_inner(asked[k], k) for k in q1]

    answer = pl.pallas_call(
        functools.partial(answer_kernel, inner=inner, late=late, heads=heads, width=width,
                          order=q1),
        out_shape=single, in_specs=[VMEM] * (inner + 3), out_specs=VMEM,
        scratch_shapes=[pltpu.VMEM((2 * late * heads, width), F32)] * 2,
        compiler_params=params(8), name="answer",
    )(facts, *found, weight, early)
    replies = [answer] + [send_inner(answer, k) for k in q2]

    chunks = 4
    first_slots, last_slots = list(range(count // 2)), list(range(count // 2, count))
    packed = jax.ShapeDtypeStruct((packed_rows, width), F32)
    products = jax.ShapeDtypeStruct((16 * heads * count, width), F32)
    mixed, scale, partial, lhs = pl.pallas_call(
        functools.partial(scores_kernel, slots=first_slots, count=count, chunks=chunks),
        out_shape=(packed, packed, jax.ShapeDtypeStruct((2, single_rows, width), F32), products),
        in_specs=[VMEM] * 3 + [ANY, HBM], out_specs=(VMEM,) * 4,
        scratch_shapes=[
            pltpu.VMEM((max(len(first_slots), 1), heads, width, width), F32),
            pltpu.VMEM(products.shape, F32),
            late_packed,
            pltpu.SemaphoreType.DMA((max(len(first_slots), 1), chunks)),
        ],
        compiler_params=params(16), name="scores",
    )(facts, rows, gain_rows, answer, in_hbm(states))

    sorted_replies = pl.pallas_call(
        functools.partial(reply_kernel, inner=inner, outer=outer, order=q2),
        out_shape=(single,) * outer,
        in_specs=[VMEM, ANY] + [VMEM] * inner, out_specs=(VMEM,) * outer,
        compiler_params=params(4), name="reply",
    )(wishes, partial, *replies)
    parts = [shift_outer(sorted_replies[k], k) for k in z2]

    output = jax.ShapeDtypeStruct((packed_rows, width), BF16)
    base, last = pl.pallas_call(
        functools.partial(local_kernel, slots=last_slots, count=count, chunks=chunks),
        out_shape=(pltpu.HBM(output.shape, output.dtype), late_rows),
        in_specs=[VMEM] * 3 + [ANY, HBM], out_specs=(VMEM, VMEM),
        scratch_shapes=[
            pltpu.VMEM((len(last_slots), heads, width, width), F32),
            pltpu.VMEM(products.shape, F32),
            pltpu.SemaphoreType.DMA((len(last_slots), chunks)),
        ],
        compiler_params=params(16), name="local",
    )(mixed, scale, lhs, sorted_replies[0], in_hbm(states))

    return unpack(pl.pallas_call(
        functools.partial(finish_kernel, count=count, heads=heads),
        out_shape=output, in_specs=[VMEM, HBM] + [VMEM] * (outer + 2), out_specs=HBM,
        scratch_shapes=[late_bf16, late_packed, pltpu.SemaphoreType.DMA((late,))],
        input_output_aliases={1: 0},
        compiler_params=params(4), name="finish",
    )(facts, in_hbm(base), last, partial, sorted_replies[0], *parts))


def solution(mesh):
    rows = P(("groups", "req"), None, None)
    in_specs = (rows, rows, rows, rows, P(("groups", "req"), None, None, None),
                P(("groups", "req")), P())
    return jax.shard_map(
        on_device, mesh=mesh, in_specs=in_specs, out_specs=rows, check_vma=False)
```

```python
import functools

import jax
import jax.numpy as jnp
from jax import lax
from jax.experimental import pallas as pl
from jax.experimental.pallas import tpu as pltpu
from jax.sharding import PartitionSpec as P

BEFORE = 3
EPS = 1e-06
F32 = jnp.float32
BF16 = jnp.bfloat16
MIB = 2**20
VMEM = pl.BlockSpec(memory_space=pltpu.VMEM)
SMEM = pl.BlockSpec(memory_space=pltpu.SMEM)
HBM = pl.BlockSpec(memory_space=pltpu.HBM)
ANY = pl.BlockSpec(memory_space=pl.ANY)


def silu(x):
    return x / (1.0 + jnp.exp(-x))


def sigmoid(x):
    return 1.0 / (1.0 + jnp.exp(-x))


def moving_slot(slots_ref, count):
    base = lax.axis_index("req") * count
    place = jnp.int32(0)
    moves = slots_ref[0] != base
    for s in range(1, count):
        here = slots_ref[s] != base + s
        place = jnp.where(here, s, place)
        moves = jnp.logical_or(moves, here)
    return place, moves


def wanted_device(slots_ref, count):
    device = lax.axis_index("req")
    result = device
    for s in range(count):
        owner = lax.div(slots_ref[s], jnp.int32(count))
        result = jnp.where(owner != device, owner, result)
    return result


OUTER, INNER, SLOT, FACTS = 0, 1, 2, 8


def wish_steps(inner):
    if inner & (inner - 1):
        return list(range(inner))
    steps, step = [0], 1
    while step < inner:
        steps, step = steps + [s ^ step for s in steps], step * 2
    return steps


def fact(ref, place, kind, rows):
    row = place * FACTS + kind
    return jnp.broadcast_to(ref[row:row + 1, :], (rows, ref.shape[1]))


def head_slope(heads, width):
    order = lax.broadcasted_iota(jnp.int32, (heads, width), 0).astype(F32)
    return jnp.exp2(-8.0 * (order + 1.0) / (2.0 * heads))


def decay_power(slope, power):
    return jnp.exp(slope * (-float(power)))


def split(x):
    high = x.astype(BF16)
    return high, (x - high.astype(F32)).astype(BF16)


def extract(packed, place, count):
    rows = packed.shape[0] // count
    result = packed[pl.ds(0, rows, stride=count), :]
    for s in range(1, count):
        result = jnp.where(place == s, packed[pl.ds(s, rows, stride=count), :], result)
    return result


def turn(position, step, size):
    return position ^ step if size & (size - 1) == 0 else (position + step) % size


def unturn(position, step, size):
    return position ^ step if size & (size - 1) == 0 else (position - step) % size


def shift(position, step, size):
    return lax.rem(position + step, size)


def inverse_step(step, size):
    return step if size & (size - 1) == 0 else (size - step) % size


def in_steps(refs, order):
    result = [refs[0]] * len(refs)
    for step, ref in zip(order, refs[1:]):
        result[step] = ref
    return result


def choose(options, index, sources):
    rows = index.shape[0]
    result = options[0][:rows, :]
    for option, source in zip(options[1:], sources[1:]):
        result = jnp.where(source == index, option[:rows, :], result)
    return result


def ask_kernel(new_slot_ref, queries_ref, out_ref, long_ref, facts_ref, slots_ref, rows_ref, wide,
               sems, *, count, inner):
    late = rows_ref.shape[0]
    first = queries_ref.shape[0] - late
    slots_copy = pltpu.make_async_copy(new_slot_ref, slots_ref, sems.at[0])
    slots_copy.start()
    copy = pltpu.make_async_copy(queries_ref.at[pl.ds(first, late)], rows_ref, sems.at[1])
    copy.start()
    slots_copy.wait()
    place, moves = moving_slot(slots_ref, count)
    wanted = wanted_device(slots_ref, count)
    kind = lax.broadcasted_iota(jnp.int32, facts_ref.shape, 0)
    facts = jnp.where(kind == INNER, lax.rem(wanted, inner), jnp.where(moves, place, count))
    facts_ref[...] = jnp.where(kind == OUTER, lax.div(wanted, inner), facts)
    copy.wait()
    wide[...] = rows_ref[...].astype(F32)
    rows = silu(extract(wide, place, count))
    out_ref[...] = rows
    long_ref[:rows.shape[0], :] = rows
    long_ref[rows.shape[0]:, :] = jnp.zeros_like(long_ref[rows.shape[0]:, :])


def pair_kernel(near_ref, far_ref, out_ref):
    rows = out_ref.shape[0] // 2
    out_ref[:rows, :] = near_ref[:rows, :]
    out_ref[rows:, :] = far_ref[:rows, :]


def prepare_kernel(slots_ref, queries_ref, keys_ref, values_ref, gates_ref, gain_ref, states_ref,
                   weight_ref, early_ref, rows_ref, gain_rows_ref, state, wide, sems, row_sems,
                   *, count, chunks):
    heads = states_ref.shape[1]
    size = heads // chunks
    place, _ = moving_slot(slots_ref, count)
    sources = (keys_ref, values_ref, queries_ref, gates_ref)
    copies = [
        pltpu.make_async_copy(ref, rows_ref.at[n], row_sems.at[n])
        for n, ref in enumerate(sources)]
    copies.append(pltpu.make_async_copy(gain_ref, gain_rows_ref, row_sems.at[len(sources)]))

    def load(c):
        part = pl.ds(c * size, size)
        return pltpu.make_async_copy(states_ref.at[place, part], state.at[part], sems.at[c])

    for copy in copies[:2]:
        copy.start()
    for c in range(chunks):
        load(c).start()
    for copy in copies[2:]:
        copy.start()
    for n, copy in enumerate(copies[:2]):
        copy.wait()
        wide[...] = rows_ref[n, :wide.shape[0], :].astype(F32)
        early_ref[n] = silu(extract(wide, place, count))
    for c in range(chunks):
        load(c).wait()
        for h in range(c * size, (c + 1) * size):
            group, n = divmod(h, weight_ref.shape[2] // state.shape[2])
            lanes = slice(n * state.shape[2], (n + 1) * state.shape[2])
            weight_ref[group, :, lanes] = jnp.concatenate(split(state[h]), axis=0)
    for copy in copies[2:]:
        copy.wait()


def route_kernel(wishes_ref, *refs, inner, outer, order):
    column, outs = in_steps(refs[:outer], order), refs[outer:]
    my_outer = lax.div(lax.axis_index("req"), inner)
    for k in range(inner):
        back = wish_steps(inner).index(inverse_step(k, inner))
        wish = fact(wishes_ref, back, OUTER, outs[k].shape[0])
        outs[k][...] = choose(column, wish, [unturn(my_outer, k, outer) for k in range(outer)])


def answer_kernel(facts_ref, *refs, inner, late, heads, width, order):
    found, (weight_ref, early_ref, out_ref, lhs, prod) = refs[:inner], refs[inner:]
    found = in_steps(found, order)
    my_inner = lax.rem(lax.axis_index("req"), inner)
    block = lambda ref, t: ref[t * heads:(t + 1) * heads, :]
    sources = [unturn(my_inner, k, inner) for k in range(inner)]
    rows = choose(found, fact(facts_ref, 0, INNER, late * heads), sources)
    q = [rows[t * heads:(t + 1) * heads, :] for t in range(late)]
    slope = head_slope(heads, width)
    for t in range(late):
        x = q[t] * decay_power(slope, t + BEFORE + 1)
        high = x.astype(BF16).astype(F32)
        lhs[t * heads:(t + 1) * heads, :] = high
        lhs[(late + t) * heads:(late + t + 1) * heads, :] = x - high
    depth = lhs.shape[0] // heads
    joint = weight_ref.shape[2] // width
    for group in range(heads // joint):
        rows = [pl.ds(group * joint + n, depth, stride=heads) for n in range(joint)]
        x = jnp.concatenate([lhs[r, :] for r in rows], axis=0).astype(BF16)
        result = jnp.dot(
            jnp.concatenate([x, x], axis=1), weight_ref[group], preferred_element_type=F32)
        for n in range(joint):
            prod[rows[n], :] = result[n * depth:(n + 1) * depth, n * width:(n + 1) * width]
    for t in range(late):
        total = block(prod, t) + block(prod, late + t)
        for s in range(BEFORE):
            score = jnp.sum(q[t] * block(early_ref.at[0], s), axis=1, keepdims=True)
            total = total + score * decay_power(slope, t + BEFORE - s) * block(
                early_ref.at[1], s)
        out_ref[t * heads:(t + 1) * heads, :] = total


def reply_kernel(wishes_ref, after_ref, *refs, inner, outer, order):
    replies, outs = in_steps(refs[:inner], order), refs[inner:]
    me = lax.axis_index("req")
    my_inner, my_outer = lax.rem(me, inner), lax.div(me, inner)
    rows = outs[0].shape[0]
    owner = [
        jnp.where(fact(wishes_ref, n, INNER, rows) == my_inner,
                  fact(wishes_ref, n, OUTER, rows), -1)
        for n in map(wish_steps(inner).index, range(inner))]
    for k in range(outer):
        result = 0.0
        for n in range(inner):
            result = jnp.where(owner[n] == shift(my_outer, k, outer), replies[n][...], result)
        outs[k][...] = result


def load_states(states_ref, state, sems, slots, chunks):
    size = states_ref.shape[1] // chunks

    def load(n, c):
        part = pl.ds(c * size, size)
        return pltpu.make_async_copy(
            states_ref.at[slots[n], part], state.at[n, part], sems.at[n, c])

    for n in range(len(slots)):
        for c in range(chunks):
            load(n, c).start()
    return load


def times_states(load, state, lhs, prod, slots, count, chunks):
    heads = state.shape[1]
    size = heads // chunks
    for n, slot in enumerate(slots):
        for c in range(chunks):
            load(n, c).wait()
            for h in range(c * size, (c + 1) * size):
                rows = pl.ds(h * count + slot, 16, stride=heads * count)
                x = lhs[rows, :].astype(BF16)
                prod[rows, :] = jnp.dot(
                    jnp.concatenate([x, x], axis=1),
                    jnp.concatenate(split(state[n, h]), axis=0),
                    preferred_element_type=F32)


def row_slot(span, count):
    return lax.rem(lax.broadcasted_iota(jnp.int32, (span, 1), 0), jnp.int32(count))


def block(ref, t, rows):
    return ref[t * rows:(t + 1) * rows, :]


def scores_kernel(facts_ref, rows_ref, gain_ref, after_ref, states_ref, mixed_ref, scale_ref, late_ref, lhs, state, prod, wide, sems,
                  *, slots, count, chunks):
    heads, width = states_ref.shape[1], states_ref.shape[2]
    span = heads * count
    keys_ref, values_ref, queries_ref, gates_ref = [rows_ref.at[n] for n in range(4)]
    steps = rows_ref.shape[1] // span
    late = steps - BEFORE
    place = fact(facts_ref, 0, SLOT, late * heads)
    load = load_states(states_ref, state, sems, slots, chunks)

    def spread(x):
        for s in range(count):
            wide[pl.ds(s, heads, stride=count), :] = x
        return wide[:span, :]

    slope = spread(head_slope(heads, width))
    gain = spread(gain_ref[...])
    decay = [decay_power(slope, p) for p in range(steps + 1)]
    q = [silu(block(queries_ref, t, span).astype(F32)) for t in range(steps)]
    k = [silu(block(keys_ref, t, span).astype(F32)) for t in range(steps)]
    v = [silu(block(values_ref, t, span).astype(F32)) for t in range(steps)]
    for t in range(steps):
        x = q[t] * decay[t + 1]
        high = x.astype(BF16).astype(F32)
        lhs[t * span:(t + 1) * span, :] = high
        lhs[(8 + t) * span:(9 + t) * span, :] = x - high
    for t in range(steps):
        total = None
        far = None
        for s in range(t + 1):
            score = jnp.sum(q[t] * k[s], axis=1, keepdims=True)
            term = score * decay[t - s] * v[s]
            if t >= BEFORE and s < BEFORE:
                far = term if far is None else far + term
            else:
                total = term if total is None else total + term
        if t >= BEFORE:
            wide[(t - BEFORE) * span:(t - BEFORE + 1) * span, :] = total
        mixed_ref[t * span:(t + 1) * span, :] = total if far is None else total + far
    late_ref[0] = extract(wide, place, count)
    for t in range(steps):
        scale = gain * sigmoid(block(gates_ref, t, span).astype(F32))
        scale_ref[t * span:(t + 1) * span, :] = scale
        if t >= BEFORE:
            wide[(t - BEFORE) * span:(t - BEFORE + 1) * span, :] = scale
    late_ref[1] = extract(wide, place, count)
    times_states(load, state, lhs, prod, slots, count, chunks)
    slot = row_slot(span, count)
    for t in range(steps):
        x = block(prod, t, span) + block(prod, 8 + t, span)
        for s in slots:
            rows = slice(t * span, (t + 1) * span)
            mixed_ref[rows, :] = mixed_ref[rows, :] + jnp.where(slot == s, x, 0.0)


def local_kernel(mixed_ref, scale_ref, lhs, after_ref, states_ref, out_ref, last_ref, state, prod,
                 sems, *, slots, count, chunks):
    heads, width = states_ref.shape[1], states_ref.shape[2]
    span = heads * count
    steps = mixed_ref.shape[0] // span
    load = load_states(states_ref, state, sems, slots, chunks)
    times_states(load, state, lhs, prod, slots, count, chunks)
    slot = row_slot(span, count)
    for t in range(steps):
        x = block(mixed_ref, t, span)
        for s in slots:
            x = x + jnp.where(slot == s, block(prod, t, span) + block(prod, 8 + t, span), 0.0)
        sums = jnp.sum(x * x, axis=1, keepdims=True)
        energy = jnp.zeros((span, 1), F32)
        for s in range(count):
            whole = jnp.sum(jnp.where(slot == s, sums, 0.0), axis=0, keepdims=True)
            energy = jnp.where(slot == s, whole, energy)
        factor = lax.rsqrt(energy * (1.0 / (heads * width)) + EPS)
        y = (x * factor * block(scale_ref, t, span)).astype(BF16)
        out_ref[t * span:(t + 1) * span, :] = y
        if t >= BEFORE:
            last_ref[(t - BEFORE) * span:(t - BEFORE + 1) * span, :] = y


def finish_kernel(facts_ref, base_ref, last_ref, late_ref, *refs, count, heads):
    parts, (out_ref, rows_ref, wide, sems) = refs[:-4], refs[-4:]
    place = fact(facts_ref, 0, SLOT, heads)
    span = heads * count
    steps = late_ref.shape[1] // heads
    first = out_ref.shape[0] - steps * span
    copies = []
    for t in range(steps):
        part = slice(t * heads, (t + 1) * heads)
        x = late_ref[0, part, :]
        for ref in parts:
            x = x + ref[part, :]
        energy = jnp.sum(jnp.sum(x * x, axis=0, keepdims=True), axis=1, keepdims=True)
        y = x * lax.rsqrt(energy * (1.0 / x.size) + EPS) * late_ref[1, part, :]
        rows = slice(t * span, (t + 1) * span)
        wide[rows, :] = last_ref[rows, :].astype(F32)
        for s in range(count):
            here = pl.ds(t * span + s, heads, stride=count)
            wide[here, :] = jnp.where(place == s, y, wide[here, :])
        rows_ref[rows, :] = wide[rows, :].astype(BF16)
        copies.append(pltpu.make_async_copy(
            rows_ref.at[pl.ds(t * span, span)], out_ref.at[pl.ds(first + t * span, span)],
            sems.at[t]))
        copies[t].start()
    for copy in copies:
        copy.wait()


def in_hbm(x):
    return pltpu.with_memory_space_constraint(x, pltpu.HBM)


def near_square(total):
    return next(
        (d, total // d) for d in range(1, total + 1) if total % d == 0 and d * d >= total)


def on_device(queries, keys, values, gates, states, new_slot, norm_gain):
    count, steps, features = queries.shape
    heads, width = states.shape[1], states.shape[2]
    late = steps - BEFORE
    packed_rows, single_rows = steps * heads * count, late * heads
    inner, outer = near_square(lax.axis_size("req"))

    def pack(x):
        return x.reshape(count, steps, heads, width).transpose(1, 2, 0, 3).reshape(
            packed_rows, width)

    def unpack(x):
        return x.reshape(steps, heads, count, width).transpose(2, 0, 1, 3).reshape(
            count, steps, features)

    def send_inner(x, k):
        return lax.ppermute(x, "req", [
            (o * inner + i, o * inner + int(turn(i, k, inner)))
            for o in range(outer) for i in range(inner)])

    def send_outer(x, k):
        return lax.ppermute(x, "req", [
            (o * inner + i, int(turn(o, k, outer)) * inner + i)
            for o in range(outer) for i in range(inner)])

    def gather_inner(x):
        if inner & (inner - 1):
            x = x[:FACTS]
            return jnp.concatenate([x] + [send_inner(x, k) for k in range(1, inner)])
        step, result = 1, x
        while step < inner:
            result = pl.pallas_call(
                pair_kernel,
                out_shape=jax.ShapeDtypeStruct((2 * step * FACTS, width), jnp.int32),
                in_specs=[VMEM, VMEM], out_specs=VMEM, compiler_params=params(4), name="pair",
            )(result, send_inner(result, step))
            step *= 2
        return result

    def shift_outer(x, k):
        return lax.ppermute(x, "req", [
            (o * inner + i, (o + k) % outer * inner + i)
            for o in range(outer) for i in range(inner)])

    def params(limit):
        return pltpu.CompilerParams(vmem_limit_bytes=limit * MIB)

    queries, keys, values, gates = pack(queries), pack(keys), pack(values), pack(gates)
    single = jax.ShapeDtypeStruct((single_rows, width), F32)
    late_packed = pltpu.VMEM((late * heads * count, width), F32)

    late_rows = jax.ShapeDtypeStruct((late * heads * count, width), BF16)
    late_bf16 = pltpu.VMEM(late_rows.shape, BF16)

    long = jax.ShapeDtypeStruct((single_rows + FACTS, width), F32)
    facts_rows = max(single_rows * 5 // (6 * FACTS), 1) * FACTS
    ask, ask_long, facts = pl.pallas_call(
        functools.partial(ask_kernel, count=count, inner=inner),
        out_shape=(single, long, jax.ShapeDtypeStruct((facts_rows, width), jnp.int32)),
        in_specs=[HBM, HBM], out_specs=(VMEM, VMEM, VMEM),
        scratch_shapes=[pltpu.SMEM((count,), jnp.int32), late_bf16, late_packed,
                        pltpu.SemaphoreType.DMA((2,))],
        compiler_params=params(4), name="ask",
    )(in_hbm(new_slot), in_hbm(queries))

    z1, z2 = list(range(1, outer)), list(range(1, outer))
    q1, q2 = list(range(inner - 1, 0, -1)), list(range(1, inner))
    column = [ask] + [send_outer(ask_long if k == outer - 1 else ask, k) for k in z1]
    wishes = gather_inner(facts)

    chunks = 8
    joint = 2 - heads % 2
    gain = norm_gain.reshape(heads, width)
    weight, early, rows, gain_rows = pl.pallas_call(
        functools.partial(prepare_kernel, count=count, chunks=chunks),
        out_shape=(jax.ShapeDtypeStruct((heads // joint, 2 * width, joint * width), BF16),
                   jax.ShapeDtypeStruct((2, BEFORE * heads, width), F32),
                   jax.ShapeDtypeStruct((4, packed_rows, width), BF16),
                   jax.ShapeDtypeStruct(gain.shape, F32)),
        in_specs=[SMEM] + [HBM] * 6, out_specs=(VMEM,) * 4,
        scratch_shapes=[pltpu.VMEM((heads, width, width), F32),
                        pltpu.VMEM((BEFORE * heads * count, width), F32),
                        pltpu.SemaphoreType.DMA((chunks,)),
                        pltpu.SemaphoreType.DMA((5,))],
        compiler_params=params(12), name="prepare",
    )(*map(in_hbm, (new_slot, queries, keys, values, gates, gain, states)))

    asked = pl.pallas_call(
        functools.partial(route_kernel, inner=inner, outer=outer, order=z1),
        out_shape=(single,) * inner,
        in_specs=[VMEM] * (1 + outer), out_specs=(VMEM,) * inner,
        compiler_params=params(4), name="route",
    )(wishes, *column)
    found = [asked[0]] + [send_inner(asked[k], k) for k in q1]

    answer = pl.pallas_call(
        functools.partial(answer_kernel, inner=inner, late=late, heads=heads, width=width,
                          order=q1),
        out_shape=single, in_specs=[VMEM] * (inner + 3), out_specs=VMEM,
        scratch_shapes=[pltpu.VMEM((-(-2 * late // 8) * 8 * heads, width), F32)] * 2,
        compiler_params=params(8), name="answer",
    )(facts, *found, weight, early)
    replies = [answer] + [send_inner(answer, k) for k in q2]

    chunks = 4
    first_slots, last_slots = list(range(count // 2)), list(range(count // 2, count))
    packed = jax.ShapeDtypeStruct((packed_rows, width), F32)
    products = jax.ShapeDtypeStruct((16 * heads * count, width), F32)
    mixed, scale, partial, lhs = pl.pallas_call(
        functools.partial(scores_kernel, slots=first_slots, count=count, chunks=chunks),
        out_shape=(packed, packed, jax.ShapeDtypeStruct((2, single_rows, width), F32), products),
        in_specs=[VMEM] * 3 + [ANY, HBM], out_specs=(VMEM,) * 4,
        scratch_shapes=[
            pltpu.VMEM((max(len(first_slots), 1), heads, width, width), F32),
            pltpu.VMEM(products.shape, F32),
            late_packed,
            pltpu.SemaphoreType.DMA((max(len(first_slots), 1), chunks)),
        ],
        compiler_params=params(16), name="scores",
    )(facts, rows, gain_rows, answer, in_hbm(states))

    sorted_replies = pl.pallas_call(
        functools.partial(reply_kernel, inner=inner, outer=outer, order=q2),
        out_shape=(single,) * outer,
        in_specs=[VMEM, ANY] + [VMEM] * inner, out_specs=(VMEM,) * outer,
        compiler_params=params(4), name="reply",
    )(wishes, partial, *replies)
    parts = [shift_outer(sorted_replies[k], k) for k in z2]

    output = jax.ShapeDtypeStruct((packed_rows, width), BF16)
    base, last = pl.pallas_call(
        functools.partial(local_kernel, slots=last_slots, count=count, chunks=chunks),
        out_shape=(pltpu.HBM(output.shape, output.dtype), late_rows),
        in_specs=[VMEM] * 3 + [ANY, HBM], out_specs=(VMEM, VMEM),
        scratch_shapes=[
            pltpu.VMEM((len(last_slots), heads, width, width), F32),
            pltpu.VMEM(products.shape, F32),
            pltpu.SemaphoreType.DMA((len(last_slots), chunks)),
        ],
        compiler_params=params(16), name="local",
    )(mixed, scale, lhs, sorted_replies[0], in_hbm(states))

    return unpack(pl.pallas_call(
        functools.partial(finish_kernel, count=count, heads=heads),
        out_shape=output, in_specs=[VMEM, HBM] + [VMEM] * (outer + 2), out_specs=HBM,
        scratch_shapes=[late_bf16, late_packed, pltpu.SemaphoreType.DMA((late,))],
        input_output_aliases={1: 0},
        compiler_params=params(4), name="finish",
    )(facts, in_hbm(base), last, partial, sorted_replies[0], *parts))


def solution(mesh):
    rows = P(("groups", "req"), None, None)
    in_specs = (rows, rows, rows, rows, P(("groups", "req"), None, None, None),
                P(("groups", "req")), P())
    return jax.shard_map(
        on_device, mesh=mesh, in_specs=in_specs, out_specs=rows, check_vma=False)
```

```python
import functools

import jax
import jax.numpy as jnp
from jax import lax
from jax.experimental import pallas as pl
from jax.experimental.pallas import tpu as pltpu
from jax.sharding import PartitionSpec as P

BEFORE = 3
EPS = 1e-06
F32 = jnp.float32
BF16 = jnp.bfloat16
MIB = 2**20
VMEM = pl.BlockSpec(memory_space=pltpu.VMEM)
SMEM = pl.BlockSpec(memory_space=pltpu.SMEM)
HBM = pl.BlockSpec(memory_space=pltpu.HBM)
ANY = pl.BlockSpec(memory_space=pl.ANY)


def silu(x):
    return x / (1.0 + jnp.exp(-x))


def sigmoid(x):
    return 1.0 / (1.0 + jnp.exp(-x))


def moving_slot(slots_ref, count):
    base = lax.axis_index("req") * count
    place = jnp.int32(0)
    moves = slots_ref[0] != base
    for s in range(1, count):
        here = slots_ref[s] != base + s
        place = jnp.where(here, s, place)
        moves = jnp.logical_or(moves, here)
    return place, moves


def wanted_device(slots_ref, count):
    device = lax.axis_index("req")
    result = device
    for s in range(count):
        owner = lax.div(slots_ref[s], jnp.int32(count))
        result = jnp.where(owner != device, owner, result)
    return result


OUTER, INNER, SLOT, FACTS = 0, 1, 2, 8


def wish_steps(inner):
    if inner & (inner - 1):
        return list(range(inner))
    steps, step = [0], 1
    while step < inner:
        steps, step = steps + [s ^ step for s in steps], step * 2
    return steps


def fact(ref, place, kind, rows):
    row = place * FACTS + kind
    return jnp.broadcast_to(ref[row:row + 1, :], (rows, ref.shape[1]))


def head_slope(heads, width):
    order = lax.broadcasted_iota(jnp.int32, (heads, width), 0).astype(F32)
    return jnp.exp2(-8.0 * (order + 1.0) / (2.0 * heads))


def decay_power(slope, power):
    return jnp.exp(slope * (-float(power)))


def split(x):
    high = x.astype(BF16)
    return high, (x - high.astype(F32)).astype(BF16)


def extract(packed, place, count):
    rows = packed.shape[0] // count
    result = packed[pl.ds(0, rows, stride=count), :]
    for s in range(1, count):
        result = jnp.where(place == s, packed[pl.ds(s, rows, stride=count), :], result)
    return result


def turn(position, step, size):
    return position ^ step if size & (size - 1) == 0 else (position + step) % size


def unturn(position, step, size):
    return position ^ step if size & (size - 1) == 0 else (position - step) % size


def shift(position, step, size):
    return lax.rem(position + step, size)


def inverse_step(step, size):
    return step if size & (size - 1) == 0 else (size - step) % size


def in_steps(refs, order):
    result = [refs[0]] * len(refs)
    for step, ref in zip(order, refs[1:]):
        result[step] = ref
    return result


def choose(options, index, sources):
    rows = index.shape[0]
    result = options[0][:rows, :]
    for option, source in zip(options[1:], sources[1:]):
        result = jnp.where(source == index, option[:rows, :], result)
    return result


def ask_kernel(new_slot_ref, queries_ref, out_ref, long_ref, facts_ref, slots_ref, rows_ref, wide,
               sems, *, count, inner):
    late = rows_ref.shape[0]
    first = queries_ref.shape[0] - late
    slots_copy = pltpu.make_async_copy(new_slot_ref, slots_ref, sems.at[0])
    slots_copy.start()
    copy = pltpu.make_async_copy(queries_ref.at[pl.ds(first, late)], rows_ref, sems.at[1])
    copy.start()
    slots_copy.wait()
    place, moves = moving_slot(slots_ref, count)
    wanted = wanted_device(slots_ref, count)
    kind = lax.broadcasted_iota(jnp.int32, facts_ref.shape, 0)
    facts = jnp.where(kind == INNER, lax.rem(wanted, inner), jnp.where(moves, place, count))
    facts_ref[...] = jnp.where(kind == OUTER, lax.div(wanted, inner), facts)
    copy.wait()
    wide[...] = rows_ref[...].astype(F32)
    rows = silu(extract(wide, place, count))
    out_ref[...] = rows
    long_ref[:rows.shape[0], :] = rows
    long_ref[rows.shape[0]:, :] = jnp.zeros_like(long_ref[rows.shape[0]:, :])


def pair_kernel(near_ref, far_ref, out_ref):
    rows = out_ref.shape[0] // 2
    out_ref[:rows, :] = near_ref[:rows, :]
    out_ref[rows:, :] = far_ref[:rows, :]


def prepare_kernel(slots_ref, queries_ref, keys_ref, values_ref, gates_ref, gain_ref, states_ref,
                   weight_ref, early_ref, rows_ref, gain_rows_ref, state, wide, sems, row_sems,
                   *, count, chunks):
    heads = states_ref.shape[1]
    size = heads // chunks
    place, _ = moving_slot(slots_ref, count)
    sources = (keys_ref, values_ref, queries_ref, gates_ref)
    copies = [
        pltpu.make_async_copy(ref, rows_ref.at[n], row_sems.at[n])
        for n, ref in enumerate(sources)]
    copies.append(pltpu.make_async_copy(gain_ref, gain_rows_ref, row_sems.at[len(sources)]))

    def load(c):
        part = pl.ds(c * size, size)
        return pltpu.make_async_copy(states_ref.at[place, part], state.at[part], sems.at[c])

    for copy in copies[:2]:
        copy.start()
    for c in range(chunks):
        load(c).start()
    for copy in copies[2:]:
        copy.start()
    for n, copy in enumerate(copies[:2]):
        copy.wait()
        wide[...] = rows_ref[n, :wide.shape[0], :].astype(F32)
        early_ref[n] = silu(extract(wide, place, count))
    for c in range(chunks):
        load(c).wait()
        for h in range(c * size, (c + 1) * size):
            weight_ref[h] = jnp.concatenate(split(state[h]), axis=0)
    for copy in copies[2:]:
        copy.wait()


def route_kernel(wishes_ref, *refs, inner, outer, order):
    column, outs = in_steps(refs[:outer], order), refs[outer:]
    my_outer = lax.div(lax.axis_index("req"), inner)
    for k in range(inner):
        back = wish_steps(inner).index(inverse_step(k, inner))
        wish = fact(wishes_ref, back, OUTER, outs[k].shape[0])
        outs[k][...] = choose(column, wish, [unturn(my_outer, k, outer) for k in range(outer)])


def answer_kernel(facts_ref, *refs, inner, late, heads, width, order):
    found, (weight_ref, early_ref, out_ref, lhs, prod) = refs[:inner], refs[inner:]
    found = in_steps(found, order)
    my_inner = lax.rem(lax.axis_index("req"), inner)
    block = lambda ref, t: ref[t * heads:(t + 1) * heads, :]
    sources = [unturn(my_inner, k, inner) for k in range(inner)]
    rows = choose(found, fact(facts_ref, 0, INNER, late * heads), sources)
    q = [rows[t * heads:(t + 1) * heads, :] for t in range(late)]
    slope = head_slope(heads, width)
    for t in range(late):
        x = q[t] * decay_power(slope, t + BEFORE + 1)
        high = x.astype(BF16).astype(F32)
        lhs[t * heads:(t + 1) * heads, :] = high
        lhs[(late + t) * heads:(late + t + 1) * heads, :] = x - high
    for h in range(heads):
        x = lhs[pl.ds(h, 2 * late, stride=heads), :].astype(BF16)
        prod[pl.ds(h, 2 * late, stride=heads), :] = jnp.dot(
            jnp.concatenate([x, x], axis=1), weight_ref[h], preferred_element_type=F32)
    for t in range(late):
        total = block(prod, t) + block(prod, late + t)
        for s in range(BEFORE):
            score = jnp.sum(q[t] * block(early_ref.at[0], s), axis=1, keepdims=True)
            total = total + score * decay_power(slope, t + BEFORE - s) * block(
                early_ref.at[1], s)
        out_ref[t * heads:(t + 1) * heads, :] = total


def reply_kernel(wishes_ref, after_ref, *refs, inner, outer, order):
    replies, outs = in_steps(refs[:inner], order), refs[inner:]
    me = lax.axis_index("req")
    my_inner, my_outer = lax.rem(me, inner), lax.div(me, inner)
    rows = outs[0].shape[0]
    owner = [
        jnp.where(fact(wishes_ref, n, INNER, rows) == my_inner,
                  fact(wishes_ref, n, OUTER, rows), -1)
        for n in map(wish_steps(inner).index, range(inner))]
    for k in range(outer):
        result = 0.0
        for n in range(inner):
            result = jnp.where(owner[n] == shift(my_outer, k, outer), replies[n][...], result)
        outs[k][...] = result


def load_states(states_ref, state, sems, slots, chunks):
    size = states_ref.shape[1] // chunks

    def load(n, c):
        part = pl.ds(c * size, size)
        return pltpu.make_async_copy(
            states_ref.at[slots[n], part], state.at[n, part], sems.at[n, c])

    for n in range(len(slots)):
        for c in range(chunks):
            load(n, c).start()
    return load


def times_states(load, state, lhs, prod, slots, count, chunks):
    heads = state.shape[1]
    size = heads // chunks
    for n, slot in enumerate(slots):
        for c in range(chunks):
            load(n, c).wait()
            for h in range(c * size, (c + 1) * size):
                rows = pl.ds(h * count + slot, 16, stride=heads * count)
                x = lhs[rows, :].astype(BF16)
                prod[rows, :] = jnp.dot(
                    jnp.concatenate([x, x], axis=1),
                    jnp.concatenate(split(state[n, h]), axis=0),
                    preferred_element_type=F32)


def row_slot(span, count):
    return lax.rem(lax.broadcasted_iota(jnp.int32, (span, 1), 0), jnp.int32(count))


def block(ref, t, rows):
    return ref[t * rows:(t + 1) * rows, :]


def scores_kernel(facts_ref, rows_ref, gain_ref, after_ref, states_ref, mixed_ref, scale_ref, late_ref, lhs, state, prod, wide, sems,
                  *, slots, count, chunks):
    heads, width = states_ref.shape[1], states_ref.shape[2]
    span = heads * count
    keys_ref, values_ref, queries_ref, gates_ref = [rows_ref.at[n] for n in range(4)]
    steps = rows_ref.shape[1] // span
    late = steps - BEFORE
    place = fact(facts_ref, 0, SLOT, late * heads)
    load = load_states(states_ref, state, sems, slots, chunks)

    def spread(x):
        for s in range(count):
            wide[pl.ds(s, heads, stride=count), :] = x
        return wide[:span, :]

    slope = spread(head_slope(heads, width))
    gain = spread(gain_ref[...])
    decay = [decay_power(slope, p) for p in range(steps + 1)]
    q = [silu(block(queries_ref, t, span).astype(F32)) for t in range(steps)]
    k = [silu(block(keys_ref, t, span).astype(F32)) for t in range(steps)]
    v = [silu(block(values_ref, t, span).astype(F32)) for t in range(steps)]
    for t in range(steps):
        x = q[t] * decay[t + 1]
        high = x.astype(BF16).astype(F32)
        lhs[t * span:(t + 1) * span, :] = high
        lhs[(8 + t) * span:(9 + t) * span, :] = x - high
    for t in range(steps):
        total = None
        far = None
        for s in range(t + 1):
            score = jnp.sum(q[t] * k[s], axis=1, keepdims=True)
            term = score * decay[t - s] * v[s]
            if t >= BEFORE and s < BEFORE:
                far = term if far is None else far + term
            else:
                total = term if total is None else total + term
        if t >= BEFORE:
            wide[(t - BEFORE) * span:(t - BEFORE + 1) * span, :] = total
        mixed_ref[t * span:(t + 1) * span, :] = total if far is None else total + far
    late_ref[0] = extract(wide, place, count)
    for t in range(steps):
        scale = gain * sigmoid(block(gates_ref, t, span).astype(F32))
        scale_ref[t * span:(t + 1) * span, :] = scale
        if t >= BEFORE:
            wide[(t - BEFORE) * span:(t - BEFORE + 1) * span, :] = scale
    late_ref[1] = extract(wide, place, count)
    times_states(load, state, lhs, prod, slots, count, chunks)
    slot = row_slot(span, count)
    for t in range(steps):
        x = block(prod, t, span) + block(prod, 8 + t, span)
        for s in slots:
            rows = slice(t * span, (t + 1) * span)
            mixed_ref[rows, :] = mixed_ref[rows, :] + jnp.where(slot == s, x, 0.0)


def local_kernel(mixed_ref, scale_ref, lhs, after_ref, states_ref, out_ref, last_ref, state, prod,
                 sems, *, slots, count, chunks):
    heads, width = states_ref.shape[1], states_ref.shape[2]
    span = heads * count
    steps = mixed_ref.shape[0] // span
    load = load_states(states_ref, state, sems, slots, chunks)
    times_states(load, state, lhs, prod, slots, count, chunks)
    slot = row_slot(span, count)
    for t in range(steps):
        x = block(mixed_ref, t, span)
        for s in slots:
            x = x + jnp.where(slot == s, block(prod, t, span) + block(prod, 8 + t, span), 0.0)
        sums = jnp.sum(x * x, axis=1, keepdims=True)
        energy = jnp.zeros((span, 1), F32)
        for s in range(count):
            whole = jnp.sum(jnp.where(slot == s, sums, 0.0), axis=0, keepdims=True)
            energy = jnp.where(slot == s, whole, energy)
        factor = lax.rsqrt(energy * (1.0 / (heads * width)) + EPS)
        y = (x * factor * block(scale_ref, t, span)).astype(BF16)
        out_ref[t * span:(t + 1) * span, :] = y
        if t >= BEFORE:
            last_ref[(t - BEFORE) * span:(t - BEFORE + 1) * span, :] = y


def finish_kernel(facts_ref, base_ref, last_ref, late_ref, *refs, count, heads):
    parts, (out_ref, rows_ref, wide, sems) = refs[:-4], refs[-4:]
    place = fact(facts_ref, 0, SLOT, heads)
    span = heads * count
    steps = late_ref.shape[1] // heads
    first = out_ref.shape[0] - steps * span
    copies = []
    for t in range(steps):
        part = slice(t * heads, (t + 1) * heads)
        x = late_ref[0, part, :]
        for ref in parts:
            x = x + ref[part, :]
        energy = jnp.sum(jnp.sum(x * x, axis=0, keepdims=True), axis=1, keepdims=True)
        y = x * lax.rsqrt(energy * (1.0 / x.size) + EPS) * late_ref[1, part, :]
        rows = slice(t * span, (t + 1) * span)
        wide[rows, :] = last_ref[rows, :].astype(F32)
        for s in range(count):
            here = pl.ds(t * span + s, heads, stride=count)
            wide[here, :] = jnp.where(place == s, y, wide[here, :])
        rows_ref[rows, :] = wide[rows, :].astype(BF16)
        copies.append(pltpu.make_async_copy(
            rows_ref.at[pl.ds(t * span, span)], out_ref.at[pl.ds(first + t * span, span)],
            sems.at[t]))
        copies[t].start()
    for copy in copies:
        copy.wait()


def in_hbm(x):
    return pltpu.with_memory_space_constraint(x, pltpu.HBM)


def near_square(total):
    return next(
        (d, total // d) for d in range(1, total + 1) if total % d == 0 and d * d >= total)


def on_device(queries, keys, values, gates, states, new_slot, norm_gain):
    count, steps, features = queries.shape
    heads, width = states.shape[1], states.shape[2]
    late = steps - BEFORE
    packed_rows, single_rows = steps * heads * count, late * heads
    inner, outer = near_square(lax.axis_size("req"))

    def pack(x):
        return x.reshape(count, steps, heads, width).transpose(1, 2, 0, 3).reshape(
            packed_rows, width)

    def unpack(x):
        return x.reshape(steps, heads, count, width).transpose(2, 0, 1, 3).reshape(
            count, steps, features)

    def send_inner(x, k):
        return lax.ppermute(x, "req", [
            (o * inner + i, o * inner + int(turn(i, k, inner)))
            for o in range(outer) for i in range(inner)])

    def send_outer(x, k):
        return lax.ppermute(x, "req", [
            (o * inner + i, int(turn(o, k, outer)) * inner + i)
            for o in range(outer) for i in range(inner)])

    def gather_inner(x):
        if inner & (inner - 1):
            x = x[:FACTS]
            return jnp.concatenate([x] + [send_inner(x, k) for k in range(1, inner)])
        step, result = 1, x
        while step < inner:
            result = pl.pallas_call(
                pair_kernel,
                out_shape=jax.ShapeDtypeStruct((2 * step * FACTS, width), jnp.int32),
                in_specs=[VMEM, VMEM], out_specs=VMEM, compiler_params=params(4), name="pair",
            )(result, send_inner(result, step))
            step *= 2
        return result

    def shift_outer(x, k):
        return lax.ppermute(x, "req", [
            (o * inner + i, (o + k) % outer * inner + i)
            for o in range(outer) for i in range(inner)])

    def params(limit):
        return pltpu.CompilerParams(vmem_limit_bytes=limit * MIB)

    queries, keys, values, gates = pack(queries), pack(keys), pack(values), pack(gates)
    single = jax.ShapeDtypeStruct((single_rows, width), F32)
    late_packed = pltpu.VMEM((late * heads * count, width), F32)

    late_rows = jax.ShapeDtypeStruct((late * heads * count, width), BF16)
    late_bf16 = pltpu.VMEM(late_rows.shape, BF16)

    long = jax.ShapeDtypeStruct((single_rows + FACTS, width), F32)
    facts_rows = max(single_rows * 5 // (6 * FACTS), 1) * FACTS
    ask, ask_long, facts = pl.pallas_call(
        functools.partial(ask_kernel, count=count, inner=inner),
        out_shape=(single, long, jax.ShapeDtypeStruct((facts_rows, width), jnp.int32)),
        in_specs=[HBM, HBM], out_specs=(VMEM, VMEM, VMEM),
        scratch_shapes=[pltpu.SMEM((count,), jnp.int32), late_bf16, late_packed,
                        pltpu.SemaphoreType.DMA((2,))],
        compiler_params=params(4), name="ask",
    )(in_hbm(new_slot), in_hbm(queries))

    z1, z2 = list(range(1, outer)), list(range(1, outer))
    q1, q2 = list(range(inner - 1, 0, -1)), list(range(1, inner))
    column = [ask] + [send_outer(ask_long if k == outer // 2 else ask, k) for k in z1]
    wishes = gather_inner(facts)

    chunks = 8
    gain = norm_gain.reshape(heads, width)
    weight, early, rows, gain_rows = pl.pallas_call(
        functools.partial(prepare_kernel, count=count, chunks=chunks),
        out_shape=(jax.ShapeDtypeStruct((heads, 2 * width, width), BF16),
                   jax.ShapeDtypeStruct((2, BEFORE * heads, width), F32),
                   jax.ShapeDtypeStruct((4, packed_rows, width), BF16),
                   jax.ShapeDtypeStruct(gain.shape, F32)),
        in_specs=[SMEM] + [HBM] * 6, out_specs=(VMEM,) * 4,
        scratch_shapes=[pltpu.VMEM((heads, width, width), F32),
                        pltpu.VMEM((BEFORE * heads * count, width), F32),
                        pltpu.SemaphoreType.DMA((chunks,)),
                        pltpu.SemaphoreType.DMA((5,))],
        compiler_params=params(12), name="prepare",
    )(*map(in_hbm, (new_slot, queries, keys, values, gates, gain, states)))

    asked = pl.pallas_call(
        functools.partial(route_kernel, inner=inner, outer=outer, order=z1),
        out_shape=(single,) * inner,
        in_specs=[VMEM] * (1 + outer), out_specs=(VMEM,) * inner,
        compiler_params=params(4), name="route",
    )(wishes, *column)
    found = [asked[0]] + [send_inner(asked[k], k) for k in q1]

    answer = pl.pallas_call(
        functools.partial(answer_kernel, inner=inner, late=late, heads=heads, width=width,
                          order=q1),
        out_shape=single, in_specs=[VMEM] * (inner + 3), out_specs=VMEM,
        scratch_shapes=[pltpu.VMEM((2 * late * heads, width), F32)] * 2,
        compiler_params=params(8), name="answer",
    )(facts, *found, weight, early)
    replies = [answer] + [send_inner(answer, k) for k in q2]

    chunks = 4
    first_slots, last_slots = list(range(count // 2)), list(range(count // 2, count))
    packed = jax.ShapeDtypeStruct((packed_rows, width), F32)
    products = jax.ShapeDtypeStruct((16 * heads * count, width), F32)
    mixed, scale, partial, lhs = pl.pallas_call(
        functools.partial(scores_kernel, slots=first_slots, count=count, chunks=chunks),
        out_shape=(packed, packed, jax.ShapeDtypeStruct((2, single_rows, width), F32), products),
        in_specs=[VMEM] * 3 + [ANY, HBM], out_specs=(VMEM,) * 4,
        scratch_shapes=[
            pltpu.VMEM((max(len(first_slots), 1), heads, width, width), F32),
            pltpu.VMEM(products.shape, F32),
            late_packed,
            pltpu.SemaphoreType.DMA((max(len(first_slots), 1), chunks)),
        ],
        compiler_params=params(16), name="scores",
    )(facts, rows, gain_rows, answer, in_hbm(states))

    sorted_replies = pl.pallas_call(
        functools.partial(reply_kernel, inner=inner, outer=outer, order=q2),
        out_shape=(single,) * outer,
        in_specs=[VMEM, ANY] + [VMEM] * inner, out_specs=(VMEM,) * outer,
        compiler_params=params(4), name="reply",
    )(wishes, partial, *replies)
    parts = [shift_outer(sorted_replies[k], k) for k in z2]

    output = jax.ShapeDtypeStruct((packed_rows, width), BF16)
    base, last = pl.pallas_call(
        functools.partial(local_kernel, slots=last_slots, count=count, chunks=chunks),
        out_shape=(pltpu.HBM(output.shape, output.dtype), late_rows),
        in_specs=[VMEM] * 3 + [ANY, HBM], out_specs=(VMEM, VMEM),
        scratch_shapes=[
            pltpu.VMEM((len(last_slots), heads, width, width), F32),
            pltpu.VMEM(products.shape, F32),
            pltpu.SemaphoreType.DMA((len(last_slots), chunks)),
        ],
        compiler_params=params(16), name="local",
    )(mixed, scale, lhs, sorted_replies[0], in_hbm(states))

    return unpack(pl.pallas_call(
        functools.partial(finish_kernel, count=count, heads=heads),
        out_shape=output, in_specs=[VMEM, HBM] + [VMEM] * (outer + 2), out_specs=HBM,
        scratch_shapes=[late_bf16, late_packed, pltpu.SemaphoreType.DMA((late,))],
        input_output_aliases={1: 0},
        compiler_params=params(4), name="finish",
    )(facts, in_hbm(base), last, partial, sorted_replies[0], *parts))


def solution(mesh):
    rows = P(("groups", "req"), None, None)
    in_specs = (rows, rows, rows, rows, P(("groups", "req"), None, None, None),
                P(("groups", "req")), P())
    return jax.shard_map(
        on_device, mesh=mesh, in_specs=in_specs, out_specs=rows, check_vma=False)
```

```python
import functools

import jax
import jax.numpy as jnp
from jax import lax
from jax.experimental import pallas as pl
from jax.experimental.pallas import tpu as pltpu
from jax.sharding import PartitionSpec as P

BEFORE = 3
EPS = 1e-06
F32 = jnp.float32
BF16 = jnp.bfloat16
MIB = 2**20
VMEM = pl.BlockSpec(memory_space=pltpu.VMEM)
SMEM = pl.BlockSpec(memory_space=pltpu.SMEM)
HBM = pl.BlockSpec(memory_space=pltpu.HBM)
ANY = pl.BlockSpec(memory_space=pl.ANY)


def silu(x):
    return x / (1.0 + jnp.exp(-x))


def sigmoid(x):
    return 1.0 / (1.0 + jnp.exp(-x))


def moving_slot(slots_ref, count):
    base = lax.axis_index("req") * count
    place = jnp.int32(0)
    moves = slots_ref[0] != base
    for s in range(1, count):
        here = slots_ref[s] != base + s
        place = jnp.where(here, s, place)
        moves = jnp.logical_or(moves, here)
    return place, moves


def wanted_device(slots_ref, count):
    device = lax.axis_index("req")
    result = device
    for s in range(count):
        owner = lax.div(slots_ref[s], jnp.int32(count))
        result = jnp.where(owner != device, owner, result)
    return result


OUTER, INNER, SLOT, FACTS = 0, 1, 2, 8


def wish_steps(inner):
    if inner & (inner - 1):
        return list(range(inner))
    steps, step = [0], 1
    while step < inner:
        steps, step = steps + [s ^ step for s in steps], step * 2
    return steps


def fact(ref, place, kind, rows):
    row = place * FACTS + kind
    return jnp.broadcast_to(ref[row:row + 1, :], (rows, ref.shape[1]))


def head_slope(heads, width):
    order = lax.broadcasted_iota(jnp.int32, (heads, width), 0).astype(F32)
    return jnp.exp2(-8.0 * (order + 1.0) / (2.0 * heads))


def decay_power(slope, power):
    return jnp.exp(slope * (-float(power)))


def split(x):
    high = x.astype(BF16)
    return high, (x - high.astype(F32)).astype(BF16)


def extract(packed, place, count):
    rows = packed.shape[0] // count
    result = packed[pl.ds(0, rows, stride=count), :]
    for s in range(1, count):
        result = jnp.where(place == s, packed[pl.ds(s, rows, stride=count), :], result)
    return result


def turn(position, step, size):
    return position ^ step if size & (size - 1) == 0 else (position + step) % size


def unturn(position, step, size):
    return position ^ step if size & (size - 1) == 0 else (position - step) % size


def shift(position, step, size):
    return lax.rem(position + step, size)


def inverse_step(step, size):
    return step if size & (size - 1) == 0 else (size - step) % size


def in_steps(refs, order):
    result = [refs[0]] * len(refs)
    for step, ref in zip(order, refs[1:]):
        result[step] = ref
    return result


def choose(options, index, sources):
    rows = index.shape[0]
    result = options[0][:rows, :]
    for option, source in zip(options[1:], sources[1:]):
        result = jnp.where(source == index, option[:rows, :], result)
    return result


def ask_kernel(new_slot_ref, queries_ref, out_ref, long_ref, facts_ref, slots_ref, rows_ref, wide,
               sems, *, count, inner):
    late = rows_ref.shape[0]
    first = queries_ref.shape[0] - late
    slots_copy = pltpu.make_async_copy(new_slot_ref, slots_ref, sems.at[0])
    slots_copy.start()
    copy = pltpu.make_async_copy(queries_ref.at[pl.ds(first, late)], rows_ref, sems.at[1])
    copy.start()
    slots_copy.wait()
    place, moves = moving_slot(slots_ref, count)
    wanted = wanted_device(slots_ref, count)
    kind = lax.broadcasted_iota(jnp.int32, facts_ref.shape, 0)
    facts = jnp.where(kind == INNER, lax.rem(wanted, inner), jnp.where(moves, place, count))
    facts_ref[...] = jnp.where(kind == OUTER, lax.div(wanted, inner), facts)
    copy.wait()
    wide[...] = rows_ref[...].astype(F32)
    rows = silu(extract(wide, place, count))
    out_ref[...] = rows
    long_ref[:rows.shape[0], :] = rows
    long_ref[rows.shape[0]:, :] = jnp.zeros_like(long_ref[rows.shape[0]:, :])


def pair_kernel(near_ref, far_ref, out_ref):
    rows = out_ref.shape[0] // 2
    out_ref[:rows, :] = near_ref[:rows, :]
    out_ref[rows:, :] = far_ref[:rows, :]


def prepare_kernel(slots_ref, queries_ref, keys_ref, values_ref, gates_ref, gain_ref, states_ref,
                   weight_ref, early_ref, rows_ref, gain_rows_ref, state, wide, sems, row_sems,
                   *, count, chunks):
    heads = states_ref.shape[1]
    size = heads // chunks
    place, _ = moving_slot(slots_ref, count)
    sources = (keys_ref, values_ref, queries_ref, gates_ref)
    copies = [
        pltpu.make_async_copy(ref, rows_ref.at[n], row_sems.at[n])
        for n, ref in enumerate(sources)]
    copies.append(pltpu.make_async_copy(gain_ref, gain_rows_ref, row_sems.at[len(sources)]))

    def load(c):
        part = pl.ds(c * size, size)
        return pltpu.make_async_copy(states_ref.at[place, part], state.at[part], sems.at[c])

    for copy in copies[:2]:
        copy.start()
    for c in range(chunks):
        load(c).start()
    for copy in copies[2:]:
        copy.start()
    for n, copy in enumerate(copies[:2]):
        copy.wait()
        wide[...] = rows_ref[n, :wide.shape[0], :].astype(F32)
        early_ref[n] = silu(extract(wide, place, count))
    for c in range(chunks):
        load(c).wait()
        for h in range(c * size, (c + 1) * size):
            weight_ref[h] = jnp.concatenate(split(state[h]), axis=0)
    for copy in copies[2:]:
        copy.wait()


def route_kernel(wishes_ref, *refs, inner, outer, order):
    column, outs = in_steps(refs[:outer], order), refs[outer:]
    my_outer = lax.div(lax.axis_index("req"), inner)
    for k in range(inner):
        back = wish_steps(inner).index(inverse_step(k, inner))
        wish = fact(wishes_ref, back, OUTER, outs[k].shape[0])
        outs[k][...] = choose(column, wish, [unturn(my_outer, k, outer) for k in range(outer)])


def answer_kernel(facts_ref, *refs, inner, late, heads, width, order):
    found, (weight_ref, early_ref, out_ref, lhs, prod) = refs[:inner], refs[inner:]
    found = in_steps(found, order)
    my_inner = lax.rem(lax.axis_index("req"), inner)
    block = lambda ref, t: ref[t * heads:(t + 1) * heads, :]
    sources = [unturn(my_inner, k, inner) for k in range(inner)]
    rows = choose(found, fact(facts_ref, 0, INNER, late * heads), sources)
    q = [rows[t * heads:(t + 1) * heads, :] for t in range(late)]
    slope = head_slope(heads, width)
    for t in range(late):
        x = q[t] * decay_power(slope, t + BEFORE + 1)
        high = x.astype(BF16).astype(F32)
        lhs[t * heads:(t + 1) * heads, :] = high
        lhs[(late + t) * heads:(late + t + 1) * heads, :] = x - high
    for h in range(heads):
        x = lhs[pl.ds(h, 2 * late, stride=heads), :].astype(BF16)
        prod[pl.ds(h, 2 * late, stride=heads), :] = jnp.dot(
            jnp.concatenate([x, x], axis=1), weight_ref[h], preferred_element_type=F32)
    for t in range(late):
        total = block(prod, t) + block(prod, late + t)
        for s in range(BEFORE):
            score = jnp.sum(q[t] * block(early_ref.at[0], s), axis=1, keepdims=True)
            total = total + score * decay_power(slope, t + BEFORE - s) * block(
                early_ref.at[1], s)
        out_ref[t * heads:(t + 1) * heads, :] = total


def reply_kernel(wishes_ref, after_ref, *refs, inner, outer, order):
    replies, outs = in_steps(refs[:inner], order), refs[inner:]
    me = lax.axis_index("req")
    my_inner, my_outer = lax.rem(me, inner), lax.div(me, inner)
    rows = outs[0].shape[0]
    owner = [
        jnp.where(fact(wishes_ref, n, INNER, rows) == my_inner,
                  fact(wishes_ref, n, OUTER, rows), -1)
        for n in map(wish_steps(inner).index, range(inner))]
    for k in range(outer):
        result = 0.0
        for n in range(inner):
            result = jnp.where(owner[n] == shift(my_outer, k, outer), replies[n][...], result)
        outs[k][...] = result


def load_states(states_ref, state, sems, slots, chunks):
    size = states_ref.shape[1] // chunks

    def load(n, c):
        part = pl.ds(c * size, size)
        return pltpu.make_async_copy(
            states_ref.at[slots[n], part], state.at[n, part], sems.at[n, c])

    for n in range(len(slots)):
        for c in range(chunks):
            load(n, c).start()
    return load


def times_states(load, state, lhs, prod, slots, count, chunks):
    heads = state.shape[1]
    size = heads // chunks
    for n, slot in enumerate(slots):
        for c in range(chunks):
            load(n, c).wait()
            for h in range(c * size, (c + 1) * size):
                rows = pl.ds(h * count + slot, 16, stride=heads * count)
                x = lhs[rows, :].astype(BF16)
                prod[rows, :] = jnp.dot(
                    jnp.concatenate([x, x], axis=1),
                    jnp.concatenate(split(state[n, h]), axis=0),
                    preferred_element_type=F32)


def row_slot(span, count):
    return lax.rem(lax.broadcasted_iota(jnp.int32, (span, 1), 0), jnp.int32(count))


def block(ref, t, rows):
    return ref[t * rows:(t + 1) * rows, :]


def scores_kernel(facts_ref, rows_ref, gain_ref, after_ref, states_ref, mixed_ref, scale_ref, late_ref, lhs, state, prod, wide, sems,
                  *, slots, count, chunks):
    heads, width = states_ref.shape[1], states_ref.shape[2]
    span = heads * count
    keys_ref, values_ref, queries_ref, gates_ref = [rows_ref.at[n] for n in range(4)]
    steps = rows_ref.shape[1] // span
    late = steps - BEFORE
    place = fact(facts_ref, 0, SLOT, late * heads)
    load = load_states(states_ref, state, sems, slots, chunks)

    def spread(x):
        for s in range(count):
            wide[pl.ds(s, heads, stride=count), :] = x
        return wide[:span, :]

    slope = spread(head_slope(heads, width))
    gain = spread(gain_ref[...])
    decay = [decay_power(slope, p) for p in range(steps + 1)]
    q = [silu(block(queries_ref, t, span).astype(F32)) for t in range(steps)]
    k = [silu(block(keys_ref, t, span).astype(F32)) for t in range(steps)]
    v = [silu(block(values_ref, t, span).astype(F32)) for t in range(steps)]
    for t in range(steps):
        x = q[t] * decay[t + 1]
        high = x.astype(BF16).astype(F32)
        lhs[t * span:(t + 1) * span, :] = high
        lhs[(8 + t) * span:(9 + t) * span, :] = x - high
    for t in range(steps):
        total = None
        far = None
        for s in range(t + 1):
            score = jnp.sum(q[t] * k[s], axis=1, keepdims=True)
            term = score * decay[t - s] * v[s]
            if t >= BEFORE and s < BEFORE:
                far = term if far is None else far + term
            else:
                total = term if total is None else total + term
        if t >= BEFORE:
            wide[(t - BEFORE) * span:(t - BEFORE + 1) * span, :] = total
        mixed_ref[t * span:(t + 1) * span, :] = total if far is None else total + far
    late_ref[0] = extract(wide, place, count)
    for t in range(steps):
        scale = gain * sigmoid(block(gates_ref, t, span).astype(F32))
        scale_ref[t * span:(t + 1) * span, :] = scale
        if t >= BEFORE:
            wide[(t - BEFORE) * span:(t - BEFORE + 1) * span, :] = scale
    late_ref[1] = extract(wide, place, count)
    times_states(load, state, lhs, prod, slots, count, chunks)
    slot = row_slot(span, count)
    for t in range(steps):
        x = block(prod, t, span) + block(prod, 8 + t, span)
        for s in slots:
            rows = slice(t * span, (t + 1) * span)
            mixed_ref[rows, :] = mixed_ref[rows, :] + jnp.where(slot == s, x, 0.0)


def local_kernel(mixed_ref, scale_ref, lhs, after_ref, states_ref, out_ref, last_ref, state, prod,
                 sems, *, slots, count, chunks):
    heads, width = states_ref.shape[1], states_ref.shape[2]
    span = heads * count
    steps = mixed_ref.shape[0] // span
    load = load_states(states_ref, state, sems, slots, chunks)
    times_states(load, state, lhs, prod, slots, count, chunks)
    slot = row_slot(span, count)
    for t in range(steps):
        x = block(mixed_ref, t, span)
        for s in slots:
            x = x + jnp.where(slot == s, block(prod, t, span) + block(prod, 8 + t, span), 0.0)
        sums = jnp.sum(x * x, axis=1, keepdims=True)
        energy = jnp.zeros((span, 1), F32)
        for s in range(count):
            whole = jnp.sum(jnp.where(slot == s, sums, 0.0), axis=0, keepdims=True)
            energy = jnp.where(slot == s, whole, energy)
        factor = lax.rsqrt(energy * (1.0 / (heads * width)) + EPS)
        y = (x * factor * block(scale_ref, t, span)).astype(BF16)
        out_ref[t * span:(t + 1) * span, :] = y
        if t >= BEFORE:
            last_ref[(t - BEFORE) * span:(t - BEFORE + 1) * span, :] = y


def finish_kernel(facts_ref, base_ref, last_ref, late_ref, *refs, count, heads):
    parts, (out_ref, rows_ref, wide, sems) = refs[:-4], refs[-4:]
    place = fact(facts_ref, 0, SLOT, heads)
    span = heads * count
    steps = late_ref.shape[1] // heads
    first = out_ref.shape[0] - steps * span
    copies = []
    for t in range(steps):
        part = slice(t * heads, (t + 1) * heads)
        x = late_ref[0, part, :]
        for ref in parts:
            x = x + ref[part, :]
        energy = jnp.sum(jnp.sum(x * x, axis=0, keepdims=True), axis=1, keepdims=True)
        y = x * lax.rsqrt(energy * (1.0 / x.size) + EPS) * late_ref[1, part, :]
        rows = slice(t * span, (t + 1) * span)
        wide[rows, :] = last_ref[rows, :].astype(F32)
        for s in range(count):
            here = pl.ds(t * span + s, heads, stride=count)
            wide[here, :] = jnp.where(place == s, y, wide[here, :])
        rows_ref[rows, :] = wide[rows, :].astype(BF16)
        copies.append(pltpu.make_async_copy(
            rows_ref.at[pl.ds(t * span, span)], out_ref.at[pl.ds(first + t * span, span)],
            sems.at[t]))
        copies[t].start()
    for copy in copies:
        copy.wait()


def in_hbm(x):
    return pltpu.with_memory_space_constraint(x, pltpu.HBM)


def near_square(total):
    return next(
        (d, total // d) for d in range(1, total + 1) if total % d == 0 and d * d >= total)


def on_device(queries, keys, values, gates, states, new_slot, norm_gain):
    count, steps, features = queries.shape
    heads, width = states.shape[1], states.shape[2]
    late = steps - BEFORE
    packed_rows, single_rows = steps * heads * count, late * heads
    inner, outer = near_square(lax.axis_size("req"))

    def pack(x):
        return x.reshape(count, steps, heads, width).transpose(1, 2, 0, 3).reshape(
            packed_rows, width)

    def unpack(x):
        return x.reshape(steps, heads, count, width).transpose(2, 0, 1, 3).reshape(
            count, steps, features)

    def send_inner(x, k):
        return lax.ppermute(x, "req", [
            (o * inner + i, o * inner + int(turn(i, k, inner)))
            for o in range(outer) for i in range(inner)])

    def send_outer(x, k):
        return lax.ppermute(x, "req", [
            (o * inner + i, int(turn(o, k, outer)) * inner + i)
            for o in range(outer) for i in range(inner)])

    def gather_inner(x):
        if inner & (inner - 1):
            x = x[:FACTS]
            return jnp.concatenate([x] + [send_inner(x, k) for k in range(1, inner)])
        step, result = 1, x
        while step < inner:
            result = pl.pallas_call(
                pair_kernel,
                out_shape=jax.ShapeDtypeStruct((2 * step * FACTS, width), jnp.int32),
                in_specs=[VMEM, VMEM], out_specs=VMEM, compiler_params=params(4), name="pair",
            )(result, send_inner(result, step))
            step *= 2
        return result

    def shift_outer(x, k):
        return lax.ppermute(x, "req", [
            (o * inner + i, (o + k) % outer * inner + i)
            for o in range(outer) for i in range(inner)])

    def params(limit):
        return pltpu.CompilerParams(vmem_limit_bytes=limit * MIB)

    queries, keys, values, gates = pack(queries), pack(keys), pack(values), pack(gates)
    single = jax.ShapeDtypeStruct((single_rows, width), F32)
    late_packed = pltpu.VMEM((late * heads * count, width), F32)

    late_rows = jax.ShapeDtypeStruct((late * heads * count, width), BF16)
    late_bf16 = pltpu.VMEM(late_rows.shape, BF16)

    long = jax.ShapeDtypeStruct((single_rows + FACTS, width), F32)
    facts_rows = max(single_rows * 5 // (6 * FACTS), 1) * FACTS
    ask, ask_long, facts = pl.pallas_call(
        functools.partial(ask_kernel, count=count, inner=inner),
        out_shape=(single, long, jax.ShapeDtypeStruct((facts_rows, width), jnp.int32)),
        in_specs=[HBM, HBM], out_specs=(VMEM, VMEM, VMEM),
        scratch_shapes=[pltpu.SMEM((count,), jnp.int32), late_bf16, late_packed,
                        pltpu.SemaphoreType.DMA((2,))],
        compiler_params=params(4), name="ask",
    )(in_hbm(new_slot), in_hbm(queries))

    z1, z2 = list(range(1, outer)), list(range(1, outer))
    q1, q2 = list(range(inner - 1, 0, -1)), [inner - 1, *range(1, inner - 1)]
    column = [ask] + [send_outer(ask_long if k == outer // 2 else ask, k) for k in z1]
    wishes = gather_inner(facts)

    chunks = 8
    gain = norm_gain.reshape(heads, width)
    weight, early, rows, gain_rows = pl.pallas_call(
        functools.partial(prepare_kernel, count=count, chunks=chunks),
        out_shape=(jax.ShapeDtypeStruct((heads, 2 * width, width), BF16),
                   jax.ShapeDtypeStruct((2, BEFORE * heads, width), F32),
                   jax.ShapeDtypeStruct((4, packed_rows, width), BF16),
                   jax.ShapeDtypeStruct(gain.shape, F32)),
        in_specs=[SMEM] + [HBM] * 6, out_specs=(VMEM,) * 4,
        scratch_shapes=[pltpu.VMEM((heads, width, width), F32),
                        pltpu.VMEM((BEFORE * heads * count, width), F32),
                        pltpu.SemaphoreType.DMA((chunks,)),
                        pltpu.SemaphoreType.DMA((5,))],
        compiler_params=params(12), name="prepare",
    )(*map(in_hbm, (new_slot, queries, keys, values, gates, gain, states)))

    asked = pl.pallas_call(
        functools.partial(route_kernel, inner=inner, outer=outer, order=z1),
        out_shape=(single,) * inner,
        in_specs=[VMEM] * (1 + outer), out_specs=(VMEM,) * inner,
        compiler_params=params(4), name="route",
    )(wishes, *column)
    found = [asked[0]] + [send_inner(asked[k], k) for k in q1]

    answer = pl.pallas_call(
        functools.partial(answer_kernel, inner=inner, late=late, heads=heads, width=width,
                          order=q1),
        out_shape=single, in_specs=[VMEM] * (inner + 3), out_specs=VMEM,
        scratch_shapes=[pltpu.VMEM((2 * late * heads, width), F32)] * 2,
        compiler_params=params(8), name="answer",
    )(facts, *found, weight, early)
    replies = [answer] + [send_inner(answer, k) for k in q2]

    chunks = 4
    first_slots, last_slots = list(range(count // 2)), list(range(count // 2, count))
    packed = jax.ShapeDtypeStruct((packed_rows, width), F32)
    products = jax.ShapeDtypeStruct((16 * heads * count, width), F32)
    mixed, scale, partial, lhs = pl.pallas_call(
        functools.partial(scores_kernel, slots=first_slots, count=count, chunks=chunks),
        out_shape=(packed, packed, jax.ShapeDtypeStruct((2, single_rows, width), F32), products),
        in_specs=[VMEM] * 3 + [ANY, HBM], out_specs=(VMEM,) * 4,
        scratch_shapes=[
            pltpu.VMEM((max(len(first_slots), 1), heads, width, width), F32),
            pltpu.VMEM(products.shape, F32),
            late_packed,
            pltpu.SemaphoreType.DMA((max(len(first_slots), 1), chunks)),
        ],
        compiler_params=params(16), name="scores",
    )(facts, rows, gain_rows, answer, in_hbm(states))

    sorted_replies = pl.pallas_call(
        functools.partial(reply_kernel, inner=inner, outer=outer, order=q2),
        out_shape=(single,) * outer,
        in_specs=[VMEM, ANY] + [VMEM] * inner, out_specs=(VMEM,) * outer,
        compiler_params=params(4), name="reply",
    )(wishes, partial, *replies)
    parts = [shift_outer(sorted_replies[k], k) for k in z2]

    output = jax.ShapeDtypeStruct((packed_rows, width), BF16)
    base, last = pl.pallas_call(
        functools.partial(local_kernel, slots=last_slots, count=count, chunks=chunks),
        out_shape=(pltpu.HBM(output.shape, output.dtype), late_rows),
        in_specs=[VMEM] * 3 + [ANY, HBM], out_specs=(VMEM, VMEM),
        scratch_shapes=[
            pltpu.VMEM((len(last_slots), heads, width, width), F32),
            pltpu.VMEM(products.shape, F32),
            pltpu.SemaphoreType.DMA((len(last_slots), chunks)),
        ],
        compiler_params=params(16), name="local",
    )(mixed, scale, lhs, sorted_replies[0], in_hbm(states))

    return unpack(pl.pallas_call(
        functools.partial(finish_kernel, count=count, heads=heads),
        out_shape=output, in_specs=[VMEM, HBM] + [VMEM] * (outer + 2), out_specs=HBM,
        scratch_shapes=[late_bf16, late_packed, pltpu.SemaphoreType.DMA((late,))],
        input_output_aliases={1: 0},
        compiler_params=params(4), name="finish",
    )(facts, in_hbm(base), last, partial, sorted_replies[0], *parts))


def solution(mesh):
    rows = P(("groups", "req"), None, None)
    in_specs = (rows, rows, rows, rows, P(("groups", "req"), None, None, None),
                P(("groups", "req")), P())
    return jax.shard_map(
        on_device, mesh=mesh, in_specs=in_specs, out_specs=rows, check_vma=False)
```
